32 devices in a mesh: dp: 8 (over y, x, core), mp: 4 (over z).
Axes of the slice: x: 2, y: 2, z: 4, core: 2. Of those that a mesh axis runs over, the one named last changes fastest.
Arguments:
- tokens: bfloat16 [16384, 768], P('dp'), may hold values from -6 to 6
- segment_ids: int32 [32, 512], P('dp'), may hold values from 0 to 3, never falling along the last dimension, each value on 1 to 256 neighbouring positions
- pad_mask: int32 [32, 512], P('dp'), may hold values 0 or 1
- top_index: int32 [32, 32, 32], P('dp'), may hold values from 0 to 511
- query_emb: bfloat16 [32, 32, 128], P('dp'), may hold values from -6 to 6
- score_cot: float32 [32, 32, 32], P('dp'), may hold values from -6 to 6
- gain_attn: bfloat16 [768], replicated, may hold values from 0.25 to 1.75
- w_query: bfloat16 [768, 768], P(None, 'mp'), may hold values from -0.02734375 to 0.02734375
- w_key: bfloat16 [768, 768], P(None, 'mp'), may hold values from -0.21875 to 0.21875
- w_value: bfloat16 [768, 768], P(None, 'mp'), may hold values from -0.21875 to 0.21875
- w_out: bfloat16 [768, 768], P('mp'), may hold values from -1.75 to 1.75
- rel_table: bfloat16 [32, 12], P(None, 'mp'), may hold values from -4 to 4
- gain_ffn: bfloat16 [768], replicated, may hold values from 0.25 to 1.75
- w_gate: bfloat16 [768, 3072], P(None, 'mp'), may hold values from -0.21875 to 0.21875
- w_up: bfloat16 [768, 3072], P(None, 'mp'), may hold values from -0.21875 to 0.21875
- w_down: bfloat16 [3072, 768], P('mp'), may hold values from -0.109375 to 0.109375
- gain_final: bfloat16 [768], replicated, may hold values from 0.25 to 1.75
- w_proj: bfloat16 [768, 128], replicated, may hold values from -0.21875 to 0.21875
Outputs:
- scores: float32 [32, 32, 32], P('dp')
- input_grad: float32 [16384, 768], P('dp')
- grad_gain_attn: float32 [768], replicated
- grad_w_query: float32 [768, 768], P(None, 'mp')
- grad_w_key: float32 [768, 768], P(None, 'mp')
- grad_w_value: float32 [768, 768], P(None, 'mp')
- grad_w_out: float32 [768, 768], P('mp')
- grad_rel_table: float32 [32, 12], P(None, 'mp')
- grad_gain_ffn: float32 [768], replicated
- grad_w_gate: float32 [768, 3072], P(None, 'mp')
- grad_w_up: float32 [768, 3072], P(None, 'mp')
- grad_w_down: float32 [3072, 768], P('mp')
- grad_gain_final: float32 [768], replicated
- grad_w_proj: float32 [768, 128], replicated
The draws below stay inside these ranges and needn't reach their ends.
Inputs may be any that keep to these rules, and one draw needn't show every extreme that they name: `segment_ids`: within each row the ids never fall; each id covers 1 to 256 positions, one exactly 256.
All inputs are finite; a program needn't handle non-finite values. No bound on the sum of `pad_mask` on one device may be relied on, other than what follows from the above.
Results may differ from the reference program's by a relative error of at most 0.023.
Values may be sent and summed in bfloat16 or wider, within the bound.
No kernel may reach another device: no remote copies, remote signals or barrier semaphores. Data moves between devices by JAX's collectives and lax.ppermute only.
A program may use at most 128 MiB of HBM per device.

```python
import math
import jax
import jax.numpy as jnp
import numpy as np
from jax import lax

D = 768
H = 12
DH = 64
FF = 3072
E = 128
NB = 32
SEQ = 512
ROWS_DEV = 4
NQ = 32
TOPK = 32
ROWS = 32
TOKENS = 16384
N_MP = 4


def touch_ends(values, own_key, smallest, high):
    shape = values.shape
    index_at = [jax.random.randint(jax.random.fold_in(own_key, axis), (), 0, shape[axis]) for axis in range(len(shape))]
    values = values.at[tuple(index_at)].set(smallest)
    longest = shape.index(max(shape))
    index_at[longest] = (index_at[longest] + 1) % shape[longest]
    return values.at[tuple(index_at)].set(high)


def block_scale(own_key, dims, cuts, smallest, high):
    level, own = 1.0, jax.random.fold_in(own_key, 6)
    for dim, parts in cuts:
        draws = jnp.exp(jax.random.uniform(jax.random.fold_in(own, dim), (parts,), jnp.float32, smallest / len(cuts), high / len(cuts)))
        level = level * jnp.repeat(draws, dims[dim] // parts).reshape([-1 if axis == dim else 1 for axis in range(len(dims))])
    return level


def profile(count, total, limit, slope):
    weights = [(1 << 20) // math.isqrt(rank ** slope) + 1 for rank in range(2, count + 1)]
    surplus, holding = total - limit - (count - 1), [1] * (count - 1)
    while surplus > 0:
        candidates = [i for i in range(count - 1) if holding[i] < limit]
        pool, left = sum([weights[i] for i in candidates]), surplus
        for i in candidates:
            addition = min(limit - holding[i], max(1, left * weights[i] // pool), surplus)
            holding[i] = holding[i] + addition
            surplus = surplus - addition
    return np.array([limit] + holding)


def uneven(stream_key, number_of, total, most, lean):
    if number_of == 2:
        one = jax.random.randint(stream_key, (), max(1, total - most), min(most, total - 1) + 1)
        return jnp.stack([one, total - one])
    tallies = jnp.asarray(profile(number_of, total, most, lean), jnp.int32)
    pairs = (number_of - 1) // 2
    source_of, taker = tallies[1:1 + 2 * pairs:2], tallies[2:2 + 2 * pairs:2]
    room = jnp.minimum(source_of - 1, most - taker)
    shifted = jax.random.randint(jax.random.fold_in(stream_key, 1), (pairs,), 0, 1 << 20) % (room + 1)
    tallies = tallies.at[1:1 + 2 * pairs:2].set(source_of - shifted).at[2:2 + 2 * pairs:2].set(taker + shifted)
    return tallies[jax.random.permutation(jax.random.fold_in(stream_key, 2), number_of)]


def scatter_about(own_key, extent, scale, limit, split=(), kind=jnp.bfloat16):
    level = block_scale(own_key, extent, split, -0.22, 0.18) if split else 1.0
    values = jax.random.normal(own_key, extent, jnp.float32) * scale * level
    return jnp.minimum(jnp.maximum(values, -limit), limit).astype(kind)


def setup_inputs(seed: int = 0) -> dict:
    key_list = jax.random.split(jax.random.key(seed), 19)
    return {
        "tokens": scatter_about(key_list[0], (TOKENS, D), 1.0, 6.0, ((0, 8),)),
        "segment_ids": jax.vmap(lambda own: jnp.searchsorted(jnp.cumsum(uneven(own, 4, SEQ, SEQ // 2, 0)), jnp.arange(SEQ), side="right"))(jax.random.split(key_list[1], ROWS)).reshape((ROWS, SEQ)).astype(jnp.int32),
        "pad_mask": touch_ends((jax.random.randint(key_list[2], (ROWS, SEQ), 0, 8) < 7).astype(jnp.int32), jax.random.fold_in(key_list[2], 1), 0, 1),
        "top_index": touch_ends(jax.random.randint(key_list[3], (ROWS, NQ, TOPK), 0, SEQ), jax.random.fold_in(key_list[3], 1), 0, SEQ - 1).astype(jnp.int32),
        "query_emb": scatter_about(key_list[4], (ROWS, NQ, E), 1.0, 6.0, ((0, 8),)),
        "score_cot": scatter_about(key_list[5], (ROWS, NQ, TOPK), 1.0, 6.0, ((0, 8),), jnp.float32),
        "gain_attn": jnp.clip(1.0 + 0.15 * jax.random.normal(key_list[6], (D,), jnp.float32), 0.25, 1.75).astype(jnp.bfloat16),
        "w_query": scatter_about(key_list[7], (D, H * DH), (D * DH) ** -0.5, 0.02734375, ((1, 4),)),
        "w_key": scatter_about(key_list[8], (D, H * DH), D ** -0.5, 0.21875, ((1, 4),)),
        "w_value": scatter_about(key_list[9], (D, H * DH), D ** -0.5, 0.21875, ((1, 4),)),
        "w_out": scatter_about(key_list[10], (H * DH, D), (max(1, H * DH // 64)) ** -0.5, 1.75, ((0, 4),)),
        "rel_table": scatter_about(key_list[11], (NB, H), 1.0, 4.0, ((1, 4),)),
        "gain_ffn": jnp.clip(1.0 + 0.15 * jax.random.normal(key_list[12], (D,), jnp.float32), 0.25, 1.75).astype(jnp.bfloat16),
        "w_gate": scatter_about(key_list[13], (D, FF), D ** -0.5, 0.21875, ((1, 4),)),
        "w_up": scatter_about(key_list[14], (D, FF), D ** -0.5, 0.21875, ((1, 4),)),
        "w_down": scatter_about(key_list[15], (FF, D), FF ** -0.5, 0.109375, ((0, 4),)),
        "gain_final": jnp.clip(1.0 + 0.15 * jax.random.normal(key_list[16], (D,), jnp.float32), 0.25, 1.75).astype(jnp.bfloat16),
        "w_proj": scatter_about(key_list[17], (D, E), D ** -0.5, 0.21875),
    }


highest = lax.Precision.HIGHEST

@jax.custom_vjp
def low(v):
    return lax.optimization_barrier(v.astype(jnp.bfloat16)).astype(jnp.float32)

@jax.custom_vjp
def low_back(v):
    return v

def low_keep(v):
    return (low(v), None)

def low_pass(kept, grad):
    return (grad,)

def back_keep(v):
    return (v, None)

def back_low(kept, grad):
    return (low(grad),)
low.defvjp(low_keep, low_pass)
low_back.defvjp(back_keep, back_low)

def bucket_table():
    places = jnp.arange(SEQ, dtype=jnp.int32)
    offset = places[None, :] - places[:, None]
    distance = jnp.abs(offset)
    far_bucket = 8 + sum(((distance >= threshold).astype(jnp.int32) for threshold in (12, 16, 23, 32, 46, 64, 91)))
    return jnp.where(distance < 8, distance, far_bucket) + 16 * (offset > 0).astype(jnp.int32)

def rms_norm(values, gain):
    scale = lax.rsqrt(lax.optimization_barrier(jnp.mean(values * values, axis=-1, keepdims=True)) + 1e-06)
    return values * scale * gain

def attend_row(query, keys, values, allowed, bias):
    logits = jnp.einsum('qhd,khd->hqk', query, keys, precision=highest)
    logits = low_back(logits) + bias
    logits = jnp.where(allowed[None], logits, -1e+30)
    largest = lax.optimization_barrier(jnp.max(logits, axis=-1, keepdims=True))
    weights = jnp.exp(logits - largest)
    probs = weights / lax.optimization_barrier(jnp.sum(weights, axis=-1, keepdims=True))
    return jnp.einsum('hqk,khd->qhd', low(probs), values, precision=highest)

def forward(params, rows_in, segments, padding, picks, queries):
    gain_attn, w_query, w_key, w_value, w_out, rel_table, gain_ffn, w_gate, w_up, w_down, gain_final, w_proj = params
    count = segments.shape[0]
    normed_attn = low(rms_norm(rows_in, gain_attn))
    shape_heads = (count, SEQ, H, DH)
    query = low_back(low(jnp.dot(normed_attn, w_query, precision=highest))).reshape(shape_heads)
    keys = low_back(low(jnp.dot(normed_attn, w_key, precision=highest))).reshape(shape_heads)
    values = low_back(low(jnp.dot(normed_attn, w_value, precision=highest))).reshape(shape_heads)
    bias = jnp.transpose(rel_table[bucket_table()], (2, 0, 1))
    allowed = (segments[:, :, None] == segments[:, None, :]) & ((padding[:, None, :] == 1) | jnp.eye(SEQ, dtype=bool)[None])
    row_step = jax.checkpoint(lambda items: attend_row(items[0], items[1], items[2], items[3], bias))
    mixed = lax.map(row_step, (query, keys, values, allowed))
    mixed = low_back(low(mixed)).reshape(count * SEQ, N_MP, H * DH // N_MP)
    attn_parts = jnp.einsum('tgc,gcd->gtd', mixed, w_out.reshape(N_MP, H * DH // N_MP, D), precision=highest)
    hidden_attn = rows_in + lax.optimization_barrier(jnp.sum(low_back(low(attn_parts)), axis=0))
    normed_ffn = low(rms_norm(hidden_attn, gain_ffn))
    gate = low_back(jnp.dot(normed_ffn, w_gate, precision=highest))
    up_proj = low_back(jnp.dot(normed_ffn, w_up, precision=highest))
    inner = low(jax.nn.gelu(gate, approximate=True) * up_proj).reshape(count * SEQ, N_MP, FF // N_MP)
    ffn_parts = jnp.einsum('tgf,gfd->gtd', inner, w_down.reshape(N_MP, FF // N_MP, D), precision=highest)
    hidden_ffn = hidden_attn + lax.optimization_barrier(jnp.sum(low_back(low(ffn_parts)), axis=0))
    normed_final = low(rms_norm(hidden_ffn, gain_final))
    embed = low_back(jnp.dot(normed_final, w_proj, precision=highest))
    inverse = lax.rsqrt(lax.optimization_barrier(jnp.sum(embed * embed, axis=-1, keepdims=True)) + 1e-06)
    unit = embed * inverse * padding.reshape(-1, 1).astype(jnp.float32)
    unit = low(unit).reshape(count, SEQ, E)
    chosen = jax.vmap(lambda table_rows, positions: table_rows[positions])(unit, picks)
    chosen = low_back(chosen)
    return lax.optimization_barrier(jnp.sum(chosen * queries[:, :, None, :], axis=-1))

def reference(tokens, segment_ids, pad_mask, top_index, query_emb, score_cot, gain_attn, w_query, w_key, w_value, w_out, rel_table, gain_ffn, w_gate, w_up, w_down, gain_final, w_proj):
    params = tuple((weight.astype(jnp.float32) for weight in (gain_attn, w_query, w_key, w_value, w_out, rel_table, gain_ffn, w_gate, w_up, w_down, gain_final, w_proj)))
    groups = segment_ids.shape[0] // ROWS_DEV
    inputs = tokens.astype(jnp.float32).reshape(groups, ROWS_DEV * SEQ, D)
    segments = segment_ids.reshape(groups, ROWS_DEV, SEQ)
    padding = pad_mask.reshape(groups, ROWS_DEV, SEQ)
    picks = top_index.reshape(groups, ROWS_DEV, NQ, TOPK)
    queries = query_emb.astype(jnp.float32).reshape(groups, ROWS_DEV, NQ, E)
    cotangent = score_cot.reshape(groups, ROWS_DEV, NQ, TOPK)

    def step(totals, items):
        rows_in, seg_rows, pad_rows, pick_rows, query_rows, cot_rows = items
        result, pullback = jax.vjp(lambda weights, values: forward(weights, values, seg_rows, pad_rows, pick_rows, query_rows), params, rows_in)
        grad_params, grad_input = pullback(cot_rows)
        return (jax.tree.map(lambda first, second: first + second, totals, grad_params), (result, grad_input))
    zeros = tuple((jnp.zeros_like(weight) for weight in params))
    totals, (result, grad_input) = lax.scan(step, zeros, (inputs, segments, padding, picks, queries, cotangent))
    return (result.reshape(ROWS, NQ, TOPK), grad_input.reshape(TOKENS, D), totals[0], totals[1], totals[2], totals[3], totals[4], totals[5], totals[6], totals[7], totals[8], totals[9], totals[10], totals[11])
```

```python
import functools
import math

import jax
import jax.numpy as jnp
import numpy as np
from jax import lax
from jax.experimental import pallas as pl
from jax.experimental.pallas import tpu as pltpu
from jax.sharding import Mesh
from jax.sharding import PartitionSpec as P

f32 = jnp.float32
bf16 = jnp.bfloat16
eps = 1e-06
masked_logit = -1e30
gelu_c = math.sqrt(2.0 / math.pi)
CORE, XBIT, YBIT = "core", "x", "y"
group = ("y", "x", "core")
dp = ("out",) + group
span = 1024
tile = 128


def bucket_hot(buckets, length):
    column = np.arange(span)
    base = length - tile
    offset = np.where(column < base + length, column - base, column - span - base)
    distance = np.abs(offset)
    far = 8 + sum((distance >= t).astype(np.int32) for t in (12, 16, 23, 32, 46, 64, 91))
    bucket = np.where(distance < 8, distance, far) + 16 * (offset > 0)
    hot = (bucket[None, :] == np.arange(tile)[:, None]) & (np.arange(tile)[:, None] < buckets)
    return hot.astype(np.float32)


def dot(a, b, dims=((1,), (0,))):
    return lax.dot_general(a, b, (dims, ((), ())), preferred_element_type=f32)


def rms_scale(v):
    return lax.rsqrt(jnp.mean(v * v, axis=-1, keepdims=True) + eps)


def rms_back(v, gain, grad):
    s = rms_scale(v)
    w = grad * gain
    value = s * w - v * ((s * s * s) * jnp.mean(w * v, axis=-1, keepdims=True))
    return value, jnp.sum(grad * v * s, axis=0, keepdims=True)


def params(mib):
    return pltpu.CompilerParams(
        vmem_limit_bytes=mib << 20, dimension_semantics=("arbitrary",)
    )


def whole(shape):
    return pl.BlockSpec(shape, lambda *_: (0,) * len(shape))


ANY = pl.BlockSpec(memory_space=pl.ANY)


class Place:
    def __init__(self):
        self.n_out, self.n_mp = lax.axis_size("out"), lax.axis_size("mp")
        self.c, self.x, self.y = (lax.axis_index(name) for name in ("core", "x", "y"))
        self.z = lax.axis_index("mp")
        self.p = self.c * 4 + self.y * 2 + self.x

    def swap(self, v, name):
        return lax.ppermute(v, name, [(0, 1), (1, 0)])

    def shift(self, v, k):
        n = self.n_mp
        return lax.ppermute(v, "mp", [(i, (i + k) % n) for i in range(n)])

    def offsets(self, rows):
        half = rows // 2
        out = []
        for flip in (0, 4):
            p = self.p ^ flip
            for other, extra in (
                (0, 0), (1, 0), (0, half), (2, half), (2, 0), (3, 0), (1, half), (3, half),
            ):
                out.append((p ^ other) * rows + extra)
        return jnp.stack(out + [self.z, self.c, self.x, self.y]).astype(jnp.int32)

    def first_round(self, a, b, after=()):
        return stack_pairs(a, self.swap(a, XBIT), b, self.swap(b, YBIT), after)

    def second_round(self, sa, sb):
        near = [sa, sb, self.swap(sa, YBIT), self.swap(sb, XBIT)]
        return near + [self.swap(t, CORE) for t in near]


def pick(v, axis, index):
    return lax.dynamic_index_in_dim(v, index, axis, keepdims=False)


def halves(v, axis):
    half = v.shape[axis] // 2
    return (
        lax.slice_in_dim(v, 0, half, axis=axis),
        lax.slice_in_dim(v, half, 2 * half, axis=axis),
    )


def chunk_copies(offs, own, arrays, dst, sems, first=0):
    slots, rows, width = dst.shape
    half = rows // 16
    pairs = [
        (ref, dst.at[0, :, pl.ds(column, ref.shape[1])]) for ref, column in own
    ]
    for at in range(16):
        src = arrays[at // 2].at[at % 2]
        if src.shape[2] != width:
            src = src.at[:, :, pl.ds(first, width)]
        start = pl.multiple_of(offs[at], 16)
        pairs.append((src, dst.at[pl.ds(1, slots - 1), pl.ds(start, half), :]))
    return [pltpu.make_async_copy(s, d, sems.at[i]) for i, (s, d) in enumerate(pairs)]


copies_per_chunk = 20


def gathered_copies(gathered, dst, sems, shard=None):
    full = gathered.shape[4]
    out = []
    for at, (c, y, x) in enumerate(np.ndindex(2, 2, 2)):
        rows = pl.ds(at * full, full)
        if shard is None:
            out.append((gathered.at[y, x, c], dst.at[:, rows, :]))
        else:
            out.append((gathered.at[y, x, c, shard], dst.at[rows, :]))
    return [pltpu.make_async_copy(s, d, sems.at[i]) for i, (s, d) in enumerate(out)]


def split_kernel(slots, *refs):
    a_ref, b_ref = refs[-2:]
    half = a_ref.shape[1]
    for k in range(slots):
        a_ref[k] = refs[k][:half, :]
        b_ref[k] = refs[k][half:, :]


def split(arrays, after=()):
    rows, width = arrays[0].shape
    out = (len(arrays), rows // 2, width)
    return pl.pallas_call(
        functools.partial(split_kernel, len(arrays)),
        grid=(1,),
        in_specs=[whole(arrays[0].shape)] * len(arrays) + [ANY] * len(after),
        out_specs=[whole(out)] * 2,
        out_shape=[jax.ShapeDtypeStruct(out, bf16)] * 2,
        compiler_params=params(16),
        name="split",
    )(*arrays, *after)


def skew(base):
    t = jnp.broadcast_to(base, (8, span))
    row = lax.broadcasted_iota(jnp.int32, (8, span), 0)
    for step in (1, 2, 4):
        t = jnp.where((row & step) != 0, pltpu.roll(t, step, 1), t)
    while t.shape[0] < tile:
        t = jnp.concatenate([t, pltpu.roll(t, t.shape[0], 1)], axis=0)
    return t


def unskew(t):
    while t.shape[0] > 8:
        n = t.shape[0] // 2
        t = t[:n] + pltpu.roll(t[n:], span - n, 1)
    row = lax.broadcasted_iota(jnp.int32, (8, span), 0)
    for step in (1, 2, 4):
        t = jnp.where((row & step) != 0, pltpu.roll(t, span - step, 1), t)
    return jnp.sum(t, axis=0, keepdims=True)


def fill_mask(mask, segs, pads, seg_cols, row):
    length = mask.shape[0]
    rows = segs.shape[0]
    chosen = lax.broadcasted_iota(jnp.int32, (rows, length), 0) == row
    seg_k = jnp.sum(jnp.where(chosen, segs, 0.0), axis=0, keepdims=True)
    pad_k = jnp.sum(jnp.where(chosen, pads, 0.0), axis=0, keepdims=True)
    code = jnp.where(pad_k == 1.0, seg_k, -1.0)
    lane = lax.broadcasted_iota(jnp.int32, seg_cols.shape, 1)
    seg_q = jnp.sum(jnp.where(lane == row, seg_cols, 0.0), axis=1, keepdims=True)
    q = lax.broadcasted_iota(jnp.int32, (tile, length), 0)
    k = lax.broadcasted_iota(jnp.int32, (tile, length), 1)
    for a in range(length // tile):
        own = seg_q[a * tile : (a + 1) * tile]
        ok = (own == code) | (q + a * tile == k)
        mask[a * tile : (a + 1) * tile, :] = jnp.where(ok, 0.0, masked_logit)


def fill_bias(bias, table, hot, heads):
    base = dot(table, hot[0 : table.shape[1], :])
    for h in range(heads):
        bias[h] = skew(base[h : h + 1, :])


def normalize(x_ref, gain, normed):
    for a in range(x_ref.shape[0] // tile):
        rows = slice(a * tile, (a + 1) * tile)
        v = x_ref[rows, :].astype(f32)
        normed[rows, :] = (v * rms_scale(v) * gain).astype(bf16)


def attend_kernel(
    first, heads, size, sc, x_ref, seg_ref, pad_ref, segc_ref, gain_ref, w_ref, hot_ref,
    out_ref, normed, qkv, mask, bias,
):
    length = x_ref.shape[0]
    wide = heads * size
    buckets = 32
    row = lax.rem(sc[16] + first + pl.program_id(0), seg_ref.shape[0])
    normalize(x_ref, gain_ref[...], normed)
    qkv[...] = dot(normed[...], w_ref[: 3 * wide, :], ((1,), (1,))).astype(bf16)
    fill_mask(mask, seg_ref[...], pad_ref[...], segc_ref[...], row)

    @pl.when(pl.program_id(0) == 0)
    def _():
        fill_bias(bias, w_ref[3 * wide : 3 * wide + 16, :tile][:, :buckets], hot_ref, heads)

    for h in range(heads):
        q_at, k_at, v_at = h * size, wide + h * size, 2 * wide + h * size
        keys = qkv[:, k_at : k_at + size]
        values = qkv[:, v_at : v_at + size]
        for a in range(length // tile):
            rows = slice(a * tile, (a + 1) * tile)
            at = length - tile - a * tile
            s = dot(qkv[rows, q_at : q_at + size], keys, ((1,), (1,)))
            s = s + bias[h, :, at : at + length] + mask[rows, :]
            e = jnp.exp(s - jnp.max(s, axis=1, keepdims=True))
            p = (e * (1.0 / jnp.sum(e, axis=1, keepdims=True))).astype(bf16)
            out_ref[0, rows, q_at : q_at + size] = dot(p, values).astype(bf16)
    out_ref[0, length:, :] = w_ref[3 * wide : 3 * wide + 16, :wide]


def attend(first, offs, tokens, segs, pads, seg_cols, gain, w_qkv, hot, heads, size):
    rows, length = segs.shape
    d = tokens.shape[1]
    wide = heads * size
    grid = pltpu.PrefetchScalarGridSpec(
        num_scalar_prefetch=1,
        grid=(rows,),
        in_specs=[
            pl.BlockSpec((length, d), lambda i, sc: (lax.rem(sc[16] + first + i, rows), 0)),
            whole(segs.shape),
            whole(pads.shape),
            whole(seg_cols.shape),
            whole(gain.shape),
            whole(w_qkv.shape),
            whole(hot.shape),
        ],
        out_specs=pl.BlockSpec((1, length + 16, wide), lambda i, sc: (i, 0, 0)),
        scratch_shapes=[
            pltpu.VMEM((length, d), bf16),
            pltpu.VMEM((length, 3 * wide), bf16),
            pltpu.VMEM((length, length), f32),
            pltpu.VMEM((heads, tile, span), f32),
        ],
    )
    return pl.pallas_call(
        functools.partial(attend_kernel, first, heads, size),
        grid_spec=grid,
        out_shape=jax.ShapeDtypeStruct((rows, length + 16, wide), bf16),
        compiler_params=params(24),
        cost_estimate=pl.CostEstimate(
            flops=rows * (2 * length * d * 3 * wide + 4 * wide * length * length),
            bytes_accessed=4 << 20,
            transcendentals=rows * heads * length * length,
        ),
        name="attend",
    )(offs, tokens, segs, pads, seg_cols, gain, w_qkv, hot)


def high_low(v):
    high = v.astype(bf16)
    return high, (v - high.astype(f32)).astype(bf16)


def attend_back_kernel(
    slot, last, heads, size, n_after, sc, x_ref, seg_ref, pad_ref, segc_ref, gain_ref, hot_ref,
    gm_ref, mixed_ref, *refs,
):
    refs = list(refs)
    acc_in = refs.pop(0) if slot else None
    if last:
        gha_ref, gat_ref, fin_ref, mid_ref, score_ref = refs[:5]
        tables, refs = refs[5 : 5 + slot], refs[5 + slot :]
    w_ref = refs[0]
    refs = refs[1 + n_after + (1 if slot else 0) :]
    left_ref, table_out = refs[:2]
    if last:
        dx_ref, both_ref, small_ref, acc = refs[2:6]
        refs = refs[6:]
    else:
        acc, refs = refs[2], refs[3:]
    w, sems, normed, qkv, mask, bias, probs, dlog, skewed, diag, dqkv = refs
    length, d = x_ref.shape
    wide = heads * size
    row = sc[16]
    gain = gain_ref[...]
    blocks = length // tile
    shard = lax.rem(row + 4 - slot, 4)
    copies = gathered_copies(w_ref, w, sems, shard)
    for copy in copies:
        copy.start()
    normalize(x_ref, gain, normed)
    fill_mask(mask, seg_ref[...], pad_ref[...], segc_ref[...], row)
    fill_bias(bias, mixed_ref[length:, :tile][:, :32], hot_ref, heads)
    diag[...] = jnp.zeros_like(diag)
    for copy in copies:
        copy.wait()
    qkv[...] = dot(normed[...], w[: 3 * wide, :], ((1,), (1,))).astype(bf16)
    for h in range(heads):
        q_at, k_at, v_at = h * size, wide + h * size, 2 * wide + h * size
        here = slice(q_at, q_at + size)
        query = qkv[:, q_at : q_at + size]
        keys = qkv[:, k_at : k_at + size]
        values = qkv[:, v_at : v_at + size]
        grad = gm_ref[0, :, here]
        skewed[...] = jnp.zeros_like(skewed)
        for a in range(blocks):
            rows = slice(a * tile, (a + 1) * tile)
            at = length - tile - a * tile
            s = dot(query[rows], keys, ((1,), (1,)))
            s = s + bias[h, :, at : at + length] + mask[rows, :]
            e = jnp.exp(s - jnp.max(s, axis=1, keepdims=True))
            p = e * (1.0 / jnp.sum(e, axis=1, keepdims=True))
            probs[rows, :] = p.astype(bf16)
            gp = dot(grad[rows], values, ((1,), (1,)))
            gl = p * (gp - jnp.sum(gp * p, axis=1, keepdims=True))
            dlog[rows, :] = gl.astype(bf16)
            skewed[:, at : at + length] += gl
        diag[h : h + 1, :] = unskew(skewed[...])
        for part, value in (
            (0, dot(dlog[...], keys)),
            (1, dot(dlog[...], query, ((0,), (0,)))),
            (2, dot(probs[...], grad, ((0,), (0,)))),
        ):
            value = value.astype(bf16)
            left_ref[0, part, :, here] = value
            dqkv[:, part * wide + q_at : part * wide + q_at + size] = value
    left_ref[0, 3] = mixed_ref[:length, :]
    high, low = high_low(diag[...])
    table = dot(high, hot_ref[...], ((1,), (1,))) + dot(low, hot_ref[...], ((1,), (1,)))
    table_out[...] = table
    value = dot(dqkv[...], w[: 3 * wide, :])
    acc[...] = value if acc_in is None else acc_in[...] + value
    if not last:
        return
    total = jnp.zeros((1, d), f32)
    for a in range(blocks):
        rows = slice(a * tile, (a + 1) * tile)
        back, part = rms_back(x_ref[rows, :].astype(f32), gain, acc[rows, :])
        dx_ref[rows, :] = (gha_ref[rows, :] + back).astype(bf16)
        total = total + part
    both_ref[0] = normed[...]
    both_ref[1] = gat_ref[...]
    dx_ref[length:, :] = jnp.zeros((dx_ref.shape[0] - length, d), bf16)
    n = score_ref.shape[0] // 16
    cols = score_ref.shape[1]
    high, low = high_low(score_ref[...])
    for i in range(n):
        rows = slice(16 * i, 16 * i + 16)
        dx_ref[length : length + 16, 2 * i * tile : 2 * i * tile + cols] = high[rows]
        dx_ref[length : length + 16, (2 * i + 1) * tile : (2 * i + 1) * tile + cols] = low[rows]
    line = lax.broadcasted_iota(jnp.int32, (8, d), 0)
    gains = jnp.where(
        line == 0, total, jnp.where(line == 1, fin_ref[...], jnp.where(line == 2, mid_ref[...], 0.0))
    )
    line = lax.broadcasted_iota(jnp.int32, (8, tile), 0)
    column = lax.broadcasted_iota(jnp.int32, (8, tile), 1)

    def turned(value, at):
        place = jnp.where(column == line + at, 1.0, 0.0).astype(bf16)
        high, low = high_low(value)
        return dot(high, place, ((0,), (0,))) + dot(low, place, ((0,), (0,)))

    gains = turned(gains, 0)
    for k, value in enumerate([t[...] for t in tables] + [table]):
        small_ref[k] = gains.astype(bf16)
        small_ref[k, 0:tile, :] = (gains[0:tile] + turned(value, tile // 2)).astype(bf16)


def attend_back(
    slot, common, grad_mixed, mixed, acc, left, finish, weights, heads, size, after=()
):
    offs, tokens, segs, pads, seg_cols, gain, hot = common
    rows, length = segs.shape
    d = tokens.shape[1]
    slots = grad_mixed.shape[0]
    wide = heads * size
    last = slot == slots - 1
    args = [offs, tokens, segs, pads, seg_cols, gain, hot, grad_mixed, mixed]
    specs = [
        pl.BlockSpec((length, d), lambda i, sc: (sc[16], 0)),
        whole(segs.shape),
        whole(pads.shape),
        whole(seg_cols.shape),
        whole(gain.shape),
        whole(hot.shape),
        pl.BlockSpec((1, length, wide), lambda i, sc: (slot, 0, 0)),
        whole(mixed.shape),
    ]
    if slot:
        args.append(acc)
        specs.append(whole(acc.shape))
    if last:
        args += finish
        specs += [whole(v.shape) for v in finish]
    args += [weights] + ([left] if slot else []) + list(after)
    specs += [ANY] * (1 + len(after) + (1 if slot else 0))
    out_specs = [
        pl.BlockSpec((1, 4, length, wide), lambda i, sc: (slot, 0, 0, 0)),
        whole((8, tile)),
    ]
    out_shape = [
        jax.ShapeDtypeStruct((slots, 4, length, wide), bf16),
        jax.ShapeDtypeStruct((8, tile), f32),
    ]
    scratch = []
    if last:
        for shape in ((length + 16, d), (2, length, d), (slots, d, tile)):
            out_specs.append(whole(shape))
            out_shape.append(jax.ShapeDtypeStruct(shape, bf16))
        scratch = [pltpu.VMEM((length, d), f32)]
    else:
        out_specs.append(whole((length, d)))
        out_shape.append(jax.ShapeDtypeStruct((length, d), f32))
    grid = pltpu.PrefetchScalarGridSpec(
        num_scalar_prefetch=1,
        grid=(1,),
        in_specs=specs,
        out_specs=out_specs,
        scratch_shapes=scratch
        + [
            pltpu.VMEM((8 * weights.shape[4], d), bf16),
            pltpu.SemaphoreType.DMA((8,)),
            pltpu.VMEM((length, d), bf16),
            pltpu.VMEM((length, 3 * wide), bf16),
            pltpu.VMEM((length, length), f32),
            pltpu.VMEM((heads, tile, span), f32),
            pltpu.VMEM((length, length), bf16),
            pltpu.VMEM((length, length), bf16),
            pltpu.VMEM((tile, span), f32),
            pltpu.VMEM((8, span), f32),
            pltpu.VMEM((length, 3 * wide), bf16),
        ],
    )
    return pl.pallas_call(
        functools.partial(attend_back_kernel, slot, last, heads, size, len(after)),
        grid_spec=grid,
        out_shape=out_shape,
        input_output_aliases={len(args) - len(after) - 1: 0} if slot else {},
        compiler_params=params(58),
        cost_estimate=pl.CostEstimate(
            flops=12 * length * d * wide + 14 * wide * length * length,
            bytes_accessed=16 << 20,
            transcendentals=heads * length * length,
        ),
        name=f"attend_back{slot}",
    )(*args)


def ffn_in_kernel(n_after, sc, x_ref, gain_ref, *refs):
    slots = 4
    mixed, own, arrays = refs[:slots], refs[slots : slots + 3], refs[slots + 3 : slots + 11]
    refs = refs[slots + 11 + n_after :]
    hid_ref, normed_ref, act_ref, dact_ref, inner_ref, w, sems = refs
    length, d = x_ref.shape
    slot = pl.program_id(0)
    hidden = act_ref.shape[2]
    copies = chunk_copies(sc, zip(own, (0, hidden, 2 * hidden)), arrays, w, sems)

    @pl.when(slot == 0)
    def _():
        for copy in copies:
            copy.start()
        for copy in copies:
            copy.wait()
        gain = gain_ref[...]
        for a in range(length // tile):
            rows = slice(a * tile, (a + 1) * tile)
            h = x_ref[rows, :].astype(f32)
            for k in range(slots):
                h = h + dot(mixed[k][rows, :], w[k, :, 2 * hidden :], ((1,), (1,)))
            hid_ref[rows, :] = h
            normed_ref[rows, :] = (h * rms_scale(h) * gain).astype(bf16)

    def step(n, carry):
        at = pl.multiple_of(n * 256, 256)
        cols = pl.ds(at, 256)
        normed = normed_ref[...]
        gate = dot(normed, w[slot, :, cols])
        up = dot(normed, w[slot, :, pl.ds(at + hidden, 256)])
        t = jnp.tanh(gelu_c * (gate + 0.044715 * gate * gate * gate))
        half = 0.5 * (1.0 + t)
        act = gate * half
        slope = half + 0.5 * gate * (1.0 - t * t) * (
            gelu_c * (1.0 + 3 * 0.044715 * gate * gate)
        )
        act_ref[0, :, cols] = act.astype(bf16)
        dact_ref[0, :, cols] = (up * slope).astype(bf16)
        inner_ref[0, :, cols] = (act * up).astype(bf16)
        return carry

    lax.fori_loop(0, hidden // 256, step, 0)


def ffn_in(offs, tokens, gain, mixed, own, arrays, length, after=()):
    d = tokens.shape[1]
    slots = len(mixed)
    hidden = own[0].shape[1]
    width = arrays[0].shape[3]
    per_slot = pl.BlockSpec((1, length, hidden), lambda i, sc: (i, 0, 0))
    grid = pltpu.PrefetchScalarGridSpec(
        num_scalar_prefetch=1,
        grid=(slots,),
        in_specs=[
            pl.BlockSpec((length, d), lambda i, sc: (sc[16], 0)),
            whole(gain.shape),
        ]
        + [whole(m.shape) for m in mixed]
        + [ANY] * (11 + len(after)),
        out_specs=[whole((length, d)), whole((length, d))] + [per_slot] * 3,
        scratch_shapes=[
            pltpu.VMEM((slots, d, width), bf16),
            pltpu.SemaphoreType.DMA((copies_per_chunk,)),
        ],
    )
    three = jax.ShapeDtypeStruct((slots, length, hidden), bf16)
    return pl.pallas_call(
        functools.partial(ffn_in_kernel, len(after)),
        grid_spec=grid,
        out_shape=[
            jax.ShapeDtypeStruct((length, d), f32),
            jax.ShapeDtypeStruct((length, d), bf16),
            three,
            three,
            three,
        ],
        compiler_params=params(58),
        cost_estimate=pl.CostEstimate(
            flops=2 * length * d * (d + 2 * slots * hidden),
            bytes_accessed=24 << 20,
            transcendentals=slots * length * hidden,
        ),
        name="ffn_in",
    )(offs, tokens, gain, *mixed, *own, *arrays, *after)


def middle_kernel(
    sc, hid_ref, inner_ref, act_ref, dact_ref, gfin_ref, gffn_ref, wp_ref, padc_ref, query_ref,
    cot_ref, top_ref, *refs,
):
    slots = 4
    own, first, second = refs[:3], refs[3:11], refs[11]
    (
        score_ref, nfin, ge, gain_fin_ref, gain_ffn_ref, gft_ref, gg_ref, gu_ref, gha_ref,
        gat_ref, gm_ref,
    ) = refs[12:23]
    w, wd, w_sems, d_sems, acc, embed, unit = refs[23:]
    length, d = hid_ref.shape
    hidden = wd.shape[1]
    step = pl.program_id(0)
    w_copies = chunk_copies(sc, zip(own, (0, hidden, 2 * hidden)), first, w, w_sems)
    d_copies = gathered_copies(second, wd, d_sems)

    def shard(k):
        return lax.rem(sc[16] + slots - k, slots)

    blocks = length // tile

    @pl.when(step == 0)
    def _():
        for copy in d_copies + w_copies:
            copy.start()
        acc[...] = hid_ref[...]
        for copy in d_copies:
            copy.wait()

    @pl.when(step < slots)
    def _():
        acc[...] += dot(inner_ref[0], wd[shard(step)])

    @pl.when(step == slots - 1)
    def _():
        lane = lax.broadcasted_iota(jnp.int32, padc_ref.shape, 1)
        pad = jnp.sum(jnp.where(lane == sc[16], padc_ref[...], 0.0), axis=1, keepdims=True)
        gain = gfin_ref[...]
        for a in range(blocks):
            rows = slice(a * tile, (a + 1) * tile)
            h = acc[rows, :]
            n = (h * rms_scale(h) * gain).astype(bf16)
            nfin[rows, :] = n
            e = dot(n, wp_ref[...])
            embed[rows, :] = e
            inverse = lax.rsqrt(jnp.sum(e * e, axis=1, keepdims=True) + eps)
            unit[rows, :] = (e * inverse * pad[rows]).astype(bf16)
        query = query_ref[0]
        cot = cot_ref[0]
        top = top_ref[0]
        scored = dot(query, unit[...], ((1,), (1,)))
        place = lax.broadcasted_iota(jnp.int32, scored.shape, 1)
        out_lane = lax.broadcasted_iota(jnp.int32, cot.shape, 1)
        chosen = jnp.zeros_like(cot)
        weight = jnp.zeros_like(scored)
        for j in range(top.shape[1]):
            here = place == top[:, j : j + 1]
            mine = jnp.sum(jnp.where(here, scored, 0.0), axis=1, keepdims=True)
            chosen = jnp.where(out_lane == j, mine, chosen)
            weight = weight + jnp.where(here, cot[:, j : j + 1], 0.0)
        score_ref[...] = chosen
        high = weight.astype(bf16)
        low = (weight - high.astype(f32)).astype(bf16)
        gunit = dot(high, query, ((0,), (0,))) + dot(low, query, ((0,), (0,)))
        total = jnp.zeros((1, d), f32)
        for a in range(blocks):
            rows = slice(a * tile, (a + 1) * tile)
            e = embed[rows, :]
            inverse = lax.rsqrt(jnp.sum(e * e, axis=1, keepdims=True) + eps)
            u = gunit[rows] * pad[rows]
            cube = (inverse * inverse * inverse) * jnp.sum(u * e, axis=1, keepdims=True)
            g = (inverse * u - e * cube).astype(bf16)
            ge[rows, :] = g
            back, part = rms_back(acc[rows, :], gain, dot(g, wp_ref[...], ((1,), (1,))))
            total = total + part
            gha_ref[rows, :] = back
            gft_ref[rows, :] = back.astype(bf16)
        gain_fin_ref[...] = total
        acc[...] = jnp.zeros_like(acc)
        for copy in w_copies:
            copy.wait()

    @pl.when(step >= slots)
    def _():
        k = step - slots

        def part(n, carry):
            cols = pl.ds(pl.multiple_of(n * 256, 256), 256)
            gi = dot(gft_ref[...], wd[shard(k), cols, :], ((1,), (1,)))
            gg_ref[0, :, cols] = (gi * dact_ref[0, :, cols].astype(f32)).astype(bf16)
            gu_ref[0, :, cols] = (gi * act_ref[0, :, cols].astype(f32)).astype(bf16)
            return carry

        lax.fori_loop(0, hidden // 256, part, 0)
        acc[...] += dot(gg_ref[0], w[k, :, :hidden], ((1,), (1,))) + dot(
            gu_ref[0], w[k, :, hidden : 2 * hidden], ((1,), (1,))
        )

    @pl.when(step == 2 * slots - 1)
    def _():
        gain = gffn_ref[...]
        total = jnp.zeros((1, d), f32)
        for a in range(blocks):
            rows = slice(a * tile, (a + 1) * tile)
            back, part = rms_back(hid_ref[rows, :], gain, acc[rows, :])
            total = total + part
            g = gha_ref[rows, :] + back
            gha_ref[rows, :] = g
            g = g.astype(bf16)
            gat_ref[rows, :] = g
            for k in range(slots):
                gm_ref[k, rows, :] = dot(g, w[k, :, 2 * hidden :]).astype(bf16)
        gain_ffn_ref[...] = total


def middle(
    offs, hid, inner, act, dact, gain_final, gain_ffn, w_proj, pad_cols, query, cot, top,
    own, first, second,
):
    length, d = hid.shape
    slots, _, hidden = inner.shape
    width = first[0].shape[3]
    wide = width - 2 * hidden
    e = w_proj.shape[1]

    def row_block(v):
        return pl.BlockSpec((1,) + v.shape[1:], lambda i, sc: (sc[16], 0, 0))

    early = pl.BlockSpec((1, length, hidden), lambda i, sc: (jnp.minimum(i, slots - 1), 0, 0))
    late = pl.BlockSpec((1, length, hidden), lambda i, sc: (jnp.maximum(i - slots, 0), 0, 0))
    chunk = jax.ShapeDtypeStruct((slots, length, hidden), bf16)
    grid = pltpu.PrefetchScalarGridSpec(
        num_scalar_prefetch=1,
        grid=(2 * slots,),
        in_specs=[
            whole(hid.shape),
            early,
            late,
            late,
            whole(gain_final.shape),
            whole(gain_ffn.shape),
            whole(w_proj.shape),
            whole(pad_cols.shape),
            row_block(query),
            row_block(cot),
            row_block(top),
        ]
        + [ANY] * 12,
        out_specs=[
            whole(cot.shape[1:]),
            whole((length, d)),
            whole((length, e)),
            whole((1, d)),
            whole((1, d)),
            whole((length, d)),
            late,
            late,
            whole((length, d)),
            whole((length, d)),
            whole((slots, length, wide)),
        ],
        scratch_shapes=[
            pltpu.VMEM((slots, d, width), bf16),
            pltpu.VMEM((slots, hidden, d), bf16),
            pltpu.SemaphoreType.DMA((copies_per_chunk,)),
            pltpu.SemaphoreType.DMA((copies_per_chunk,)),
            pltpu.VMEM((length, d), f32),
            pltpu.VMEM((length, e), f32),
            pltpu.VMEM((length, e), bf16),
        ],
    )
    return pl.pallas_call(
        middle_kernel,
        grid_spec=grid,
        out_shape=[
            jax.ShapeDtypeStruct(cot.shape[1:], f32),
            jax.ShapeDtypeStruct((length, d), bf16),
            jax.ShapeDtypeStruct((length, e), bf16),
            jax.ShapeDtypeStruct((1, d), f32),
            jax.ShapeDtypeStruct((1, d), f32),
            jax.ShapeDtypeStruct((length, d), bf16),
            chunk,
            chunk,
            jax.ShapeDtypeStruct((length, d), f32),
            jax.ShapeDtypeStruct((length, d), bf16),
            jax.ShapeDtypeStruct((slots, length, wide), bf16),
        ],
        compiler_params=params(58),
        cost_estimate=pl.CostEstimate(
            flops=2 * length * d * (4 * slots * hidden + d),
            bytes_accessed=32 << 20,
            transcendentals=length,
        ),
        name="middle",
    )(
        offs, hid, inner, act, dact, gain_final, gain_ffn, w_proj, pad_cols, query, cot, top,
        *own, *first, second,
    )


def keep_parts(sc, out, refs):
    send_a, keep_a, send_b, keep_b = refs
    half = send_a.shape[2]
    x, y = sc[18], sc[19]

    def rows(y, x, extra):
        at = pl.multiple_of((2 * y + x) * (2 * half) + extra, 16)
        return out[pl.ds(at, half), :]

    for other in range(2):
        send_a[0, other] = rows(other, 1 - x, 0)
        keep_a[0, other] = rows(other, x, 0)
        send_b[0, other] = rows(1 - y, other, half)
        keep_b[0, other] = rows(y, other, half)


def parts_of(slots, rows, width):
    part = (1, 2, rows // 8, width)
    spec = pl.BlockSpec(part, lambda i, sc: (i, 0, 0, 0))
    return [spec] * 4, [jax.ShapeDtypeStruct((slots,) + part[1:], bf16)] * 4


def product_kernel(lefts, pairs, keep, sc, *refs):
    left_refs, right_refs = refs[:lefts], refs[lefts : lefts + len(pairs)]
    refs = refs[lefts + len(pairs) :]
    out = refs[-1] if keep else refs[-1].at[0]
    at = 0
    for right_ref, which in zip(right_refs, pairs):
        right = right_ref[...]
        left = left_refs[which][...]
        left, right = (v.reshape(v.shape[-2:]) for v in (left, right))
        cols = slice(at, at + right.shape[1])
        value = dot(left, right, ((0,), (0,)))
        if keep:
            value = value + refs[0][0, :, cols].astype(f32)
        out[:, cols] = value.astype(bf16)
        at += right.shape[1]
    if keep:
        keep_parts(sc, out, refs[1:5])


def products(offs, lefts, rights, slots, got=None):
    keep = got is not None
    length, half = lefts[0].shape[-2], lefts[0].shape[-1] // 2
    width = sum(right.shape[-1] for right, _ in rights)

    def which(sc):
        return sc[17] if keep else 1 - sc[17]

    specs = []
    for left in lefts:
        if left.ndim == 3:
            specs.append(pl.BlockSpec((1, length, half), lambda i, sc: (i, 0, which(sc))))
        else:
            specs.append(pl.BlockSpec((length, half), lambda i, sc: (0, which(sc))))
    for right, _ in rights:
        if right.ndim == 3:
            specs.append(pl.BlockSpec((1,) + right.shape[1:], lambda i, sc: (i, 0, 0)))
        else:
            specs.append(whole(right.shape))
    args = list(lefts) + [right for right, _ in rights]
    block = pl.BlockSpec((1, half, width), lambda i, sc: (i, 0, 0))
    out_specs, out_shape = block, jax.ShapeDtypeStruct((slots, half, width), bf16)
    scratch = []
    if keep:
        specs.append(block)
        args.append(got)
        out_specs, out_shape = parts_of(slots, half, width)
        scratch = [pltpu.VMEM((half, width), bf16)]
    return pl.pallas_call(
        functools.partial(product_kernel, len(lefts), [i for _, i in rights], keep),
        grid_spec=pltpu.PrefetchScalarGridSpec(
            num_scalar_prefetch=1,
            grid=(slots,),
            in_specs=specs,
            out_specs=out_specs,
            scratch_shapes=scratch,
        ),
        out_shape=out_shape,
        compiler_params=params(48),
        cost_estimate=cheap,
        name="products_keep" if keep else "products_send",
    )(offs, *args)


cheap = pl.CostEstimate(flops=1 << 20, bytes_accessed=1 << 16, transcendentals=0)


def attn_product_kernel(keep, sc, la, lb, ra, rb, small, *refs):
    out = refs[-1] if keep else refs[-1].at[0]
    quarter, d = la.shape[3], ra.shape[2]
    for left, right, at in ((la, ra, 0), (lb, rb, quarter)):
        value = dot(left[0, 0], right[0], ((0,), (0,)))
        if keep:
            value = value + refs[0][0, at : at + quarter, :d].astype(f32)
        out[at : at + quarter, :d] = value.astype(bf16)
    value = small[0]
    if keep:
        value = add(value, refs[0][0, :, d:])
    out[:, d:] = value
    if keep:
        keep_parts(sc, out, refs[1:5])


def attn_products(offs, left, both, small, got=None):
    keep = got is not None
    slots, _, length, quarter = left.shape
    d = both.shape[2]
    width = d + small.shape[2]
    half = 2 * quarter

    def which(sc):
        return sc[17] if keep else 1 - sc[17]

    block = pl.BlockSpec((1, half, width), lambda i, sc: (i, 0, 0))
    specs = [
        pl.BlockSpec((1, 1, length, quarter), lambda i, sc: (i, 2 * which(sc), 0, 0)),
        pl.BlockSpec((1, 1, length, quarter), lambda i, sc: (i, 2 * which(sc) + 1, 0, 0)),
        pl.BlockSpec((1, length, d), lambda i, sc: (0, 0, 0)),
        pl.BlockSpec((1, length, d), lambda i, sc: (which(sc), 0, 0)),
        pl.BlockSpec((1, half, small.shape[2]), lambda i, sc: (i, which(sc), 0)),
    ]
    args = [left, left, both, both, small]
    out_specs, out_shape = block, jax.ShapeDtypeStruct((slots, half, width), bf16)
    scratch = []
    if keep:
        specs.append(block)
        args.append(got)
        out_specs, out_shape = parts_of(slots, half, width)
        scratch = [pltpu.VMEM((half, width), bf16)]
    return pl.pallas_call(
        functools.partial(attn_product_kernel, keep),
        grid_spec=pltpu.PrefetchScalarGridSpec(
            num_scalar_prefetch=1,
            grid=(slots,),
            in_specs=specs,
            out_specs=out_specs,
            scratch_shapes=scratch,
        ),
        out_shape=out_shape,
        compiler_params=params(48),
        cost_estimate=cheap,
        name="attn_keep" if keep else "attn_send",
    )(offs, *args)


def add(a, b):
    return (a.astype(f32) + b.astype(f32)).astype(bf16)


def second_kernel(sc, ka, ra, kb, rb, *refs):
    send_a, keep_a, send_b, keep_b = refs[-4:]
    x, y = sc[18], sc[19]
    send_a[0] = add(ka[0, 1 - y], ra[0, 1 - y])
    keep_a[0] = add(ka[0, y], ra[0, y])
    send_b[0] = add(kb[0, 1 - x], rb[0, 1 - x])
    keep_b[0] = add(kb[0, x], rb[0, x])


def second_sums(offs, *arrays, after=()):
    slots, _, half, width = arrays[0].shape
    into = pl.BlockSpec((1, 2, half, width), lambda i, sc: (i, 0, 0, 0))
    out = pl.BlockSpec((1, half, width), lambda i, sc: (i, 0, 0))
    return pl.pallas_call(
        second_kernel,
        grid_spec=pltpu.PrefetchScalarGridSpec(
            num_scalar_prefetch=1,
            grid=(slots,),
            in_specs=[into] * 4 + [ANY] * len(after),
            out_specs=[out] * 4,
        ),
        out_shape=[jax.ShapeDtypeStruct((slots, half, width), bf16)] * 4,
        compiler_params=params(48),
        cost_estimate=cheap,
        name="second_sums",
    )(offs, *arrays, *after)


def third_kernel(ka, ra, kb, rb, *refs):
    half = ka.shape[1]
    for k, out in enumerate(refs[-ka.shape[0] :]):
        out[:half, :] = add(ka[k], ra[k])
        out[half:, :] = add(kb[k], rb[k])


def third_sums(*arrays, after=()):
    slots, half, width = arrays[0].shape
    shape = (2 * half, width)
    return pl.pallas_call(
        third_kernel,
        grid=(1,),
        in_specs=[whole(arrays[0].shape)] * 4 + [ANY] * len(after),
        out_specs=[whole(shape)] * slots,
        out_shape=[jax.ShapeDtypeStruct(shape, bf16)] * slots,
        compiler_params=params(48),
        cost_estimate=cheap,
        name="third_sums",
    )(*arrays, *after)


def last_kernel(*refs):
    t = [ref[...].astype(f32) for ref in refs[:4]]
    refs[-1][...] = ((t[0] + t[2]) + (t[1] + t[3])).astype(refs[-1].dtype)


def last_sum(arrays, dtype, after=()):
    shape = arrays[0].shape
    return pl.pallas_call(
        last_kernel,
        grid=(1,),
        in_specs=[whole(shape)] * 4 + [ANY] * len(after),
        out_specs=whole(shape),
        out_shape=jax.ShapeDtypeStruct(shape, dtype),
        compiler_params=params(48),
        cost_estimate=cheap,
        name="last_sum",
    )(*arrays, *after)


def stack_kernel(a, xa, b, yb, *refs):
    sa, sb = refs[-2:]
    sa[0], sa[1], sb[0], sb[1] = a[...], xa[...], b[...], yb[...]


def stack_pairs(a, xa, b, yb, after):
    out = (2,) + a.shape
    return pl.pallas_call(
        stack_kernel,
        grid=(1,),
        in_specs=[whole(a.shape)] * 4 + [ANY] * len(after),
        out_specs=[whole(out)] * 2,
        out_shape=[jax.ShapeDtypeStruct(out, bf16)] * 2,
        compiler_params=params(48),
        cost_estimate=cheap,
        name="stack_pairs",
    )(a, xa, b, yb, *after)


class Reduce:
    def __init__(self, place, offs, kept):
        self.place, self.offs, self.kept = place, offs, kept

    def first(self, after=()):
        send_a, keep_a, send_b, keep_b = self.kept
        ra, rb = self.place.swap(send_a, XBIT), self.place.swap(send_b, YBIT)
        self.kept = second_sums(self.offs, keep_a, ra, keep_b, rb, after=after)

    def second(self, after=()):
        send_a, keep_a, send_b, keep_b = self.kept
        ra, rb = self.place.swap(send_a, YBIT), self.place.swap(send_b, XBIT)
        self.kept = third_sums(keep_a, ra, keep_b, rb, after=after)

    def third(self, after=()):
        p = self.place
        t = [self.kept[0]] + [p.shift(self.kept[k], -k) for k in range(1, p.n_mp)]
        if p.n_out > 1:
            return lax.psum(last_sum(t, f32, after), "out").astype(bf16)
        return last_sum(t, bf16, after)


def gathered(v):
    rows, width = v.shape
    out = lax.all_gather(v, group, tiled=False).reshape(2, 2, 2, rows, width)
    return out.transpose(2, 0, 1, 3, 4).reshape(8 * rows, width).astype(f32)


def unpack_kernel(offs, *refs):
    arrays, outs, small, full = refs[:8], refs[8:-2], refs[-2], refs[-1]
    for at in range(16):
        value = arrays[at // 2][at % 2]
        rows = pl.ds(pl.multiple_of(offs[at], 16), value.shape[0])
        full[rows, :] = value.astype(f32)
    rows, d = outs[0].shape
    for i, out in enumerate(outs):
        out[...] = full[i * rows : (i + 1) * rows, :d]
    small[...] = full[:, d:]


def unpack(offs, arrays, count, small):
    half, width = arrays[0].shape[1:]
    rows, d = 16 * half, width - small
    shapes = [(rows // count, d)] * count + [(rows, small)]
    return pl.pallas_call(
        unpack_kernel,
        grid_spec=pltpu.PrefetchScalarGridSpec(
            num_scalar_prefetch=1,
            grid=(1,),
            in_specs=[whole(v.shape) for v in arrays],
            out_specs=[whole(s) for s in shapes],
            scratch_shapes=[pltpu.VMEM((rows, width), f32)],
        ),
        out_shape=[jax.ShapeDtypeStruct(s, f32) for s in shapes],
        compiler_params=params(24),
        cost_estimate=cheap,
        name="unpack",
    )(offs, *arrays)


def spread_rows(place, v, length):
    n = place.n_mp
    right = left = v
    slots = [v] + [None] * (n - 1)
    for k in range(1, n):
        right = lax.ppermute(right, "mp", [(i, i + 1) for i in range(n - 1)])
        left = lax.ppermute(left, "mp", [(i + 1, i) for i in range(n - 1)])
        for at, value in ((k, right), (n - k, left)):
            slots[at] = value if slots[at] is None else slots[at] + value
    out = jnp.zeros((n, length) + v.shape[1:], f32)
    rest = jnp.zeros((n, v.shape[0] - length) + v.shape[1:], v.dtype)
    for k in range(n):
        at = (place.z - k) % n
        out = lax.dynamic_update_index_in_dim(out, slots[k][:length].astype(f32), at, 0)
        rest = lax.dynamic_update_index_in_dim(rest, slots[k][length:], at, 0)
    return out, rest


def local(
    tokens, segment_ids, pad_mask, top_index, query_emb, score_cot, gain_attn, w_query, w_key,
    w_value, w_out, rel_table, gain_ffn, w_gate, w_up, w_down, gain_final, w_proj,
):
    place = Place()
    slots = place.n_mp
    rows, length = segment_ids.shape
    d = tokens.shape[1]
    heads = rel_table.shape[1]
    size = w_query.shape[1] // heads
    wide = heads * size
    hot = jnp.asarray(bucket_hot(rel_table.shape[0], length), bf16)
    segs, pads = segment_ids.astype(f32), pad_mask.astype(f32)
    seg_cols, pad_cols = segs.T, pads.T
    gain_a, gain_f, gain_l = (
        g.astype(f32).reshape(1, d) for g in (gain_attn, gain_ffn, gain_final)
    )
    offs = place.offsets(d // 8)

    buckets = rel_table.shape[0]
    table = jnp.zeros((64, d), bf16).at[:heads, :buckets].set(rel_table.T)
    w_qkv = jnp.concatenate([w_query.T, w_key.T, w_value.T, table])
    w_out_t = w_out.T
    eighth = d // 8

    def piece(*arrays):
        parts = []
        for v in arrays:
            rows = v.shape[0] // 8
            parts.append(lax.dynamic_slice_in_dim(v, place.p * rows, rows, 0))
        return jnp.concatenate(parts, axis=1) if len(parts) > 1 else parts[0]

    def all_pieces(v):
        out = lax.all_gather(piece(v), group + ("mp",))
        return out.reshape((2, 2, 2, slots) + out.shape[1:])

    common = (offs, tokens, segs, pads, seg_cols, gain_a)
    piece1 = piece(w_gate, w_up, w_out_t)
    z1 = [place.shift(piece1, k) for k in range(1, slots)]
    all_down = all_pieces(w_down)
    all_qkv = all_pieces(w_qkv)
    attended = attend(1, *common, w_qkv, hot, heads, size)
    mixed = [attended[slots - 1]] + [place.shift(attended[k - 1], k) for k in range(1, slots)]
    s1 = place.first_round(*split(z1, (attended,)), mixed[1:])
    first = place.second_round(*s1)
    own = (w_gate, w_up, w_out_t)
    hid, normed_ffn, act, dact, inner = ffn_in(
        offs, tokens, gain_f, mixed, own, first, length
    )
    score, nfin, ge, gain_fin, gain_mid, gft, gg, gu, gha, gat, gm = middle(
        offs, hid, inner, act, dact, gain_l, gain_f, w_proj, pad_cols, query_emb, score_cot,
        top_index, own, first, all_down,
    )

    down_sides = ([inner, nfin], [(gft, 0), (ge, 1)])
    gu_sides = ([normed_ffn], [(gg, 0), (gu, 0)])
    down_got = place.swap(products(offs, *down_sides, slots), CORE)
    gu_got = place.swap(products(offs, *gu_sides, slots), CORE)
    down = Reduce(place, offs, products(offs, *down_sides, slots, down_got))
    gate_up = Reduce(place, offs, products(offs, *gu_sides, slots, gu_got))
    kept_gu = (gate_up.kept[0], gate_up.kept[2])
    down.first(kept_gu)

    finish = [gha, gat, gain_fin, gain_mid, score]

    def back(slot, acc, left, after):
        return attend_back(
            slot, common + (hot,), gm, mixed[slot], acc, left, finish, all_qkv, heads, size, after
        )

    left, table0, acc = back(0, None, None, kept_gu + (down.kept[0], down.kept[2]))
    down.second((table0,))
    left, table1, acc = back(1, acc, left, tuple(down.kept[1:]))
    down = down.third((table1,))
    gate_up.first((table1,))
    left, table2, acc = back(2, acc, left, (gate_up.kept[0], gate_up.kept[2]))
    gate_up.second((table2,))
    finish += [table0, table1, table2]
    left, _, dx, both, small = back(3, acc, left, tuple(gate_up.kept[1:]))
    gate_up = gate_up.third((both,))
    attn_got = place.swap(attn_products(offs, left, both, small), CORE)
    attn = Reduce(place, offs, attn_products(offs, left, both, small, attn_got))
    attn.first()
    attn.second()
    attn = place.second_round(*place.first_round(*halves(attn.third(), 0)))
    grad_q, grad_k, grad_v, grad_out, small = unpack(offs, attn, 4, small.shape[2])
    grad_down = gathered(down)
    grad_gu = gathered(gate_up)
    hidden = w_gate.shape[1]

    input_grad, packed = spread_rows(place, dx, length)
    input_grad = input_grad.reshape(rows * length, d)
    n, m = score.shape
    packed = packed.astype(f32).reshape(slots, 16, d // 128, 128)[:, :, : 2 * (n // 16), :m]
    packed = packed[:, :, 0::2] + packed[:, :, 1::2]
    scores = packed.transpose(0, 2, 1, 3).reshape(slots, n, m)
    return (
        scores,
        input_grad,
        small[:, 0],
        grad_q.T,
        grad_k.T,
        grad_v.T,
        grad_out,
        small[:buckets, 64 : 64 + heads],
        small[:, 2],
        grad_gu[:, :hidden],
        grad_gu[:, hidden:],
        grad_down[:, :d],
        small[:, 1],
        grad_down[:, d:],
    )


def solution(mesh):
    n_dp, n_mp = mesh.shape["dp"], mesh.shape["mp"]
    mesh = Mesh(mesh.devices.reshape(n_dp // 8, 2, 2, 2, n_mp), dp + ("mp",))
    return jax.shard_map(
        local,
        mesh=mesh,
        in_specs=(
            P(dp, None),
            P(dp, None),
            P(dp, None),
            P(dp, None, None),
            P(dp, None, None),
            P(dp, None, None),
            P(),
            P(None, "mp"),
            P(None, "mp"),
            P(None, "mp"),
            P("mp", None),
            P(None, "mp"),
            P(),
            P(None, "mp"),
            P(None, "mp"),
            P("mp", None),
            P(),
            P(),
        ),
        out_specs=(
            P(dp, None, None),
            P(dp, None),
            P(),
            P(None, "mp"),
            P(None, "mp"),
            P(None, "mp"),
            P("mp", None),
            P(None, "mp"),
            P(),
            P(None, "mp"),
            P(None, "mp"),
            P("mp", None),
            P(),
            P(),
        ),
        check_vma=False,
    )
```

```python
import functools
import math

import jax
import jax.numpy as jnp
import numpy as np
from jax import lax
from jax.experimental import pallas as pl
from jax.experimental.pallas import tpu as pltpu
from jax.sharding import Mesh
from jax.sharding import PartitionSpec as P

f32 = jnp.float32
bf16 = jnp.bfloat16
eps = 1e-06
masked_logit = -1e30
gelu_c = math.sqrt(2.0 / math.pi)
CORE, XBIT, YBIT = "core", "x", "y"
group = ("y", "x", "core")
dp = ("out",) + group
span = 1024
tile = 128


def bucket_hot(buckets, length):
    column = np.arange(span)
    base = length - tile
    offset = np.where(column < base + length, column - base, column - span - base)
    distance = np.abs(offset)
    far = 8 + sum((distance >= t).astype(np.int32) for t in (12, 16, 23, 32, 46, 64, 91))
    bucket = np.where(distance < 8, distance, far) + 16 * (offset > 0)
    hot = (bucket[None, :] == np.arange(tile)[:, None]) & (np.arange(tile)[:, None] < buckets)
    return hot.astype(np.float32)


def dot(a, b, dims=((1,), (0,))):
    return lax.dot_general(a, b, (dims, ((), ())), preferred_element_type=f32)


def rms_scale(v):
    return lax.rsqrt(jnp.mean(v * v, axis=-1, keepdims=True) + eps)


def rms_back(v, gain, grad):
    s = rms_scale(v)
    w = grad * gain
    value = s * w - v * ((s * s * s) * jnp.mean(w * v, axis=-1, keepdims=True))
    return value, jnp.sum(grad * v * s, axis=0, keepdims=True)


def whole(shape):
    return pl.BlockSpec(shape, lambda *_: (0,) * len(shape))


ANY = pl.BlockSpec(memory_space=pl.ANY)
token_shape = (8, 128)


def launch(
    kernel, name, args, in_specs, out_specs, out_shape, grid=(1,), offs=None, scratch=(),
    cost=None, after=(), alias=None, n_alias=1, mib=16,
):
    first = 0 if offs is None else 1
    n_in, n_out, n_after = first + len(args), len(out_shape), len(after)

    def body(*refs):
        ins, rest = refs[:n_in], refs[n_in + n_after :]
        outs, token, own = rest[:n_out], rest[n_out], rest[n_out + 1 :]
        token[...] = jnp.zeros(token_shape, f32)
        kernel(*ins, *outs, *own)

    specs = dict(
        grid=grid,
        in_specs=list(in_specs) + [ANY] * n_after,
        out_specs=list(out_specs) + [whole(token_shape)],
        scratch_shapes=list(scratch),
    )
    if offs is None:
        specs = dict(specs)
        scalars = []
    else:
        specs = dict(grid_spec=pltpu.PrefetchScalarGridSpec(num_scalar_prefetch=1, **specs))
        scalars = [offs]
    *outs, token = pl.pallas_call(
        body,
        out_shape=list(out_shape) + [jax.ShapeDtypeStruct(token_shape, f32)],
        input_output_aliases=(
            {} if alias is None else {alias + first + i: i for i in range(n_alias)}
        ),
        compiler_params=pltpu.CompilerParams(
            vmem_limit_bytes=mib << 20, dimension_semantics=("arbitrary",)
        ),
        cost_estimate=cost or cheap,
        name=name,
        **specs,
    )(*scalars, *args, *after)
    return outs, token


cheap = pl.CostEstimate(flops=1 << 20, bytes_accessed=1 << 16, transcendentals=0)


def cost(flops, mib, transcendentals=0):
    return pl.CostEstimate(
        flops=flops, bytes_accessed=mib << 20, transcendentals=transcendentals
    )


def like(dtype, *shapes):
    return [jax.ShapeDtypeStruct(shape, dtype) for shape in shapes]


class Place:
    def __init__(self):
        self.n_out, self.n_mp = lax.axis_size("out"), lax.axis_size("mp")
        self.c, self.x, self.y = (lax.axis_index(name) for name in ("core", "x", "y"))
        self.z = lax.axis_index("mp")
        self.p = self.c * 4 + self.y * 2 + self.x

    def swap(self, v, name):
        return lax.ppermute(v, name, [(0, 1), (1, 0)])

    def shift(self, v, k):
        n = self.n_mp
        return lax.ppermute(v, "mp", [(i, (i + k) % n) for i in range(n)])

    def offsets(self, rows):
        half = rows // 2
        out = []
        for flip in (0, 4):
            p = self.p ^ flip
            for other, extra in (
                (0, 0), (1, 0), (0, half), (2, half), (2, 0), (3, 0), (1, half), (3, half),
            ):
                out.append((p ^ other) * rows + extra)
        return jnp.stack(out + [self.z, self.c, self.x, self.y]).astype(jnp.int32)

    def both_ways(self, right, left):
        n = self.n_mp
        right = lax.ppermute(right, "mp", [(i, i + 1) for i in range(n - 1)])
        return right, lax.ppermute(left, "mp", [(i + 1, i) for i in range(n - 1)])

    def first_round(self, a, b, after=()):
        return stack_pairs(a, self.swap(a, XBIT), b, self.swap(b, YBIT), after)

    def second_round(self, sa, sb, after=()):
        ya, xb = self.swap(sa, YBIT), self.swap(sb, XBIT)
        if after:
            ya, xb = relay(ya, xb, after)
        near = [sa, sb, ya, xb]
        return near + [self.swap(t, CORE) for t in near]


def pick(v, axis, index):
    return lax.dynamic_index_in_dim(v, index, axis, keepdims=False)


def halves(v, axis):
    half = v.shape[axis] // 2
    return (
        lax.slice_in_dim(v, 0, half, axis=axis),
        lax.slice_in_dim(v, half, 2 * half, axis=axis),
    )


def chunk_copies(offs, own, arrays, dst, sems, first=0, slot=0):
    slots, rows, width = dst.shape
    half = rows // 16
    skip = 0 if slot else 1
    pairs = [
        (ref, dst.at[0, :, pl.ds(column, ref.shape[1])]) for ref, column in own
    ]
    for at in range(16):
        src = arrays[at // 2].at[at % 2, pl.ds(slot + skip - 1, slots - skip)]
        if src.shape[2] != width:
            src = src.at[:, :, pl.ds(first, width)]
        start = pl.multiple_of(offs[at], 16)
        pairs.append((src, dst.at[pl.ds(skip, slots - skip), pl.ds(start, half), :]))
    return [pltpu.make_async_copy(s, d, sems.at[i]) for i, (s, d) in enumerate(pairs)]


copies_per_chunk = 20


def gathered_copies(gathered, dst, sems, shard=None):
    full = gathered.shape[4]
    out = []
    for at, (c, y, x) in enumerate(np.ndindex(2, 2, 2)):
        rows = pl.ds(at * full, full)
        if shard is None:
            out.append((gathered.at[y, x, c], dst.at[:, rows, :]))
        else:
            out.append((gathered.at[y, x, c, shard], dst.at[rows, :]))
    return [pltpu.make_async_copy(s, d, sems.at[i]) for i, (s, d) in enumerate(out)]


def split_kernel(sc, v_ref, a_ref, b_ref, *rest):
    half = a_ref.shape[1]
    n = v_ref.shape[0]
    for ref in rest:
        ref[...] = v_ref[:, 2 * half :, :]
    for k in range(1, n):
        at = lax.rem(sc[16] + n - k, n)
        a_ref[k - 1] = v_ref[at, :half, :]
        b_ref[k - 1] = v_ref[at, half : 2 * half, :]


def split(offs, v, rows, after=()):
    n, _, width = v.shape
    out = (n - 1, rows // 2, width)
    shapes = [out, out] + ([(n, v.shape[1] - rows, width)] if v.shape[1] > rows else [])
    return launch(
        split_kernel, "split", [v], [whole(v.shape)], [whole(shape) for shape in shapes],
        like(bf16, *shapes), offs=offs, after=after,
    )


def relay_kernel(a, b, c, d):
    c[...] = a[...]
    d[...] = b[...]


def relay(a, b, after):
    return launch(
        relay_kernel, "relay", [a, b], [whole(a.shape)] * 2, [whole(a.shape)] * 2,
        like(a.dtype, a.shape, a.shape), after=after,
    )[0]


def collect_kernel(step, n, sc, right, left, own, *refs):
    out, rest, *on = refs
    length = out.shape[1]
    side = pl.program_id(0)
    z = sc[16]

    @pl.when((side == 0) & (z >= step))
    def _():
        out[0] = right[:length, :].astype(f32)
        rest[0] = right[length:, :]

    @pl.when((side == 1) & (z + step < n))
    def _():
        out[0] = left[:length, :].astype(f32)
        rest[0] = left[length:, :]

    @pl.when(((side == 0) & (z < step)) | ((side == 1) & (z + step >= n)))
    def _():
        out[0] = own[:length, :].astype(f32)
        rest[0] = own[length:, :]

    @pl.when(side == 0)
    def _():
        for new, old in zip(on, (right, left)):
            new[...] = old[...]


def collect(step, n, offs, right, left, own, so_far, after):
    rows, d = own.shape
    length = rows // tile * tile

    def index(i, sc):
        z = sc[16]
        near, far = jnp.where(z >= step, z - step, z), jnp.where(z + step < n, z + step, z)
        return (jnp.where(i == 0, near, far), 0, 0)

    goes_on = step < n - 1
    kept = list(so_far or ())
    shapes = [(n, length, d), (n, rows - length, d)]
    out_shape = like(f32, shapes[0]) + like(bf16, shapes[1])
    out_specs = [pl.BlockSpec((1,) + shape[1:], index) for shape in shapes]
    if goes_on:
        out_shape += like(bf16, own.shape, own.shape)
        out_specs += [whole(own.shape)] * 2

    def kernel(sc, right, left, own, *refs):
        collect_kernel(step, n, sc, right, left, own, *refs[len(kept) :])

    return launch(
        kernel, f"collect{step}", [right, left, own, *kept],
        [whole(own.shape)] * 3 + [ANY] * len(kept), out_specs, out_shape, grid=(2,), offs=offs,
        after=after, alias=3 if kept else None, n_alias=2,
    )


def skew(base):
    t = jnp.broadcast_to(base, (8, span))
    row = lax.broadcasted_iota(jnp.int32, (8, span), 0)
    for step in (1, 2, 4):
        t = jnp.where((row & step) != 0, pltpu.roll(t, step, 1), t)
    while t.shape[0] < tile:
        t = jnp.concatenate([t, pltpu.roll(t, t.shape[0], 1)], axis=0)
    return t


def unskew(t):
    while t.shape[0] > 8:
        n = t.shape[0] // 2
        t = t[:n] + pltpu.roll(t[n:], span - n, 1)
    row = lax.broadcasted_iota(jnp.int32, (8, span), 0)
    for step in (1, 2, 4):
        t = jnp.where((row & step) != 0, pltpu.roll(t, span - step, 1), t)
    return jnp.sum(t, axis=0, keepdims=True)


def fill_mask(mask, segs, pads, seg_cols, row):
    length = mask.shape[0]
    rows = segs.shape[0]
    chosen = lax.broadcasted_iota(jnp.int32, (rows, length), 0) == row
    seg_k = jnp.sum(jnp.where(chosen, segs, 0.0), axis=0, keepdims=True)
    pad_k = jnp.sum(jnp.where(chosen, pads, 0.0), axis=0, keepdims=True)
    code = jnp.where(pad_k == 1.0, seg_k, -1.0)
    lane = lax.broadcasted_iota(jnp.int32, seg_cols.shape, 1)
    seg_q = jnp.sum(jnp.where(lane == row, seg_cols, 0.0), axis=1, keepdims=True)
    q = lax.broadcasted_iota(jnp.int32, (tile, length), 0)
    k = lax.broadcasted_iota(jnp.int32, (tile, length), 1)
    for a in range(length // tile):
        own = seg_q[a * tile : (a + 1) * tile]
        ok = (own == code) | (q + a * tile == k)
        mask[a * tile : (a + 1) * tile, :] = jnp.where(ok, 0.0, masked_logit)


def fill_bias(bias, table, hot, heads):
    base = dot(table, hot[0 : table.shape[1], :])
    for h in range(heads):
        bias[h] = skew(base[h : h + 1, :])


def normalize(x_ref, gain, normed):
    for a in range(x_ref.shape[0] // tile):
        rows = slice(a * tile, (a + 1) * tile)
        v = x_ref[rows, :].astype(f32)
        normed[rows, :] = (v * rms_scale(v) * gain).astype(bf16)


chunk = 32


def head_groups(heads, size):
    per = tile // size
    out = []
    for first in range(0, heads, per):
        members = range(first, min(heads, first + per))
        lanes = slice(first * size, (members[-1] + 1) * size)
        out.append((lanes, [(h, (h - first) * size) for h in members]))
    return out


def only(v, lane, size):
    if v.shape[1] == size:
        return v
    at = lax.broadcasted_iota(jnp.int32, v.shape, 1)
    return jnp.where((at >= lane) & (at < lane + size), v, jnp.zeros_like(v))


def merge(parts, size):
    out = parts[0]
    at = lax.broadcasted_iota(jnp.int32, out.shape, 1)
    for i, part in enumerate(parts[1:]):
        out = jnp.where(at >= (i + 1) * size, part, out)
    return out


def project_heads(normed_ref, w, parts):
    rows = parts[0].shape[1]
    for i, part in enumerate(parts):
        part[...] = dot(
            normed_ref[...], w[i * rows : (i + 1) * rows, :], ((1,), (1,))
        ).astype(bf16)


def softmax_chunks(length):
    for r in range(0, length, chunk):
        at = length - tile - r // tile * tile
        yield slice(r, r + chunk), slice(r % tile, r % tile + chunk), slice(at, at + length)


def attend_kernel(
    first, heads, size, sc, x_ref, seg_ref, pad_ref, segc_ref, gain_ref, w_ref, hot_ref,
    out_ref, normed, query, keys, values, mask, bias, logits, probs, inverse,
):
    length = x_ref.shape[0]
    wide = heads * size
    buckets = 32
    row = lax.rem(sc[16] + first + pl.program_id(0), seg_ref.shape[0])
    normalize(x_ref, gain_ref[...], normed)
    project_heads(normed, w_ref, (query, keys, values))
    fill_mask(mask, seg_ref[...], pad_ref[...], segc_ref[...], row)

    @pl.when(pl.program_id(0) == 0)
    def _():
        fill_bias(bias, w_ref[3 * wide : 3 * wide + 16, :tile][:, :buckets], hot_ref, heads)

    for lanes, members in head_groups(heads, size):
        parts = []
        for i, (h, lane) in enumerate(members):
            logits[i % 2] = dot(only(query[:, lanes], lane, size), keys[:, lanes], ((1,), (1,)))
            for rows, inner, at in softmax_chunks(length):
                v = logits[i % 2, rows, :] + bias[h, inner, at] + mask[rows, :]
                e = jnp.exp(v - jnp.max(v, axis=1, keepdims=True))
                total = jnp.sum(e, axis=1, keepdims=True)
                inverse[rows, :] = jnp.broadcast_to(1.0 / total, (chunk, tile))
                probs[i % 2, rows, :] = e.astype(bf16)
            part = dot(probs[i % 2], values[:, lanes])
            parts.append(part * inverse[:, : part.shape[1]])
        out_ref[0, :length, lanes] = merge(parts, size).astype(bf16)
    out_ref[0, length:, :] = w_ref[3 * wide : 3 * wide + 16, :wide]


def attend(first, offs, tokens, segs, pads, seg_cols, gain, w_qkv, hot, heads, size, after=()):
    rows, length = segs.shape
    d = tokens.shape[1]
    wide = heads * size
    args = [tokens, segs, pads, seg_cols, gain, w_qkv, hot]
    specs = [pl.BlockSpec((length, d), lambda i, sc: (lax.rem(sc[16] + first + i, rows), 0))]
    return launch(
        functools.partial(attend_kernel, first, heads, size), "attend", args,
        specs + [whole(v.shape) for v in args[1:]],
        [pl.BlockSpec((1, length + 16, wide), lambda i, sc: (i, 0, 0))],
        like(bf16, (rows, length + 16, wide)),
        grid=(rows,), offs=offs,
        scratch=[
            pltpu.VMEM((length, d), bf16),
            pltpu.VMEM((length, wide), bf16),
            pltpu.VMEM((length, wide), bf16),
            pltpu.VMEM((length, wide), bf16),
            pltpu.VMEM((length, length), f32),
            pltpu.VMEM((heads, tile, span), f32),
            pltpu.VMEM((2, length, length), f32),
            pltpu.VMEM((2, length, length), bf16),
            pltpu.VMEM((length, tile), f32),
        ],
        cost=cost(
            rows * (6 * length * d * wide + 4 * wide * length * length), 4,
            rows * heads * length * length,
        ),
        after=after,
    )


def high_low(v):
    high = v.astype(bf16)
    return high, (v - high.astype(f32)).astype(bf16)


def attend_back_slot(
    heads, size, mixed_ref, gm_ref, hot_ref, w, left_ref, table_out, acc,
    normed, query, keys, values, mask, bias, logits, gprobs, probs, dlog, skewed, diag,
):
    length = normed.shape[0]
    wide = heads * size
    fill_bias(bias, mixed_ref[length:, :tile][:, :32], hot_ref, heads)
    project_heads(normed, w, (query, keys, values))
    for lanes, members in head_groups(heads, size):
        q, k, v = query[:, lanes], keys[:, lanes], values[:, lanes]
        grad = gm_ref[:, lanes]
        results = []
        for h, lane in members:
            logits[...] = dot(only(q, lane, size), k, ((1,), (1,)))
            gprobs[...] = dot(only(grad, lane, size), v, ((1,), (1,)))
            skewed[...] = jnp.zeros_like(skewed)
            for rows, inner, at in softmax_chunks(length):
                t = logits[rows, :] + bias[h, inner, at] + mask[rows, :]
                e = jnp.exp(t - jnp.max(t, axis=1, keepdims=True))
                p = e * (1.0 / jnp.sum(e, axis=1, keepdims=True))
                probs[rows, :] = p.astype(bf16)
                gp = gprobs[rows, :]
                gl = p * (gp - jnp.sum(gp * p, axis=1, keepdims=True))
                dlog[rows, :] = gl.astype(bf16)
                skewed[inner, at] += gl
            diag[h : h + 1, :] = unskew(skewed[...])
            results.append(
                (
                    dot(dlog[...], k),
                    dot(dlog[...], q, ((0,), (0,))),
                    dot(probs[...], grad, ((0,), (0,))),
                )
            )
        for part in range(3):
            merged = merge([r[part] for r in results], size)
            left_ref[part, :, lanes] = merged.astype(bf16)
    left_ref[3] = mixed_ref[:length, :]
    high, low = high_low(diag[...])
    table = dot(high, hot_ref[...], ((1,), (1,))) + dot(low, hot_ref[...], ((1,), (1,)))
    table_out[...] = table
    value = sum(
        dot(left_ref[part], w[part * wide : (part + 1) * wide, :]) for part in range(3)
    )
    acc[...] += value


def attend_back_kernel(
    first, count, last, heads, size, sc, x_ref, seg_ref, pad_ref, segc_ref, gain_ref, hot_ref,
    gm_ref, *refs,
):
    mixed_refs, refs = refs[:count], list(refs[count:])
    acc_in = refs.pop(0) if first else None
    if last:
        gha_ref, gat_ref, fin_ref, mid_ref, score_ref = refs[:5]
        refs = refs[5:]
        tables = [refs.pop(0)] if first else []
    w_ref = refs[0]
    refs = refs[1 + (1 if first else 0) :]
    left_ref, table_out = refs[:2]
    if last:
        dx_ref, both_ref, small_ref, acc = refs[2:6]
        refs = refs[6:]
    else:
        acc, refs = refs[2], refs[3:]
    (
        w, sems, normed, query, keys, values, mask, bias, logits, gprobs, probs, dlog, skewed, diag,
    ) = refs
    length, d = x_ref.shape
    wide = heads * size
    row = sc[16]
    gain = gain_ref[...]
    blocks = length // tile
    copies = [
        gathered_copies(w_ref, w.at[i], sems.at[i], lax.rem(row + 4 - first - i, 4))
        for i in range(count)
    ]
    for copy in sum(copies, []):
        copy.start()
    normalize(x_ref, gain, normed)
    fill_mask(mask, seg_ref[...], pad_ref[...], segc_ref[...], row)
    diag[...] = jnp.zeros_like(diag)
    if acc_in is None:
        acc[...] = jnp.zeros_like(acc)
    else:
        acc[...] = acc_in[...]
    for i in range(count):
        for copy in copies[i]:
            copy.wait()
        attend_back_slot(
            heads, size, mixed_refs[i], gm_ref.at[i], hot_ref, w.at[i], left_ref.at[i],
            table_out.at[8 * i : 8 * i + 8], acc,
            normed, query, keys, values, mask, bias, logits, gprobs, probs, dlog, skewed, diag,
        )
    if not last:
        return
    total = jnp.zeros((1, d), f32)
    for a in range(blocks):
        rows = slice(a * tile, (a + 1) * tile)
        back, part = rms_back(x_ref[rows, :].astype(f32), gain, acc[rows, :])
        dx_ref[rows, :] = (gha_ref[rows, :] + back).astype(bf16)
        total = total + part
    both_ref[0] = normed[...]
    both_ref[1] = gat_ref[...]
    dx_ref[length:, :] = jnp.zeros((dx_ref.shape[0] - length, d), bf16)
    n = score_ref.shape[0] // 16
    cols = score_ref.shape[1]
    high, low = high_low(score_ref[...])
    for i in range(n):
        rows = slice(16 * i, 16 * i + 16)
        dx_ref[length : length + 16, 2 * i * tile : 2 * i * tile + cols] = high[rows]
        dx_ref[length : length + 16, (2 * i + 1) * tile : (2 * i + 1) * tile + cols] = low[rows]
    line = lax.broadcasted_iota(jnp.int32, (8, d), 0)
    gains = jnp.where(
        line == 0, total, jnp.where(line == 1, fin_ref[...], jnp.where(line == 2, mid_ref[...], 0.0))
    )
    line = lax.broadcasted_iota(jnp.int32, (8, tile), 0)
    column = lax.broadcasted_iota(jnp.int32, (8, tile), 1)

    def turned(value, at):
        place = jnp.where(column == line + at, 1.0, 0.0).astype(bf16)
        high, low = high_low(value)
        return dot(high, place, ((0,), (0,))) + dot(low, place, ((0,), (0,)))

    gains = turned(gains, 0)
    tables = [t[8 * i : 8 * i + 8] for t in tables + [table_out] for i in range(t.shape[0] // 8)]
    for k, value in enumerate(tables):
        small_ref[k] = gains.astype(bf16)
        small_ref[k, 0:tile, :] = (gains[0:tile] + turned(value, tile // 2)).astype(bf16)


def attend_back(
    first, count, common, grad_mixed, mixed, acc, left, finish, weights, heads, size, after=()
):
    offs, *shared = common
    rows, length = shared[1].shape
    d = shared[0].shape[1]
    slots = grad_mixed.shape[0]
    wide = heads * size
    last = first + count == slots
    mixed = mixed[first : first + count]
    args = [*shared, grad_mixed, *mixed]
    specs = [pl.BlockSpec((length, d), lambda i, sc: (sc[16], 0))]
    specs += [whole(v.shape) for v in shared[1:]]
    specs.append(pl.BlockSpec((count, length, wide), lambda i, sc: (first // count, 0, 0)))
    specs += [whole(m.shape) for m in mixed]
    if first:
        args.append(acc)
        specs.append(whole(acc.shape))
    if last:
        args += finish
        specs += [whole(v.shape) for v in finish]
    args += [weights] + ([left] if first else [])
    specs += [ANY] * (2 if first else 1)
    out_specs = [
        pl.BlockSpec((count, 4, length, wide), lambda i, sc: (first // count, 0, 0, 0)),
        whole((8 * count, tile)),
    ]
    out_shape = like(bf16, (slots, 4, length, wide)) + like(f32, (8 * count, tile))
    scratch = []
    if last:
        shapes = ((length + 16, d), (2, length, d), (slots, d, tile))
        out_specs += [whole(shape) for shape in shapes]
        out_shape += like(bf16, *shapes)
        scratch = [pltpu.VMEM((length, d), f32)]
    else:
        out_specs.append(whole((length, d)))
        out_shape += like(f32, (length, d))
    return launch(
        functools.partial(attend_back_kernel, first, count, last, heads, size),
        f"attend_back{first}",
        args, specs, out_specs, out_shape, offs=offs,
        scratch=scratch
        + [
            pltpu.VMEM((count, 8 * weights.shape[4], d), bf16),
            pltpu.SemaphoreType.DMA((count, 8)),
            pltpu.VMEM((length, d), bf16),
            pltpu.VMEM((length, wide), bf16),
            pltpu.VMEM((length, wide), bf16),
            pltpu.VMEM((length, wide), bf16),
            pltpu.VMEM((length, length), f32),
            pltpu.VMEM((heads, tile, span), f32),
            pltpu.VMEM((length, length), f32),
            pltpu.VMEM((length, length), f32),
            pltpu.VMEM((length, length), bf16),
            pltpu.VMEM((length, length), bf16),
            pltpu.VMEM((tile, span), f32),
            pltpu.VMEM((8, span), f32),
        ],
        cost=cost(
            count * (12 * length * d * wide + 14 * wide * length * length), 16,
            count * heads * length * length,
        ),
        after=after, alias=len(args) - 1 if first else None, mib=32,
    )


def ffn_in_first_kernel(count, sc, x_ref, gain_ref, *refs):
    slots = 4
    mixed, own, arrays = refs[:slots], refs[slots : slots + 3], refs[slots + 3 : slots + 11]
    hid_ref, normed_ref, *outs = refs[slots + 11 : slots + 16]
    w, wo, sems, o_sems = refs[slots + 16 :]
    length, d = x_ref.shape
    hidden = outs[0].shape[2]
    copies = chunk_copies(sc, zip(own, (0, hidden)), arrays, w, sems)
    o_copies = chunk_copies(sc, [(own[2], 0)], arrays, wo, o_sems, 2 * hidden)

    @pl.when(pl.program_id(0) == 0)
    def _():
        for copy in o_copies + copies:
            copy.start()
        for copy in o_copies:
            copy.wait()
        gain = gain_ref[...]
        for a in range(length // tile):
            rows = slice(a * tile, (a + 1) * tile)
            h = x_ref[rows, :].astype(f32)
            for k in range(slots):
                h = h + dot(mixed[k][rows, :], wo[k], ((1,), (1,)))
            hid_ref[rows, :] = h
            normed_ref[rows, :] = (h * rms_scale(h) * gain).astype(bf16)
        for copy in copies:
            copy.wait()

    gate_up(normed_ref, w.at[pl.program_id(0)], *outs)


def ffn_in_rest_kernel(first, sc, normed_ref, *refs):
    arrays, outs, (w, sems) = refs[:8], refs[8:11], refs[11:]
    copies = chunk_copies(sc, (), arrays, w, sems, 0, first)

    @pl.when(pl.program_id(0) == 0)
    def _():
        for copy in copies:
            copy.start()
        for copy in copies:
            copy.wait()

    gate_up(normed_ref, w.at[pl.program_id(0)], *outs)


def gate_up(normed_ref, w, act_ref, dact_ref, inner_ref):
    hidden = act_ref.shape[2]
    for n in range(hidden // 256):
        cols = slice(n * 256, (n + 1) * 256)
        normed = normed_ref[...]
        gate = dot(normed, w[:, cols])
        up = dot(normed, w[:, hidden + n * 256 : hidden + (n + 1) * 256])
        t = jnp.tanh(gelu_c * (gate + 0.044715 * gate * gate * gate))
        half = 0.5 * (1.0 + t)
        act = gate * half
        slope = half + 0.5 * gate * (1.0 - t * t) * (
            gelu_c * (1.0 + 3 * 0.044715 * gate * gate)
        )
        act_ref[0, :, cols] = act.astype(bf16)
        dact_ref[0, :, cols] = (up * slope).astype(bf16)
        inner_ref[0, :, cols] = (act * up).astype(bf16)


def ffn_in_first(count, offs, tokens, gain, mixed, own, arrays, length, after=()):
    d = tokens.shape[1]
    slots = len(mixed)
    hidden = own[0].shape[1]
    wide = own[2].shape[1]
    per_slot = pl.BlockSpec((1, length, hidden), lambda i, sc: (i, 0, 0))
    three = (slots, length, hidden)
    specs = [pl.BlockSpec((length, d), lambda i, sc: (sc[16], 0)), whole(gain.shape)]
    return launch(
        functools.partial(ffn_in_first_kernel, count), "ffn_in_first",
        [tokens, gain, *mixed, *own, *arrays],
        specs + [whole(m.shape) for m in mixed] + [ANY] * 11,
        [whole((length, d)), whole((length, d))] + [per_slot] * 3,
        like(f32, (length, d)) + like(bf16, (length, d), three, three, three),
        grid=(count,), offs=offs,
        scratch=[
            pltpu.VMEM((count, d, 2 * hidden), bf16),
            pltpu.VMEM((slots, d, wide), bf16),
            pltpu.SemaphoreType.DMA((copies_per_chunk,)),
            pltpu.SemaphoreType.DMA((copies_per_chunk,)),
        ],
        cost=cost(2 * length * d * (d + 2 * count * hidden), 16, count * length * hidden),
        after=after, mib=24,
    )


def ffn_in_rest(count, offs, normed, so_far, arrays, after=()):
    length, d = normed.shape
    slots, _, hidden = so_far[0].shape
    first = slots - count
    per_slot = pl.BlockSpec((1, length, hidden), lambda i, sc: (i + first, 0, 0))

    def kernel(sc, normed_ref, *refs):
        ffn_in_rest_kernel(first, sc, normed_ref, *refs[:8], *refs[11:])

    return launch(
        kernel, "ffn_in_rest", [normed, *arrays, *so_far],
        [whole(normed.shape)] + [ANY] * 11, [per_slot] * 3,
        like(bf16, *[v.shape for v in so_far]), grid=(count,), offs=offs,
        scratch=[
            pltpu.VMEM((count, d, 2 * hidden), bf16),
            pltpu.SemaphoreType.DMA((copies_per_chunk,)),
        ],
        cost=cost(4 * length * d * count * hidden, 16, count * length * hidden),
        after=after, mib=20, alias=9, n_alias=3,
    )


def ffn_out_kernel(
    sc, hid_ref, inner_ref, gain_ref, wp_ref, padc_ref, query_ref, cot_ref, top_ref, own, *refs
):
    arrays = refs[:8]
    score_ref, nfin, ge, total_ref, gft_ref, ghf_ref, wd, sems, acc, embed, unit = refs[8:]
    length, d = hid_ref.shape
    step = pl.program_id(0)
    copies = chunk_copies(sc, [(own, 0)], arrays, wd, sems)
    blocks = length // tile

    @pl.when(step == 0)
    def _():
        for copy in copies:
            copy.start()
        acc[...] = hid_ref[...]
        for copy in copies:
            copy.wait()

    acc[...] += dot(inner_ref[0], wd[step])

    @pl.when(step == pl.num_programs(0) - 1)
    def _():
        lane = lax.broadcasted_iota(jnp.int32, padc_ref.shape, 1)
        pad = jnp.sum(jnp.where(lane == sc[16], padc_ref[...], 0.0), axis=1, keepdims=True)
        gain = gain_ref[...]
        for a in range(blocks):
            rows = slice(a * tile, (a + 1) * tile)
            h = acc[rows, :]
            n = (h * rms_scale(h) * gain).astype(bf16)
            nfin[rows, :] = n
            e = dot(n, wp_ref[...])
            embed[rows, :] = e
            inverse = lax.rsqrt(jnp.sum(e * e, axis=1, keepdims=True) + eps)
            unit[rows, :] = (e * inverse * pad[rows]).astype(bf16)
        query = query_ref[0]
        cot = cot_ref[0]
        top = top_ref[0]
        scored = dot(query, unit[...], ((1,), (1,)))
        place = lax.broadcasted_iota(jnp.int32, scored.shape, 1)
        out_lane = lax.broadcasted_iota(jnp.int32, cot.shape, 1)
        chosen = jnp.zeros_like(cot)
        weight = jnp.zeros_like(scored)
        for j in range(top.shape[1]):
            here = place == top[:, j : j + 1]
            mine = jnp.sum(jnp.where(here, scored, 0.0), axis=1, keepdims=True)
            chosen = jnp.where(out_lane == j, mine, chosen)
            weight = weight + jnp.where(here, cot[:, j : j + 1], 0.0)
        score_ref[...] = chosen
        high, low = high_low(weight)
        gunit = dot(high, query, ((0,), (0,))) + dot(low, query, ((0,), (0,)))
        total = jnp.zeros((1, d), f32)
        for a in range(blocks):
            rows = slice(a * tile, (a + 1) * tile)
            e = embed[rows, :]
            inverse = lax.rsqrt(jnp.sum(e * e, axis=1, keepdims=True) + eps)
            u = gunit[rows] * pad[rows]
            cube = (inverse * inverse * inverse) * jnp.sum(u * e, axis=1, keepdims=True)
            g = (inverse * u - e * cube).astype(bf16)
            ge[rows, :] = g
            back, part = rms_back(acc[rows, :], gain, dot(g, wp_ref[...], ((1,), (1,))))
            total = total + part
            ghf_ref[rows, :] = back
            gft_ref[rows, :] = back.astype(bf16)
        total_ref[...] = total


def ffn_out(offs, hid, inner, gain, w_proj, pad_cols, query, cot, top, own, arrays):
    length, d = hid.shape
    slots, _, hidden = inner.shape
    e = w_proj.shape[1]

    def row_block(v):
        return pl.BlockSpec((1,) + v.shape[1:], lambda i, sc: (sc[16], 0, 0))

    score, low, embed, total = cot.shape[1:], (length, d), (length, e), (1, d)
    return launch(
        ffn_out_kernel, "ffn_out",
        [hid, inner, gain, w_proj, pad_cols, query, cot, top, own, *arrays],
        [whole(hid.shape), pl.BlockSpec((1, length, hidden), lambda i, sc: (i, 0, 0))]
        + [whole(v.shape) for v in (gain, w_proj, pad_cols)]
        + [row_block(v) for v in (query, cot, top)]
        + [ANY] * 9,
        [whole(v) for v in (score, low, embed, total, low, low)],
        like(f32, score) + like(bf16, low, embed) + like(f32, total) + like(bf16, low)
        + like(f32, low),
        grid=(slots,), offs=offs,
        scratch=[
            pltpu.VMEM((slots, hidden, d), bf16),
            pltpu.SemaphoreType.DMA((copies_per_chunk,)),
            pltpu.VMEM((length, d), f32),
            pltpu.VMEM((length, e), f32),
            pltpu.VMEM((length, e), bf16),
        ],
        cost=cost(2 * length * d * slots * hidden, 16), mib=24,
    )


def ffn_back_kernel(sc, hid_ref, gft_ref, ghf_ref, act_ref, dact_ref, gain_ref, *refs):
    slots = 4
    own, first, own_down, second = refs[:3], refs[3:11], refs[11], refs[12:20]
    refs = refs[20:]
    gg_ref, gu_ref, gha_ref, gat_ref, gm_ref, total_ref, w, wd, w_sems, d_sems, acc = refs
    length, d = hid_ref.shape
    hidden = wd.shape[1]
    step = pl.program_id(0)
    w_copies = chunk_copies(sc, zip(own, (0, hidden, 2 * hidden)), first, w, w_sems)
    d_copies = chunk_copies(sc, [(own_down, 0)], second, wd, d_sems)
    blocks = length // tile

    @pl.when(step == 0)
    def _():
        for copy in d_copies + w_copies:
            copy.start()
        acc[...] = jnp.zeros_like(acc)
        for copy in d_copies:
            copy.wait()

    def part(n, carry):
        cols = pl.ds(pl.multiple_of(n * 256, 256), 256)
        gi = dot(gft_ref[...], wd[step, cols, :], ((1,), (1,)))
        gg_ref[0, :, cols] = (gi * dact_ref[0, :, cols].astype(f32)).astype(bf16)
        gu_ref[0, :, cols] = (gi * act_ref[0, :, cols].astype(f32)).astype(bf16)
        return carry

    lax.fori_loop(0, hidden // 256, part, 0)

    @pl.when(step == 0)
    def _():
        for copy in w_copies:
            copy.wait()

    acc[...] += dot(gg_ref[0], w[step, :, :hidden], ((1,), (1,))) + dot(
        gu_ref[0], w[step, :, hidden : 2 * hidden], ((1,), (1,))
    )

    @pl.when(step == slots - 1)
    def _():
        gain = gain_ref[...]
        total = jnp.zeros((1, d), f32)
        for a in range(blocks):
            rows = slice(a * tile, (a + 1) * tile)
            back, part = rms_back(hid_ref[rows, :], gain, acc[rows, :])
            total = total + part
            g = ghf_ref[rows, :] + back
            gha_ref[rows, :] = g
            g = g.astype(bf16)
            gat_ref[rows, :] = g
            for k in range(slots):
                gm_ref[k, rows, :] = dot(g, w[k, :, 2 * hidden :]).astype(bf16)
        total_ref[...] = total


def ffn_back(offs, hid, gft, ghf, act, dact, gain, own, first, own_down, second, after=()):
    length, d = hid.shape
    slots, _, hidden = act.shape
    width = first[0].shape[3]
    mixed = (slots, length, width - 2 * hidden)
    block = pl.BlockSpec((1, length, hidden), lambda i, sc: (i, 0, 0))
    return launch(
        ffn_back_kernel, "ffn_back",
        [hid, gft, ghf, act, dact, gain, *own, *first, own_down, *second],
        [whole(v.shape) for v in (hid, gft, ghf)] + [block] * 2 + [whole(gain.shape)] + [ANY] * 20,
        [block, block] + [whole(v) for v in (hid.shape, hid.shape, mixed, (1, d))],
        like(bf16, act.shape, act.shape) + like(f32, hid.shape) + like(bf16, hid.shape, mixed)
        + like(f32, (1, d)),
        grid=(slots,), offs=offs,
        scratch=[
            pltpu.VMEM((slots, d, width), bf16),
            pltpu.VMEM((slots, hidden, d), bf16),
            pltpu.SemaphoreType.DMA((copies_per_chunk,)),
            pltpu.SemaphoreType.DMA((copies_per_chunk,)),
            pltpu.VMEM((length, d), f32),
        ],
        cost=cost(2 * length * d * (3 * slots * hidden + d), 24),
        after=after, mib=42,
    )


def keep_parts(sc, out, refs):
    send_a, keep_a, send_b, keep_b = refs
    half = send_a.shape[2]
    x, y = sc[18], sc[19]

    def rows(y, x, extra):
        at = pl.multiple_of((2 * y + x) * (2 * half) + extra, 16)
        return out[pl.ds(at, half), :]

    for other in range(2):
        send_a[0, other] = rows(other, 1 - x, 0)
        keep_a[0, other] = rows(other, x, 0)
        send_b[0, other] = rows(1 - y, other, half)
        keep_b[0, other] = rows(y, other, half)


def parts_of(slots, rows, width):
    part = (1, 2, rows // 8, width)
    spec = pl.BlockSpec(part, lambda i, sc: (i, 0, 0, 0))
    return [spec] * 4, [jax.ShapeDtypeStruct((slots,) + part[1:], bf16)] * 4


def product_kernel(lefts, pairs, keep, sc, *refs):
    left_refs, right_refs = refs[:lefts], refs[lefts : lefts + len(pairs)]
    refs = refs[lefts + len(pairs) :]
    out = refs[-1] if keep else refs[-1].at[0]
    at = 0
    for right_ref, which in zip(right_refs, pairs):
        right = right_ref[...]
        left = left_refs[which][...]
        left, right = (v.reshape(v.shape[-2:]) for v in (left, right))
        cols = slice(at, at + right.shape[1])
        value = dot(left, right, ((0,), (0,)))
        if keep:
            value = value + refs[0][0, :, cols].astype(f32)
        out[:, cols] = value.astype(bf16)
        at += right.shape[1]
    if keep:
        keep_parts(sc, out, refs[-5:-1])


def products(offs, lefts, rights, slots, got=None, after=()):
    keep = got is not None
    length, half = lefts[0].shape[-2], lefts[0].shape[-1] // 2
    width = sum(right.shape[-1] for right, _ in rights)

    def which(sc):
        return sc[17] if keep else 1 - sc[17]

    specs = []
    for left in lefts:
        if left.ndim == 3:
            specs.append(pl.BlockSpec((1, length, half), lambda i, sc: (i, 0, which(sc))))
        else:
            specs.append(pl.BlockSpec((length, half), lambda i, sc: (0, which(sc))))
    for right, _ in rights:
        if right.ndim == 3:
            specs.append(pl.BlockSpec((1,) + right.shape[1:], lambda i, sc: (i, 0, 0)))
        else:
            specs.append(whole(right.shape))
    args = list(lefts) + [right for right, _ in rights]
    block = pl.BlockSpec((1, half, width), lambda i, sc: (i, 0, 0))
    out_specs, out_shape, scratch = [block], like(bf16, (slots, half, width)), []
    if keep:
        specs.append(block)
        args.append(got)
        out_specs, out_shape = parts_of(slots, half, width)
        scratch = [pltpu.VMEM((half, width), bf16)]
    return launch(
        functools.partial(product_kernel, len(lefts), [i for _, i in rights], keep),
        "products_keep" if keep else "products_send",
        args, specs, out_specs, out_shape, grid=(slots,), offs=offs, scratch=scratch, after=after,
        mib=16,
    )


def attn_product_kernel(keep, sc, la, lb, ra, rb, small, *refs):
    out = refs[-1] if keep else refs[-1].at[0]
    quarter, d = la.shape[3], ra.shape[2]
    for left, right, at in ((la, ra, 0), (lb, rb, quarter)):
        value = dot(left[0, 0], right[0], ((0,), (0,)))
        if keep:
            value = value + refs[0][0, at : at + quarter, :d].astype(f32)
        out[at : at + quarter, :d] = value.astype(bf16)
    value = small[0]
    if keep:
        value = add(value, refs[0][0, :, d:])
    out[:, d:] = value
    if keep:
        keep_parts(sc, out, refs[1:5])


def attn_products(offs, left, both, small, got=None, after=()):
    keep = got is not None
    slots, _, length, quarter = left.shape
    d = both.shape[2]
    width = d + small.shape[2]
    half = 2 * quarter

    def which(sc):
        return sc[17] if keep else 1 - sc[17]

    block = pl.BlockSpec((1, half, width), lambda i, sc: (i, 0, 0))
    specs = [
        pl.BlockSpec((1, 1, length, quarter), lambda i, sc: (i, 2 * which(sc), 0, 0)),
        pl.BlockSpec((1, 1, length, quarter), lambda i, sc: (i, 2 * which(sc) + 1, 0, 0)),
        pl.BlockSpec((1, length, d), lambda i, sc: (0, 0, 0)),
        pl.BlockSpec((1, length, d), lambda i, sc: (which(sc), 0, 0)),
        pl.BlockSpec((1, half, small.shape[2]), lambda i, sc: (i, which(sc), 0)),
    ]
    args = [left, left, both, both, small]
    out_specs, out_shape, scratch = [block], like(bf16, (slots, half, width)), []
    if keep:
        specs.append(block)
        args.append(got)
        out_specs, out_shape = parts_of(slots, half, width)
        scratch = [pltpu.VMEM((half, width), bf16)]
    return launch(
        functools.partial(attn_product_kernel, keep), "attn_keep" if keep else "attn_send",
        args, specs, out_specs, out_shape, grid=(slots,), offs=offs, scratch=scratch, after=after,
        mib=16,
    )


def add(a, b):
    return (a.astype(f32) + b.astype(f32)).astype(bf16)


def second_kernel(sc, ka, ra, kb, rb, send_a, keep_a, send_b, keep_b):
    x, y = sc[18], sc[19]
    send_a[0] = add(ka[0, 1 - y], ra[0, 1 - y])
    keep_a[0] = add(ka[0, y], ra[0, y])
    send_b[0] = add(kb[0, 1 - x], rb[0, 1 - x])
    keep_b[0] = add(kb[0, x], rb[0, x])


def second_sums(offs, *arrays, after=()):
    slots, _, half, width = arrays[0].shape
    into = pl.BlockSpec((1, 2, half, width), lambda i, sc: (i, 0, 0, 0))
    out = pl.BlockSpec((1, half, width), lambda i, sc: (i, 0, 0))
    return launch(
        second_kernel, "second_sums", arrays, [into] * 4, [out] * 4,
        like(bf16, *[(slots, half, width)] * 4), grid=(slots,), offs=offs, after=after,
    )


def third_kernel(ka, ra, kb, rb, *outs):
    half = ka.shape[1]
    for k, out in enumerate(outs):
        out[:half, :] = add(ka[k], ra[k])
        out[half:, :] = add(kb[k], rb[k])


def third_sums(*arrays, after=()):
    slots, half, width = arrays[0].shape
    shape = (2 * half, width)
    return launch(
        third_kernel, "third_sums", arrays, [whole(arrays[0].shape)] * 4, [whole(shape)] * slots,
        like(bf16, *[shape] * slots), after=after,
    )


def third_stacked_kernel(sc, ka, ra, kb, rb, out):
    n, half, _ = ka.shape
    for k in range(n):
        to = lax.rem(sc[16] + n - k, n)
        out[to, :half, :] = add(ka[k], ra[k])
        out[to, half:, :] = add(kb[k], rb[k])


def third_stacked(offs, *arrays, after=()):
    slots, half, width = arrays[0].shape
    shape = (slots, 2 * half, width)
    (out,), token = launch(
        third_stacked_kernel, "third_stacked", arrays, [whole(arrays[0].shape)] * 4,
        [whole(shape)], like(bf16, shape), offs=offs, after=after,
    )
    return out, token


def last_kernel(*refs):
    t = [ref[...].astype(f32) for ref in refs[:4]]
    refs[4][...] = ((t[0] + t[2]) + (t[1] + t[3])).astype(refs[4].dtype)


def last_sum(arrays, dtype, after=()):
    shape = arrays[0].shape
    return launch(
        last_kernel, "last_sum", arrays, [whole(shape)] * 4, [whole(shape)], like(dtype, shape),
        after=after,
    )


def stack_kernel(a, xa, b, yb, sa, sb):
    sa[0], sa[1], sb[0], sb[1] = a[...], xa[...], b[...], yb[...]


def stack_pairs(a, xa, b, yb, after):
    out = (2,) + a.shape
    return launch(
        stack_kernel, "stack_pairs", [a, xa, b, yb], [whole(a.shape)] * 4, [whole(out)] * 2,
        like(bf16, out, out), after=after,
    )


class Reduce:
    def __init__(self, place, offs, kept):
        self.place, self.offs, self.kept = place, offs, kept

    def first(self, after=()):
        send_a, keep_a, send_b, keep_b = self.kept
        ra, rb = self.place.swap(send_a, XBIT), self.place.swap(send_b, YBIT)
        self.kept, token = second_sums(self.offs, keep_a, ra, keep_b, rb, after=after)
        return token

    def second(self, after=()):
        send_a, keep_a, send_b, keep_b = self.kept
        ra, rb = self.place.swap(send_a, YBIT), self.place.swap(send_b, XBIT)
        self.kept, token = third_sums(keep_a, ra, keep_b, rb, after=after)
        return token

    def second_and_third(self, after=()):
        send_a, keep_a, send_b, keep_b = self.kept
        ra, rb = self.place.swap(send_a, YBIT), self.place.swap(send_b, XBIT)
        v, token = third_stacked(self.offs, keep_a, ra, keep_b, rb, after=after)
        total = lax.psum_scatter(v, "mp", scatter_dimension=0, tiled=True)
        if self.place.n_out > 1:
            total = lax.psum(total.astype(f32), "out").astype(bf16)
        self.total = total.reshape(v.shape[1:])
        return token

    def third(self, after=()):
        p = self.place
        t = [self.kept[0]] + [p.shift(self.kept[k], -k) for k in range(1, p.n_mp)]
        if p.n_out > 1:
            (total,), token = last_sum(t, f32, after)
            self.total = lax.psum(total, "out").astype(bf16)
        else:
            (self.total,), token = last_sum(t, bf16, after)
        return token


def open_kernel(v_ref, *outs):
    rows = v_ref.shape[3]
    for at, (c, y, x) in enumerate(np.ndindex(2, 2, 2)):
        left = 0
        for out in outs:
            value = v_ref[y, x, c, :, left : left + out.shape[1]]
            out[at * rows : (at + 1) * rows, :] = value.astype(f32)
            left += out.shape[1]


def beside_kernel(a, b, out):
    out[:, : a.shape[1]] = a[...]
    out[:, a.shape[1] :] = b[...]


def gathered(a, b, cuts, start_after, after):
    rows, width = a.shape[0], a.shape[1] + b.shape[1]
    (v,), _ = launch(
        beside_kernel, "beside", [a, b], [whole(a.shape), whole(b.shape)],
        [whole((rows, width))], like(bf16, (rows, width)), after=start_after,
    )
    v = lax.all_gather(v, group, tiled=False).reshape(2, 2, 2, rows, width)
    shapes = [(8 * rows, cut) for cut in cuts]
    return launch(
        open_kernel, "open", [v], [whole(v.shape)], [whole(shape) for shape in shapes],
        like(f32, *shapes), after=after, mib=58,
    )


def unpack_kernel(offs, *refs):
    arrays, outs, small, full = refs[:8], refs[8:-2], refs[-2], refs[-1]
    for at in range(16):
        value = arrays[at // 2][at % 2]
        rows = pl.ds(pl.multiple_of(offs[at], 16), value.shape[0])
        full[rows, :] = value.astype(f32)
    rows, d = outs[0].shape
    for i, out in enumerate(outs):
        out[...] = full[i * rows : (i + 1) * rows, :d]
    small[...] = full[:, d:]


def unpack(offs, arrays, count, small):
    half, width = arrays[0].shape[1:]
    rows, d = 16 * half, width - small
    shapes = [(rows // count, d)] * count + [(rows, small)]
    outs, _ = launch(
        unpack_kernel, "unpack", arrays, [whole(v.shape) for v in arrays],
        [whole(v) for v in shapes], like(f32, *shapes), offs=offs,
        scratch=[pltpu.VMEM((rows, width), f32)],
    )
    return outs


def local(
    tokens, segment_ids, pad_mask, top_index, query_emb, score_cot, gain_attn, w_query, w_key,
    w_value, w_out, rel_table, gain_ffn, w_gate, w_up, w_down, gain_final, w_proj,
):
    place = Place()
    slots = place.n_mp
    rows, length = segment_ids.shape
    d = tokens.shape[1]
    heads = rel_table.shape[1]
    size = w_query.shape[1] // heads
    wide = heads * size
    hot = jnp.asarray(bucket_hot(rel_table.shape[0], length), bf16)
    segs, pads = segment_ids.astype(f32), pad_mask.astype(f32)
    seg_cols, pad_cols = segs.T, pads.T
    gain_a, gain_f, gain_l = (
        g.astype(f32).reshape(1, d) for g in (gain_attn, gain_ffn, gain_final)
    )
    offs = place.offsets(d // 8)

    buckets = rel_table.shape[0]
    table = jnp.zeros((64, d), bf16).at[:heads, :buckets].set(rel_table.T)
    w_qkv = jnp.concatenate([w_query.T, w_key.T, w_value.T, table])
    w_out_t = w_out.T
    eighth = d // 8
    hidden = w_gate.shape[1]

    def piece(*arrays):
        parts = []
        for v in arrays:
            rows = v.shape[0] // 8
            parts.append(lax.dynamic_slice_in_dim(v, place.p * rows, rows, 0))
        return jnp.concatenate(parts, axis=1) if len(parts) > 1 else parts[0]

    common = (offs, tokens, segs, pads, seg_cols, gain_a)
    z1 = lax.all_gather(piece(w_gate, w_up, w_out_t), "mp")
    piece2 = jnp.concatenate([piece(w_down), piece(w_qkv)])
    z2 = lax.all_gather(piece2, "mp")
    (attended,), done = attend(1, *common, w_qkv, hot, heads, size, (piece2,))
    mixed = [attended[slots - 1]] + [place.shift(attended[k - 1], k) for k in range(1, slots)]
    halved, _ = split(offs, z1, eighth, (done,))
    s1, done1 = place.first_round(*halved, mixed[1:])
    first = place.second_round(*s1)
    (*halved, z2), done = split(offs, z2, eighth, (done1,))
    all_qkv = lax.all_gather(z2, group)
    all_qkv = all_qkv.reshape((2, 2, 2) + all_qkv.shape[-3:])
    own = (w_gate, w_up, w_out_t)
    (hid, normed_ffn, *gates), done = ffn_in_first(
        slots // 2, offs, tokens, gain_f, mixed, own, first, length, (done,)
    )
    s2, done = place.first_round(*halved, (done,))
    (act, dact, inner), done = ffn_in_rest(slots // 2, offs, normed_ffn, gates, first, (done,))
    second = place.second_round(*s2, (done,))
    (score, nfin, ge, gain_fin, gft, ghf), _ = ffn_out(
        offs, hid, inner, gain_l, w_proj, pad_cols, query_emb, score_cot, top_index, w_down, second
    )
    down_sides = ([inner, nfin], [(gft, 0), (ge, 1)])
    (send,), _ = products(offs, *down_sides, slots)
    kept, kept_done = products(offs, *down_sides, slots, place.swap(send, CORE))
    down = Reduce(place, offs, kept)
    (gg, gu, gha, gat, gm, gain_mid), done = ffn_back(
        offs, hid, gft, ghf, act, dact, gain_f, own, first, w_down, second, (kept_done,)
    )
    done = down.first((done,))
    gu_sides = ([normed_ffn], [(gg, 0), (gu, 0)])
    (send,), _ = products(offs, *gu_sides, slots, None, (done,))
    got = place.swap(send, CORE)
    finish = [gha, gat, gain_fin, gain_mid, score]

    def back(first, acc, left, after):
        return attend_back(
            first, slots // 2, common + (hot,), gm, mixed, acc, left, finish, all_qkv, heads, size,
            after,
        )

    (left, tables, acc), done = back(0, None, None, (done,))
    done = down.second((done,))
    kept, done = products(offs, *gu_sides, slots, got, (done,))
    gate_up = Reduce(place, offs, kept)
    finish.append(tables)
    (left, _, dx, both, small), done = back(slots // 2, acc, left, (done,))
    right, left_ = place.both_ways(dx, dx)
    done = down.third((done,))
    done = gate_up.first((done,))
    (send,), _ = attn_products(offs, left, both, small, None, (done,))
    kept, done = attn_products(offs, left, both, small, place.swap(send, CORE))
    attn = Reduce(place, offs, kept)
    (*so_far, right, left_), done = collect(1, slots, offs, right, left_, dx, None, (done,))
    done = gate_up.second_and_third((done,))
    done = attn.first((done,))
    right, left_ = place.both_ways(right, left_)
    done = attn.second((done,))
    (*so_far, right, left_), done = collect(2, slots, offs, right, left_, dx, so_far, (done,))
    start_after = (done,)
    right, left_ = place.both_ways(right, left_)
    done = attn.third((done,))
    (input_grad, packed), done = collect(3, slots, offs, right, left_, dx, so_far, (done,))
    (grad_down, grad_proj, grad_gate, grad_up), done = gathered(
        down.total, gate_up.total, (d, w_proj.shape[1], hidden, hidden), start_after, (done,)
    )
    last, _ = place.first_round(*halves(attn.total, 0), (done,))
    grad_q, grad_k, grad_v, grad_out, small = unpack(
        offs, place.second_round(*last), 4, small.shape[2]
    )

    input_grad = input_grad.reshape(rows * length, d)
    n, m = score.shape
    packed = packed.astype(f32).reshape(slots, 16, d // 128, 128)[:, :, : 2 * (n // 16), :m]
    packed = packed[:, :, 0::2] + packed[:, :, 1::2]
    scores = packed.transpose(0, 2, 1, 3).reshape(slots, n, m)
    return (
        scores,
        input_grad,
        small[:, 0],
        grad_q.T,
        grad_k.T,
        grad_v.T,
        grad_out,
        small[:buckets, 64 : 64 + heads],
        small[:, 2],
        grad_gate,
        grad_up,
        grad_down,
        small[:, 1],
        grad_proj,
    )


def solution(mesh):
    n_dp, n_mp = mesh.shape["dp"], mesh.shape["mp"]
    mesh = Mesh(mesh.devices.reshape(n_dp // 8, 2, 2, 2, n_mp), dp + ("mp",))
    return jax.shard_map(
        local,
        mesh=mesh,
        in_specs=(
            P(dp, None),
            P(dp, None),
            P(dp, None),
            P(dp, None, None),
            P(dp, None, None),
            P(dp, None, None),
            P(),
            P(None, "mp"),
            P(None, "mp"),
            P(None, "mp"),
            P("mp", None),
            P(None, "mp"),
            P(),
            P(None, "mp"),
            P(None, "mp"),
            P("mp", None),
            P(),
            P(),
        ),
        out_specs=(
            P(dp, None, None),
            P(dp, None),
            P(),
            P(None, "mp"),
            P(None, "mp"),
            P(None, "mp"),
            P("mp", None),
            P(None, "mp"),
            P(),
            P(None, "mp"),
            P(None, "mp"),
            P("mp", None),
            P(),
            P(),
        ),
        check_vma=False,
    )
```

```python
import functools
import math

import jax
import jax.numpy as jnp
import numpy as np
from jax import lax
from jax.experimental import pallas as pl
from jax.experimental.pallas import tpu as pltpu
from jax.sharding import Mesh
from jax.sharding import PartitionSpec as P

f32 = jnp.float32
bf16 = jnp.bfloat16
eps = 1e-06
masked_logit = -1e30
gelu_c = math.sqrt(2.0 / math.pi)
CORE, XBIT, YBIT = "core", "x", "y"
group = ("y", "x", "core")
dp = ("out",) + group
span = 1024
tile = 128


def bucket_hot(buckets, length):
    column = np.arange(span)
    base = length - tile
    offset = np.where(column < base + length, column - base, column - span - base)
    distance = np.abs(offset)
    far = 8 + sum((distance >= t).astype(np.int32) for t in (12, 16, 23, 32, 46, 64, 91))
    bucket = np.where(distance < 8, distance, far) + 16 * (offset > 0)
    hot = (bucket[None, :] == np.arange(tile)[:, None]) & (np.arange(tile)[:, None] < buckets)
    return hot.astype(np.float32)


def dot(a, b, dims=((1,), (0,))):
    return lax.dot_general(a, b, (dims, ((), ())), preferred_element_type=f32)


def rms_scale(v):
    return lax.rsqrt(jnp.mean(v * v, axis=-1, keepdims=True) + eps)


def rms_back(v, gain, grad):
    s = rms_scale(v)
    w = grad * gain
    value = s * w - v * ((s * s * s) * jnp.mean(w * v, axis=-1, keepdims=True))
    return value, jnp.sum(grad * v * s, axis=0, keepdims=True)


def whole(shape):
    return pl.BlockSpec(shape, lambda *_: (0,) * len(shape))


ANY = pl.BlockSpec(memory_space=pl.ANY)
token_shape = (8, 128)


def launch(
    kernel, name, args, in_specs, out_specs, out_shape, grid=(1,), offs=None, scratch=(),
    cost=None, after=(), alias=None, n_alias=1, mib=16,
):
    first = 0 if offs is None else 1
    n_in, n_out, n_after = first + len(args), len(out_shape), len(after)

    def body(*refs):
        ins, rest = refs[:n_in], refs[n_in + n_after :]
        outs, token, own = rest[:n_out], rest[n_out], rest[n_out + 1 :]
        token[...] = jnp.zeros(token_shape, f32)
        kernel(*ins, *outs, *own)

    specs = dict(
        grid=grid,
        in_specs=list(in_specs) + [ANY] * n_after,
        out_specs=list(out_specs) + [whole(token_shape)],
        scratch_shapes=list(scratch),
    )
    if offs is None:
        specs = dict(specs)
        scalars = []
    else:
        specs = dict(grid_spec=pltpu.PrefetchScalarGridSpec(num_scalar_prefetch=1, **specs))
        scalars = [offs]
    *outs, token = pl.pallas_call(
        body,
        out_shape=list(out_shape) + [jax.ShapeDtypeStruct(token_shape, f32)],
        input_output_aliases=(
            {} if alias is None else {alias + first + i: i for i in range(n_alias)}
        ),
        compiler_params=pltpu.CompilerParams(
            vmem_limit_bytes=mib << 20, dimension_semantics=("arbitrary",)
        ),
        cost_estimate=cost or cheap,
        name=name,
        **specs,
    )(*scalars, *args, *after)
    return outs, token


cheap = pl.CostEstimate(flops=1 << 20, bytes_accessed=1 << 16, transcendentals=0)


def cost(flops, mib, transcendentals=0):
    return pl.CostEstimate(
        flops=flops, bytes_accessed=mib << 20, transcendentals=transcendentals
    )


def like(dtype, *shapes):
    return [jax.ShapeDtypeStruct(shape, dtype) for shape in shapes]


class Place:
    def __init__(self):
        self.n_out, self.n_mp = lax.axis_size("out"), lax.axis_size("mp")
        self.c, self.x, self.y = (lax.axis_index(name) for name in ("core", "x", "y"))
        self.z = lax.axis_index("mp")
        self.p = self.c * 4 + self.y * 2 + self.x

    def swap(self, v, name):
        return lax.ppermute(v, name, [(0, 1), (1, 0)])

    def shift(self, v, k):
        n = self.n_mp
        return lax.ppermute(v, "mp", [(i, (i + k) % n) for i in range(n)])

    def offsets(self, rows):
        half = rows // 2
        out = []
        for flip in (0, 4):
            p = self.p ^ flip
            for other, extra in (
                (0, 0), (1, 0), (0, half), (2, half), (2, 0), (3, 0), (1, half), (3, half),
            ):
                out.append((p ^ other) * rows + extra)
        return jnp.stack(out + [self.z, self.c, self.x, self.y]).astype(jnp.int32)

    def both_ways(self, right, left):
        n = self.n_mp
        right = lax.ppermute(right, "mp", [(i, i + 1) for i in range(n - 1)])
        return right, lax.ppermute(left, "mp", [(i + 1, i) for i in range(n - 1)])

    def first_round(self, a, b, after=()):
        return stack_pairs(a, self.swap(a, XBIT), b, self.swap(b, YBIT), after)

    def second_round(self, sa, sb):
        near = [sa, sb, self.swap(sa, YBIT), self.swap(sb, XBIT)]
        return near + [self.swap(t, CORE) for t in near]


def pick(v, axis, index):
    return lax.dynamic_index_in_dim(v, index, axis, keepdims=False)


def halves(v, axis):
    half = v.shape[axis] // 2
    return (
        lax.slice_in_dim(v, 0, half, axis=axis),
        lax.slice_in_dim(v, half, 2 * half, axis=axis),
    )


def chunk_copies(offs, own, arrays, dst, sems, first=0, slot=0):
    slots, rows, width = dst.shape
    half = rows // 16
    skip = 0 if slot else 1
    pairs = [
        (ref, dst.at[0, :, pl.ds(column, ref.shape[1])]) for ref, column in own
    ]
    for at in range(16):
        src = arrays[at // 2].at[at % 2, pl.ds(slot + skip - 1, slots - skip)]
        if src.shape[2] != width:
            src = src.at[:, :, pl.ds(first, width)]
        start = pl.multiple_of(offs[at], 16)
        pairs.append((src, dst.at[pl.ds(skip, slots - skip), pl.ds(start, half), :]))
    return [pltpu.make_async_copy(s, d, sems.at[i]) for i, (s, d) in enumerate(pairs)]


copies_per_chunk = 20


def gathered_copies(gathered, dst, sems, shard=None):
    full = gathered.shape[4]
    out = []
    for at, (c, y, x) in enumerate(np.ndindex(2, 2, 2)):
        rows = pl.ds(at * full, full)
        if shard is None:
            out.append((gathered.at[y, x, c], dst.at[:, rows, :]))
        else:
            out.append((gathered.at[y, x, c, shard], dst.at[rows, :]))
    return [pltpu.make_async_copy(s, d, sems.at[i]) for i, (s, d) in enumerate(out)]


def split_kernel(sc, v_ref, a_ref, b_ref, *rest):
    half = a_ref.shape[1]
    n = v_ref.shape[0]
    for ref in rest:
        ref[...] = v_ref[:, 2 * half :, :]
    for k in range(1, n):
        at = lax.rem(sc[16] + n - k, n)
        a_ref[k - 1] = v_ref[at, :half, :]
        b_ref[k - 1] = v_ref[at, half : 2 * half, :]


def split(offs, v, rows, after=()):
    n, _, width = v.shape
    out = (n - 1, rows // 2, width)
    shapes = [out, out] + ([(n, v.shape[1] - rows, width)] if v.shape[1] > rows else [])
    return launch(
        split_kernel, "split", [v], [whole(v.shape)], [whole(shape) for shape in shapes],
        like(bf16, *shapes), offs=offs, after=after,
    )


def relay_kernel(a, b):
    b[...] = a[...]


def relay(a, after):
    (a,), _ = launch(
        relay_kernel, "relay", [a], [whole(a.shape)], [whole(a.shape)], like(a.dtype, a.shape),
        after=after,
    )
    return a


def collect_kernel(step, n, sc, right, left, own, *refs):
    out, rest, *on = refs
    length = out.shape[1]
    side = pl.program_id(0)
    z = sc[16]

    @pl.when((side == 0) & (z >= step))
    def _():
        out[0] = right[:length, :].astype(f32)
        rest[0] = right[length:, :]

    @pl.when((side == 1) & (z + step < n))
    def _():
        out[0] = left[:length, :].astype(f32)
        rest[0] = left[length:, :]

    @pl.when(((side == 0) & (z < step)) | ((side == 1) & (z + step >= n)))
    def _():
        out[0] = own[:length, :].astype(f32)
        rest[0] = own[length:, :]

    @pl.when(side == 0)
    def _():
        for new, old in zip(on, (right, left)):
            new[...] = old[...]


def collect(step, n, offs, right, left, own, so_far, after):
    rows, d = own.shape
    length = rows // tile * tile

    def index(i, sc):
        z = sc[16]
        near, far = jnp.where(z >= step, z - step, z), jnp.where(z + step < n, z + step, z)
        return (jnp.where(i == 0, near, far), 0, 0)

    goes_on = step < n - 1
    kept = list(so_far or ())
    shapes = [(n, length, d), (n, rows - length, d)]
    out_shape = like(f32, shapes[0]) + like(bf16, shapes[1])
    out_specs = [pl.BlockSpec((1,) + shape[1:], index) for shape in shapes]
    if goes_on:
        out_shape += like(bf16, own.shape, own.shape)
        out_specs += [whole(own.shape)] * 2

    def kernel(sc, right, left, own, *refs):
        collect_kernel(step, n, sc, right, left, own, *refs[len(kept) :])

    return launch(
        kernel, f"collect{step}", [right, left, own, *kept],
        [whole(own.shape)] * 3 + [ANY] * len(kept), out_specs, out_shape, grid=(2,), offs=offs,
        after=after, alias=3 if kept else None, n_alias=2,
    )


def skew(base):
    t = jnp.broadcast_to(base, (8, span))
    row = lax.broadcasted_iota(jnp.int32, (8, span), 0)
    for step in (1, 2, 4):
        t = jnp.where((row & step) != 0, pltpu.roll(t, step, 1), t)
    while t.shape[0] < tile:
        t = jnp.concatenate([t, pltpu.roll(t, t.shape[0], 1)], axis=0)
    return t


def unskew(t):
    while t.shape[0] > 8:
        n = t.shape[0] // 2
        t = t[:n] + pltpu.roll(t[n:], span - n, 1)
    row = lax.broadcasted_iota(jnp.int32, (8, span), 0)
    for step in (1, 2, 4):
        t = jnp.where((row & step) != 0, pltpu.roll(t, span - step, 1), t)
    return jnp.sum(t, axis=0, keepdims=True)


def fill_mask(mask, segs, pads, seg_cols, row):
    length = mask.shape[0]
    rows = segs.shape[0]
    chosen = lax.broadcasted_iota(jnp.int32, (rows, length), 0) == row
    seg_k = jnp.sum(jnp.where(chosen, segs, 0.0), axis=0, keepdims=True)
    pad_k = jnp.sum(jnp.where(chosen, pads, 0.0), axis=0, keepdims=True)
    code = jnp.where(pad_k == 1.0, seg_k, -1.0)
    lane = lax.broadcasted_iota(jnp.int32, seg_cols.shape, 1)
    seg_q = jnp.sum(jnp.where(lane == row, seg_cols, 0.0), axis=1, keepdims=True)
    q = lax.broadcasted_iota(jnp.int32, (tile, length), 0)
    k = lax.broadcasted_iota(jnp.int32, (tile, length), 1)
    for a in range(length // tile):
        own = seg_q[a * tile : (a + 1) * tile]
        ok = (own == code) | (q + a * tile == k)
        mask[a * tile : (a + 1) * tile, :] = jnp.where(ok, 0.0, masked_logit)


def fill_bias(bias, table, hot, heads):
    base = dot(table, hot[0 : table.shape[1], :])
    for h in range(heads):
        bias[h] = skew(base[h : h + 1, :])


def normalize(x_ref, gain, normed):
    for a in range(x_ref.shape[0] // tile):
        rows = slice(a * tile, (a + 1) * tile)
        v = x_ref[rows, :].astype(f32)
        normed[rows, :] = (v * rms_scale(v) * gain).astype(bf16)


chunk = 32


def head_groups(heads, size):
    per = tile // size
    out = []
    for first in range(0, heads, per):
        members = range(first, min(heads, first + per))
        lanes = slice(first * size, (members[-1] + 1) * size)
        out.append((lanes, [(h, (h - first) * size) for h in members]))
    return out


def only(v, lane, size):
    if v.shape[1] == size:
        return v
    at = lax.broadcasted_iota(jnp.int32, v.shape, 1)
    return jnp.where((at >= lane) & (at < lane + size), v, jnp.zeros_like(v))


def merge(parts, size):
    out = parts[0]
    at = lax.broadcasted_iota(jnp.int32, out.shape, 1)
    for i, part in enumerate(parts[1:]):
        out = jnp.where(at >= (i + 1) * size, part, out)
    return out


def project_heads(normed_ref, w, parts):
    rows = parts[0].shape[1]
    for i, part in enumerate(parts):
        part[...] = dot(
            normed_ref[...], w[i * rows : (i + 1) * rows, :], ((1,), (1,))
        ).astype(bf16)


def softmax_chunks(length):
    for r in range(0, length, chunk):
        at = length - tile - r // tile * tile
        yield slice(r, r + chunk), slice(r % tile, r % tile + chunk), slice(at, at + length)


def attend_kernel(
    first, heads, size, sc, x_ref, seg_ref, pad_ref, segc_ref, gain_ref, w_ref, hot_ref,
    out_ref, normed, query, keys, values, mask, bias, logits, probs, inverse,
):
    length = x_ref.shape[0]
    wide = heads * size
    buckets = 32
    row = lax.rem(sc[16] + first + pl.program_id(0), seg_ref.shape[0])
    normalize(x_ref, gain_ref[...], normed)
    project_heads(normed, w_ref, (query, keys, values))
    fill_mask(mask, seg_ref[...], pad_ref[...], segc_ref[...], row)

    @pl.when(pl.program_id(0) == 0)
    def _():
        fill_bias(bias, w_ref[3 * wide : 3 * wide + 16, :tile][:, :buckets], hot_ref, heads)

    for lanes, members in head_groups(heads, size):
        parts = []
        for i, (h, lane) in enumerate(members):
            logits[i % 2] = dot(only(query[:, lanes], lane, size), keys[:, lanes], ((1,), (1,)))
            for rows, inner, at in softmax_chunks(length):
                v = logits[i % 2, rows, :] + bias[h, inner, at] + mask[rows, :]
                e = jnp.exp(v - jnp.max(v, axis=1, keepdims=True))
                total = jnp.sum(e, axis=1, keepdims=True)
                inverse[rows, :] = jnp.broadcast_to(1.0 / total, (chunk, tile))
                probs[i % 2, rows, :] = e.astype(bf16)
            part = dot(probs[i % 2], values[:, lanes])
            parts.append(part * inverse[:, : part.shape[1]])
        out_ref[0, :length, lanes] = merge(parts, size).astype(bf16)
    out_ref[0, length:, :] = w_ref[3 * wide : 3 * wide + 16, :wide]


def attend(first, offs, tokens, segs, pads, seg_cols, gain, w_qkv, hot, heads, size, after=()):
    rows, length = segs.shape
    d = tokens.shape[1]
    wide = heads * size
    args = [tokens, segs, pads, seg_cols, gain, w_qkv, hot]
    specs = [pl.BlockSpec((length, d), lambda i, sc: (lax.rem(sc[16] + first + i, rows), 0))]
    return launch(
        functools.partial(attend_kernel, first, heads, size), "attend", args,
        specs + [whole(v.shape) for v in args[1:]],
        [pl.BlockSpec((1, length + 16, wide), lambda i, sc: (i, 0, 0))],
        like(bf16, (rows, length + 16, wide)),
        grid=(rows,), offs=offs,
        scratch=[
            pltpu.VMEM((length, d), bf16),
            pltpu.VMEM((length, wide), bf16),
            pltpu.VMEM((length, wide), bf16),
            pltpu.VMEM((length, wide), bf16),
            pltpu.VMEM((length, length), f32),
            pltpu.VMEM((heads, tile, span), f32),
            pltpu.VMEM((2, length, length), f32),
            pltpu.VMEM((2, length, length), bf16),
            pltpu.VMEM((length, tile), f32),
        ],
        cost=cost(
            rows * (6 * length * d * wide + 4 * wide * length * length), 4,
            rows * heads * length * length,
        ),
        after=after,
    )


def high_low(v):
    high = v.astype(bf16)
    return high, (v - high.astype(f32)).astype(bf16)


def attend_back_slot(
    heads, size, mixed_ref, gm_ref, hot_ref, w, left_ref, table_out, acc,
    normed, query, keys, values, mask, bias, logits, gprobs, probs, dlog, skewed, diag,
):
    length = normed.shape[0]
    wide = heads * size
    fill_bias(bias, mixed_ref[length:, :tile][:, :32], hot_ref, heads)
    project_heads(normed, w, (query, keys, values))
    for lanes, members in head_groups(heads, size):
        q, k, v = query[:, lanes], keys[:, lanes], values[:, lanes]
        grad = gm_ref[:, lanes]
        results = []
        for h, lane in members:
            logits[...] = dot(only(q, lane, size), k, ((1,), (1,)))
            gprobs[...] = dot(only(grad, lane, size), v, ((1,), (1,)))
            skewed[...] = jnp.zeros_like(skewed)
            for rows, inner, at in softmax_chunks(length):
                t = logits[rows, :] + bias[h, inner, at] + mask[rows, :]
                e = jnp.exp(t - jnp.max(t, axis=1, keepdims=True))
                p = e * (1.0 / jnp.sum(e, axis=1, keepdims=True))
                probs[rows, :] = p.astype(bf16)
                gp = gprobs[rows, :]
                gl = p * (gp - jnp.sum(gp * p, axis=1, keepdims=True))
                dlog[rows, :] = gl.astype(bf16)
                skewed[inner, at] += gl
            diag[h : h + 1, :] = unskew(skewed[...])
            results.append(
                (
                    dot(dlog[...], k),
                    dot(dlog[...], q, ((0,), (0,))),
                    dot(probs[...], grad, ((0,), (0,))),
                )
            )
        for part in range(3):
            merged = merge([r[part] for r in results], size)
            left_ref[part, :, lanes] = merged.astype(bf16)
    left_ref[3] = mixed_ref[:length, :]
    high, low = high_low(diag[...])
    table = dot(high, hot_ref[...], ((1,), (1,))) + dot(low, hot_ref[...], ((1,), (1,)))
    table_out[...] = table
    value = sum(
        dot(left_ref[part], w[part * wide : (part + 1) * wide, :]) for part in range(3)
    )
    acc[...] += value


def attend_back_kernel(
    first, count, last, heads, size, sc, x_ref, seg_ref, pad_ref, segc_ref, gain_ref, hot_ref,
    gm_ref, *refs,
):
    mixed_refs, refs = refs[:count], list(refs[count:])
    acc_in = refs.pop(0) if first else None
    if last:
        gha_ref, gat_ref, fin_ref, mid_ref, score_ref = refs[:5]
        refs = refs[5:]
        tables = [refs.pop(0)] if first else []
    w_ref = refs[0]
    refs = refs[1 + (1 if first else 0) :]
    left_ref, table_out = refs[:2]
    if last:
        dx_ref, both_ref, small_ref, acc = refs[2:6]
        refs = refs[6:]
    else:
        acc, refs = refs[2], refs[3:]
    (
        w, sems, normed, query, keys, values, mask, bias, logits, gprobs, probs, dlog, skewed, diag,
    ) = refs
    length, d = x_ref.shape
    wide = heads * size
    row = sc[16]
    gain = gain_ref[...]
    blocks = length // tile
    copies = [
        gathered_copies(w_ref, w.at[i], sems.at[i], lax.rem(row + 4 - first - i, 4))
        for i in range(count)
    ]
    for copy in sum(copies, []):
        copy.start()
    normalize(x_ref, gain, normed)
    fill_mask(mask, seg_ref[...], pad_ref[...], segc_ref[...], row)
    diag[...] = jnp.zeros_like(diag)
    if acc_in is None:
        acc[...] = jnp.zeros_like(acc)
    else:
        acc[...] = acc_in[...]
    for i in range(count):
        for copy in copies[i]:
            copy.wait()
        attend_back_slot(
            heads, size, mixed_refs[i], gm_ref.at[i], hot_ref, w.at[i], left_ref.at[i],
            table_out.at[8 * i : 8 * i + 8], acc,
            normed, query, keys, values, mask, bias, logits, gprobs, probs, dlog, skewed, diag,
        )
    if not last:
        return
    total = jnp.zeros((1, d), f32)
    for a in range(blocks):
        rows = slice(a * tile, (a + 1) * tile)
        back, part = rms_back(x_ref[rows, :].astype(f32), gain, acc[rows, :])
        dx_ref[rows, :] = (gha_ref[rows, :] + back).astype(bf16)
        total = total + part
    both_ref[0] = normed[...]
    both_ref[1] = gat_ref[...]
    dx_ref[length:, :] = jnp.zeros((dx_ref.shape[0] - length, d), bf16)
    n = score_ref.shape[0] // 16
    cols = score_ref.shape[1]
    high, low = high_low(score_ref[...])
    for i in range(n):
        rows = slice(16 * i, 16 * i + 16)
        dx_ref[length : length + 16, 2 * i * tile : 2 * i * tile + cols] = high[rows]
        dx_ref[length : length + 16, (2 * i + 1) * tile : (2 * i + 1) * tile + cols] = low[rows]
    line = lax.broadcasted_iota(jnp.int32, (8, d), 0)
    gains = jnp.where(
        line == 0, total, jnp.where(line == 1, fin_ref[...], jnp.where(line == 2, mid_ref[...], 0.0))
    )
    line = lax.broadcasted_iota(jnp.int32, (8, tile), 0)
    column = lax.broadcasted_iota(jnp.int32, (8, tile), 1)

    def turned(value, at):
        place = jnp.where(column == line + at, 1.0, 0.0).astype(bf16)
        high, low = high_low(value)
        return dot(high, place, ((0,), (0,))) + dot(low, place, ((0,), (0,)))

    gains = turned(gains, 0)
    tables = [t[8 * i : 8 * i + 8] for t in tables + [table_out] for i in range(t.shape[0] // 8)]
    for k, value in enumerate(tables):
        small_ref[k] = gains.astype(bf16)
        small_ref[k, 0:tile, :] = (gains[0:tile] + turned(value, tile // 2)).astype(bf16)


def attend_back(
    first, count, common, grad_mixed, mixed, acc, left, finish, weights, heads, size, after=()
):
    offs, *shared = common
    rows, length = shared[1].shape
    d = shared[0].shape[1]
    slots = grad_mixed.shape[0]
    wide = heads * size
    last = first + count == slots
    mixed = mixed[first : first + count]
    args = [*shared, grad_mixed, *mixed]
    specs = [pl.BlockSpec((length, d), lambda i, sc: (sc[16], 0))]
    specs += [whole(v.shape) for v in shared[1:]]
    specs.append(pl.BlockSpec((count, length, wide), lambda i, sc: (first // count, 0, 0)))
    specs += [whole(m.shape) for m in mixed]
    if first:
        args.append(acc)
        specs.append(whole(acc.shape))
    if last:
        args += finish
        specs += [whole(v.shape) for v in finish]
    args += [weights] + ([left] if first else [])
    specs += [ANY] * (2 if first else 1)
    out_specs = [
        pl.BlockSpec((count, 4, length, wide), lambda i, sc: (first // count, 0, 0, 0)),
        whole((8 * count, tile)),
    ]
    out_shape = like(bf16, (slots, 4, length, wide)) + like(f32, (8 * count, tile))
    scratch = []
    if last:
        shapes = ((length + 16, d), (2, length, d), (slots, d, tile))
        out_specs += [whole(shape) for shape in shapes]
        out_shape += like(bf16, *shapes)
        scratch = [pltpu.VMEM((length, d), f32)]
    else:
        out_specs.append(whole((length, d)))
        out_shape += like(f32, (length, d))
    return launch(
        functools.partial(attend_back_kernel, first, count, last, heads, size),
        f"attend_back{first}",
        args, specs, out_specs, out_shape, offs=offs,
        scratch=scratch
        + [
            pltpu.VMEM((count, 8 * weights.shape[4], d), bf16),
            pltpu.SemaphoreType.DMA((count, 8)),
            pltpu.VMEM((length, d), bf16),
            pltpu.VMEM((length, wide), bf16),
            pltpu.VMEM((length, wide), bf16),
            pltpu.VMEM((length, wide), bf16),
            pltpu.VMEM((length, length), f32),
            pltpu.VMEM((heads, tile, span), f32),
            pltpu.VMEM((length, length), f32),
            pltpu.VMEM((length, length), f32),
            pltpu.VMEM((length, length), bf16),
            pltpu.VMEM((length, length), bf16),
            pltpu.VMEM((tile, span), f32),
            pltpu.VMEM((8, span), f32),
        ],
        cost=cost(
            count * (12 * length * d * wide + 14 * wide * length * length), 16,
            count * heads * length * length,
        ),
        after=after, alias=len(args) - 1 if first else None, mib=32,
    )


def gate_up(normed_ref, w, act_ref, dact_ref, inner_ref):
    hidden = act_ref.shape[2]
    for n in range(hidden // 256):
        cols = slice(n * 256, (n + 1) * 256)
        normed = normed_ref[...]
        gate = dot(normed, w[:, cols])
        up = dot(normed, w[:, hidden + n * 256 : hidden + (n + 1) * 256])
        t = jnp.tanh(gelu_c * (gate + 0.044715 * gate * gate * gate))
        half = 0.5 * (1.0 + t)
        act = gate * half
        slope = half + 0.5 * gate * (1.0 - t * t) * (
            gelu_c * (1.0 + 3 * 0.044715 * gate * gate)
        )
        act_ref[0, :, cols] = act.astype(bf16)
        dact_ref[0, :, cols] = (up * slope).astype(bf16)
        inner_ref[0, :, cols] = (act * up).astype(bf16)


def forward_kernel(
    sc, x_ref, gain_ref, gain_l_ref, wp_ref, padc_ref, query_ref, cot_ref, top_ref, *refs
):
    slots = 4
    mixed, own, arrays = refs[:slots], refs[slots : slots + 4], refs[slots + 4 : slots + 12]
    hid_ref, normed_ref, act_ref, dact_ref, inner_ref = refs[slots + 12 : slots + 17]
    score_ref, nfin, ge, total_ref, gft_ref, ghf_ref = refs[slots + 17 : slots + 23]
    w, wd, wo, w_sems, d_sems, o_sems, acc, embed, unit = refs[slots + 23 :]
    length, d = x_ref.shape
    hidden = act_ref.shape[2]
    step = pl.program_id(0)
    blocks = length // tile
    w_copies = chunk_copies(sc, zip(own, (0, hidden)), arrays, w, w_sems)
    d_copies = chunk_copies(sc, [(own[2], 0)], arrays, wd, d_sems, 2 * hidden)
    o_copies = chunk_copies(sc, [(own[3], 0)], arrays, wo, o_sems, 3 * hidden)

    @pl.when(step == 0)
    def _():
        for copy in o_copies + w_copies + d_copies:
            copy.start()
        for copy in o_copies:
            copy.wait()
        gain = gain_ref[...]
        for a in range(blocks):
            rows = slice(a * tile, (a + 1) * tile)
            h = x_ref[rows, :].astype(f32)
            for k in range(slots):
                h = h + dot(mixed[k][rows, :], wo[k], ((1,), (1,)))
            hid_ref[rows, :] = h
            acc[rows, :] = h
            normed_ref[rows, :] = (h * rms_scale(h) * gain).astype(bf16)
        for copy in w_copies[:2] + d_copies[:1]:
            copy.wait()

    @pl.when(step == 1)
    def _():
        for copy in w_copies[2:] + d_copies[1:]:
            copy.wait()

    gate_up(normed_ref, w.at[step], act_ref, dact_ref, inner_ref)
    acc[...] += dot(inner_ref[0], wd[step])

    @pl.when(step == slots - 1)
    def _():
        lane = lax.broadcasted_iota(jnp.int32, padc_ref.shape, 1)
        pad = jnp.sum(jnp.where(lane == sc[16], padc_ref[...], 0.0), axis=1, keepdims=True)
        gain = gain_l_ref[...]
        for a in range(blocks):
            rows = slice(a * tile, (a + 1) * tile)
            h = acc[rows, :]
            n = (h * rms_scale(h) * gain).astype(bf16)
            nfin[rows, :] = n
            e = dot(n, wp_ref[...])
            embed[rows, :] = e
            inverse = lax.rsqrt(jnp.sum(e * e, axis=1, keepdims=True) + eps)
            unit[rows, :] = (e * inverse * pad[rows]).astype(bf16)
        query = query_ref[0]
        cot = cot_ref[0]
        top = top_ref[0]
        scored = dot(query, unit[...], ((1,), (1,)))
        place = lax.broadcasted_iota(jnp.int32, scored.shape, 1)
        out_lane = lax.broadcasted_iota(jnp.int32, cot.shape, 1)
        chosen = jnp.zeros_like(cot)
        weight = jnp.zeros_like(scored)
        for j in range(top.shape[1]):
            here = place == top[:, j : j + 1]
            mine = jnp.sum(jnp.where(here, scored, 0.0), axis=1, keepdims=True)
            chosen = jnp.where(out_lane == j, mine, chosen)
            weight = weight + jnp.where(here, cot[:, j : j + 1], 0.0)
        score_ref[...] = chosen
        high, low = high_low(weight)
        gunit = dot(high, query, ((0,), (0,))) + dot(low, query, ((0,), (0,)))
        total = jnp.zeros((1, d), f32)
        for a in range(blocks):
            rows = slice(a * tile, (a + 1) * tile)
            e = embed[rows, :]
            inverse = lax.rsqrt(jnp.sum(e * e, axis=1, keepdims=True) + eps)
            u = gunit[rows] * pad[rows]
            cube = (inverse * inverse * inverse) * jnp.sum(u * e, axis=1, keepdims=True)
            g = (inverse * u - e * cube).astype(bf16)
            ge[rows, :] = g
            back, part = rms_back(acc[rows, :], gain, dot(g, wp_ref[...], ((1,), (1,))))
            total = total + part
            ghf_ref[rows, :] = back
            gft_ref[rows, :] = back.astype(bf16)
        total_ref[...] = total


def forward(
    offs, tokens, gain, gain_l, w_proj, pad_cols, query, cot, top, mixed, own, arrays, length
):
    d = tokens.shape[1]
    slots = len(mixed)
    hidden = own[0].shape[1]
    wide = own[3].shape[1]
    e = w_proj.shape[1]
    three = (slots, length, hidden)
    score, low, embed, total = cot.shape[1:], (length, d), (length, e), (1, d)
    per_slot = pl.BlockSpec((1, length, hidden), lambda i, sc: (i, 0, 0))

    def row_block(v):
        return pl.BlockSpec((1,) + v.shape[1:], lambda i, sc: (sc[16], 0, 0))

    return launch(
        forward_kernel, "forward",
        [tokens, gain, gain_l, w_proj, pad_cols, query, cot, top, *mixed, *own, *arrays],
        [pl.BlockSpec((length, d), lambda i, sc: (sc[16], 0))]
        + [whole(v.shape) for v in (gain, gain_l, w_proj, pad_cols)]
        + [row_block(v) for v in (query, cot, top)]
        + [whole(m.shape) for m in mixed]
        + [ANY] * 12,
        [whole(low), whole(low)] + [per_slot] * 3
        + [whole(v) for v in (score, low, embed, total, low, low)],
        like(f32, low) + like(bf16, low, three, three, three) + like(f32, score)
        + like(bf16, low, embed) + like(f32, total) + like(bf16, low) + like(f32, low),
        grid=(slots,), offs=offs,
        scratch=[
            pltpu.VMEM((slots, d, 2 * hidden), bf16),
            pltpu.VMEM((slots, hidden, d), bf16),
            pltpu.VMEM((slots, d, wide), bf16),
            pltpu.SemaphoreType.DMA((copies_per_chunk,)),
            pltpu.SemaphoreType.DMA((copies_per_chunk,)),
            pltpu.SemaphoreType.DMA((copies_per_chunk,)),
            pltpu.VMEM((length, d), f32),
            pltpu.VMEM((length, e), f32),
            pltpu.VMEM((length, e), bf16),
        ],
        cost=cost(2 * length * d * (d + 3 * slots * hidden), 24, slots * length * hidden),
        mib=58,
    )


def ffn_back_kernel(sc, hid_ref, gft_ref, ghf_ref, act_ref, dact_ref, gain_ref, *refs):
    slots = 4
    own, arrays, refs = refs[:4], refs[4:12], refs[12:]
    gg_ref, gu_ref, gha_ref, gat_ref, gm_ref, total_ref, w, wd, wo, w_sems, d_sems, acc = refs
    length, d = hid_ref.shape
    hidden = wd.shape[1]
    step = pl.program_id(0)
    w_copies = chunk_copies(sc, zip(own, (0, hidden)), arrays, w, w_sems.at[0])
    w_copies += chunk_copies(sc, [(own[3], 0)], arrays, wo, w_sems.at[1], 3 * hidden)
    d_copies = chunk_copies(sc, [(own[2], 0)], arrays, wd, d_sems, 2 * hidden)
    blocks = length // tile

    @pl.when(step == 0)
    def _():
        for copy in d_copies[:1] + w_copies[:2] + d_copies[1:] + w_copies[2:]:
            copy.start()
        acc[...] = jnp.zeros_like(acc)
        for copy in d_copies[:1] + w_copies[:2]:
            copy.wait()

    @pl.when(step == 1)
    def _():
        for copy in d_copies[1:] + w_copies[2:]:
            copy.wait()

    def part(n, carry):
        cols = pl.ds(pl.multiple_of(n * 256, 256), 256)
        gi = dot(gft_ref[...], wd[step, cols, :], ((1,), (1,)))
        gg_ref[0, :, cols] = (gi * dact_ref[0, :, cols].astype(f32)).astype(bf16)
        gu_ref[0, :, cols] = (gi * act_ref[0, :, cols].astype(f32)).astype(bf16)
        return carry

    lax.fori_loop(0, hidden // 256, part, 0)
    acc[...] += dot(gg_ref[0], w[step, :, :hidden], ((1,), (1,))) + dot(
        gu_ref[0], w[step, :, hidden : 2 * hidden], ((1,), (1,))
    )

    @pl.when(step == slots - 1)
    def _():
        gain = gain_ref[...]
        total = jnp.zeros((1, d), f32)
        for a in range(blocks):
            rows = slice(a * tile, (a + 1) * tile)
            back, part = rms_back(hid_ref[rows, :], gain, acc[rows, :])
            total = total + part
            g = ghf_ref[rows, :] + back
            gha_ref[rows, :] = g
            g = g.astype(bf16)
            gat_ref[rows, :] = g
            for k in range(slots):
                gm_ref[k, rows, :] = dot(g, wo[k]).astype(bf16)
        total_ref[...] = total


def ffn_back(offs, hid, gft, ghf, act, dact, gain, own, arrays, after=()):
    length, d = hid.shape
    slots, _, hidden = act.shape
    wide = own[3].shape[1]
    mixed = (slots, length, wide)
    block = pl.BlockSpec((1, length, hidden), lambda i, sc: (i, 0, 0))
    return launch(
        ffn_back_kernel, "ffn_back",
        [hid, gft, ghf, act, dact, gain, *own, *arrays],
        [whole(v.shape) for v in (hid, gft, ghf)] + [block] * 2 + [whole(gain.shape)] + [ANY] * 12,
        [block, block] + [whole(v) for v in (hid.shape, hid.shape, mixed, (1, d))],
        like(bf16, act.shape, act.shape) + like(f32, hid.shape) + like(bf16, hid.shape, mixed)
        + like(f32, (1, d)),
        grid=(slots,), offs=offs,
        scratch=[
            pltpu.VMEM((slots, d, 2 * hidden), bf16),
            pltpu.VMEM((slots, hidden, d), bf16),
            pltpu.VMEM((slots, d, wide), bf16),
            pltpu.SemaphoreType.DMA((2, copies_per_chunk)),
            pltpu.SemaphoreType.DMA((copies_per_chunk,)),
            pltpu.VMEM((length, d), f32),
        ],
        cost=cost(2 * length * d * (3 * slots * hidden + d), 24),
        after=after, mib=42,
    )


def keep_parts(sc, out, refs):
    send_a, keep_a, send_b, keep_b = refs
    half = send_a.shape[2]
    x, y = sc[18], sc[19]

    def rows(y, x, extra):
        at = pl.multiple_of((2 * y + x) * (2 * half) + extra, 16)
        return out[pl.ds(at, half), :]

    for other in range(2):
        send_a[0, other] = rows(other, 1 - x, 0)
        keep_a[0, other] = rows(other, x, 0)
        send_b[0, other] = rows(1 - y, other, half)
        keep_b[0, other] = rows(y, other, half)


def parts_of(slots, rows, width):
    part = (1, 2, rows // 8, width)
    spec = pl.BlockSpec(part, lambda i, sc: (i, 0, 0, 0))
    return [spec] * 4, [jax.ShapeDtypeStruct((slots,) + part[1:], bf16)] * 4


def product_kernel(lefts, pairs, keep, sc, *refs):
    left_refs, right_refs = refs[:lefts], refs[lefts : lefts + len(pairs)]
    refs = refs[lefts + len(pairs) :]
    out = refs[-1] if keep else refs[-1].at[0]
    at = 0
    for right_ref, which in zip(right_refs, pairs):
        right = right_ref[...]
        left = left_refs[which][...]
        left, right = (v.reshape(v.shape[-2:]) for v in (left, right))
        cols = slice(at, at + right.shape[1])
        value = dot(left, right, ((0,), (0,)))
        if keep:
            value = value + refs[0][0, :, cols].astype(f32)
        out[:, cols] = value.astype(bf16)
        at += right.shape[1]
    if keep:
        keep_parts(sc, out, refs[-5:-1])


def products(offs, lefts, rights, slots, got=None, after=(), mib=16):
    keep = got is not None
    length, half = lefts[0].shape[-2], lefts[0].shape[-1] // 2
    width = sum(right.shape[-1] for right, _ in rights)

    def which(sc):
        return sc[17] if keep else 1 - sc[17]

    specs = []
    for left in lefts:
        if left.ndim == 3:
            specs.append(pl.BlockSpec((1, length, half), lambda i, sc: (i, 0, which(sc))))
        else:
            specs.append(pl.BlockSpec((length, half), lambda i, sc: (0, which(sc))))
    for right, _ in rights:
        if right.ndim == 3:
            specs.append(pl.BlockSpec((1,) + right.shape[1:], lambda i, sc: (i, 0, 0)))
        else:
            specs.append(whole(right.shape))
    args = list(lefts) + [right for right, _ in rights]
    block = pl.BlockSpec((1, half, width), lambda i, sc: (i, 0, 0))
    out_specs, out_shape, scratch = [block], like(bf16, (slots, half, width)), []
    if keep:
        specs.append(block)
        args.append(got)
        out_specs, out_shape = parts_of(slots, half, width)
        scratch = [pltpu.VMEM((half, width), bf16)]
    return launch(
        functools.partial(product_kernel, len(lefts), [i for _, i in rights], keep),
        "products_keep" if keep else "products_send",
        args, specs, out_specs, out_shape, grid=(slots,), offs=offs, scratch=scratch, after=after,
        mib=mib,
    )


def attn_product_kernel(keep, sc, la, lb, ra, rb, small, *refs):
    out = refs[-1] if keep else refs[-1].at[0]
    quarter, d = la.shape[3], ra.shape[2]
    for left, right, at in ((la, ra, 0), (lb, rb, quarter)):
        value = dot(left[0, 0], right[0], ((0,), (0,)))
        if keep:
            value = value + refs[0][0, at : at + quarter, :d].astype(f32)
        out[at : at + quarter, :d] = value.astype(bf16)
    value = small[0]
    if keep:
        value = add(value, refs[0][0, :, d:])
    out[:, d:] = value
    if keep:
        keep_parts(sc, out, refs[1:5])


def attn_products(offs, left, both, small, got=None, after=()):
    keep = got is not None
    slots, _, length, quarter = left.shape
    d = both.shape[2]
    width = d + small.shape[2]
    half = 2 * quarter

    def which(sc):
        return sc[17] if keep else 1 - sc[17]

    block = pl.BlockSpec((1, half, width), lambda i, sc: (i, 0, 0))
    specs = [
        pl.BlockSpec((1, 1, length, quarter), lambda i, sc: (i, 2 * which(sc), 0, 0)),
        pl.BlockSpec((1, 1, length, quarter), lambda i, sc: (i, 2 * which(sc) + 1, 0, 0)),
        pl.BlockSpec((1, length, d), lambda i, sc: (0, 0, 0)),
        pl.BlockSpec((1, length, d), lambda i, sc: (which(sc), 0, 0)),
        pl.BlockSpec((1, half, small.shape[2]), lambda i, sc: (i, which(sc), 0)),
    ]
    args = [left, left, both, both, small]
    out_specs, out_shape, scratch = [block], like(bf16, (slots, half, width)), []
    if keep:
        specs.append(block)
        args.append(got)
        out_specs, out_shape = parts_of(slots, half, width)
        scratch = [pltpu.VMEM((half, width), bf16)]
    return launch(
        functools.partial(attn_product_kernel, keep), "attn_keep" if keep else "attn_send",
        args, specs, out_specs, out_shape, grid=(slots,), offs=offs, scratch=scratch, after=after,
        mib=16,
    )


def add(a, b):
    return (a.astype(f32) + b.astype(f32)).astype(bf16)


def second_kernel(sc, ka, ra, kb, rb, send_a, keep_a, send_b, keep_b):
    x, y = sc[18], sc[19]
    send_a[0] = add(ka[0, 1 - y], ra[0, 1 - y])
    keep_a[0] = add(ka[0, y], ra[0, y])
    send_b[0] = add(kb[0, 1 - x], rb[0, 1 - x])
    keep_b[0] = add(kb[0, x], rb[0, x])


def second_sums(offs, *arrays, after=()):
    slots, _, half, width = arrays[0].shape
    into = pl.BlockSpec((1, 2, half, width), lambda i, sc: (i, 0, 0, 0))
    out = pl.BlockSpec((1, half, width), lambda i, sc: (i, 0, 0))
    return launch(
        second_kernel, "second_sums", arrays, [into] * 4, [out] * 4,
        like(bf16, *[(slots, half, width)] * 4), grid=(slots,), offs=offs, after=after,
    )


def third_kernel(ka, ra, kb, rb, *outs):
    half = ka.shape[1]
    for k, out in enumerate(outs):
        out[:half, :] = add(ka[k], ra[k])
        out[half:, :] = add(kb[k], rb[k])


def third_sums(*arrays, after=()):
    slots, half, width = arrays[0].shape
    shape = (2 * half, width)
    return launch(
        third_kernel, "third_sums", arrays, [whole(arrays[0].shape)] * 4, [whole(shape)] * slots,
        like(bf16, *[shape] * slots), after=after,
    )


def third_stacked_kernel(sc, ka, ra, kb, rb, out):
    n, half, _ = ka.shape
    for k in range(n):
        to = lax.rem(sc[16] + n - k, n)
        out[to, :half, :] = add(ka[k], ra[k])
        out[to, half:, :] = add(kb[k], rb[k])


def third_stacked(offs, *arrays, after=()):
    slots, half, width = arrays[0].shape
    shape = (slots, 2 * half, width)
    (out,), token = launch(
        third_stacked_kernel, "third_stacked", arrays, [whole(arrays[0].shape)] * 4,
        [whole(shape)], like(bf16, shape), offs=offs, after=after,
    )
    return out, token


def last_kernel(*refs):
    t = [ref[...].astype(f32) for ref in refs[:4]]
    refs[4][...] = ((t[0] + t[2]) + (t[1] + t[3])).astype(refs[4].dtype)


def last_sum(arrays, dtype, after=()):
    shape = arrays[0].shape
    return launch(
        last_kernel, "last_sum", arrays, [whole(shape)] * 4, [whole(shape)], like(dtype, shape),
        after=after,
    )


def stack_kernel(a, xa, b, yb, sa, sb):
    sa[0], sa[1], sb[0], sb[1] = a[...], xa[...], b[...], yb[...]


def stack_pairs(a, xa, b, yb, after):
    out = (2,) + a.shape
    return launch(
        stack_kernel, "stack_pairs", [a, xa, b, yb], [whole(a.shape)] * 4, [whole(out)] * 2,
        like(bf16, out, out), after=after,
    )


class Reduce:
    def __init__(self, place, offs, kept):
        self.place, self.offs, self.kept = place, offs, kept

    def first(self, after=()):
        send_a, keep_a, send_b, keep_b = self.kept
        ra, rb = self.place.swap(send_a, XBIT), self.place.swap(send_b, YBIT)
        self.kept, token = second_sums(self.offs, keep_a, ra, keep_b, rb, after=after)
        return token

    def second(self, after=()):
        send_a, keep_a, send_b, keep_b = self.kept
        ra, rb = self.place.swap(send_a, YBIT), self.place.swap(send_b, XBIT)
        self.kept, token = third_sums(keep_a, ra, keep_b, rb, after=after)
        return token

    def second_and_third(self, after=()):
        send_a, keep_a, send_b, keep_b = self.kept
        ra, rb = self.place.swap(send_a, YBIT), self.place.swap(send_b, XBIT)
        v, token = third_stacked(self.offs, keep_a, ra, keep_b, rb, after=after)
        total = lax.psum_scatter(v, "mp", scatter_dimension=0, tiled=True)
        if self.place.n_out > 1:
            total = lax.psum(total.astype(f32), "out").astype(bf16)
        self.total = total.reshape(v.shape[1:])
        return token

    def third(self, after=()):
        p = self.place
        t = [self.kept[0]] + [p.shift(self.kept[k], -k) for k in range(1, p.n_mp)]
        if p.n_out > 1:
            (total,), token = last_sum(t, f32, after)
            self.total = lax.psum(total, "out").astype(bf16)
        else:
            (self.total,), token = last_sum(t, bf16, after)
        return token


def open_kernel(v_ref, *outs):
    rows = v_ref.shape[3]
    for at, (c, y, x) in enumerate(np.ndindex(2, 2, 2)):
        left = 0
        for out in outs:
            value = v_ref[y, x, c, :, left : left + out.shape[1]]
            out[at * rows : (at + 1) * rows, :] = value.astype(f32)
            left += out.shape[1]


def beside_kernel(a, b, out):
    out[:, : a.shape[1]] = a[...]
    out[:, a.shape[1] :] = b[...]


def gathered(a, b, cuts, start_after, after):
    rows, width = a.shape[0], a.shape[1] + b.shape[1]
    (v,), _ = launch(
        beside_kernel, "beside", [a, b], [whole(a.shape), whole(b.shape)],
        [whole((rows, width))], like(bf16, (rows, width)), after=start_after,
    )
    v = lax.all_gather(v, group, tiled=False).reshape(2, 2, 2, rows, width)
    shapes = [(8 * rows, cut) for cut in cuts]
    return launch(
        open_kernel, "open", [v], [whole(v.shape)], [whole(shape) for shape in shapes],
        like(f32, *shapes), after=after, mib=58,
    )


def unpack_kernel(offs, *refs):
    arrays, outs, small, full = refs[:8], refs[8:-2], refs[-2], refs[-1]
    for at in range(16):
        value = arrays[at // 2][at % 2]
        rows = pl.ds(pl.multiple_of(offs[at], 16), value.shape[0])
        full[rows, :] = value.astype(f32)
    rows, d = outs[0].shape
    for i, out in enumerate(outs):
        out[...] = full[i * rows : (i + 1) * rows, :d]
    small[...] = full[:, d:]


def unpack(offs, arrays, count, small):
    half, width = arrays[0].shape[1:]
    rows, d = 16 * half, width - small
    shapes = [(rows // count, d)] * count + [(rows, small)]
    outs, _ = launch(
        unpack_kernel, "unpack", arrays, [whole(v.shape) for v in arrays],
        [whole(v) for v in shapes], like(f32, *shapes), offs=offs,
        scratch=[pltpu.VMEM((rows, width), f32)],
    )
    return outs


def local(
    tokens, segment_ids, pad_mask, top_index, query_emb, score_cot, gain_attn, w_query, w_key,
    w_value, w_out, rel_table, gain_ffn, w_gate, w_up, w_down, gain_final, w_proj,
):
    place = Place()
    slots = place.n_mp
    rows, length = segment_ids.shape
    d = tokens.shape[1]
    heads = rel_table.shape[1]
    size = w_query.shape[1] // heads
    wide = heads * size
    hot = jnp.asarray(bucket_hot(rel_table.shape[0], length), bf16)
    segs, pads = segment_ids.astype(f32), pad_mask.astype(f32)
    seg_cols, pad_cols = segs.T, pads.T
    gain_a, gain_f, gain_l = (
        g.astype(f32).reshape(1, d) for g in (gain_attn, gain_ffn, gain_final)
    )
    offs = place.offsets(d // 8)

    buckets = rel_table.shape[0]
    table = jnp.zeros((64, d), bf16).at[:heads, :buckets].set(rel_table.T)
    w_qkv = jnp.concatenate([w_query.T, w_key.T, w_value.T, table])
    w_out_t = w_out.T
    eighth = d // 8
    hidden = w_gate.shape[1]

    def piece(*arrays):
        parts = []
        for v in arrays:
            rows = v.shape[0] // 8
            parts.append(lax.dynamic_slice_in_dim(v, place.p * rows, rows, 0))
        return jnp.concatenate(parts, axis=1) if len(parts) > 1 else parts[0]

    common = (offs, tokens, segs, pads, seg_cols, gain_a)
    own = (w_gate, w_up, w_down, w_out_t)
    z1 = lax.all_gather(piece(*own), "mp")
    (attended,), done = attend(1, *common, w_qkv, hot, heads, size)
    mixed = [attended[slots - 1]] + [place.shift(attended[k - 1], k) for k in range(1, slots)]
    halved, _ = split(offs, z1, eighth, (done,))
    s1, _ = place.first_round(*halved, mixed[1:])
    arrays = place.second_round(*s1)
    (hid, normed_ffn, act, dact, inner, score, nfin, ge, gain_fin, gft, ghf), done = forward(
        offs, tokens, gain_f, gain_l, w_proj, pad_cols, query_emb, score_cot, top_index, mixed,
        own, arrays, length,
    )
    all_qkv = lax.all_gather(relay(piece(w_qkv), (done,)), group + ("mp",))
    all_qkv = all_qkv.reshape((2, 2, 2, slots) + all_qkv.shape[-2:])
    down_sides = ([inner, nfin], [(gft, 0), (ge, 1)])
    (send,), _ = products(offs, *down_sides, slots, mib=58)
    kept, kept_done = products(offs, *down_sides, slots, place.swap(send, CORE))
    down = Reduce(place, offs, kept)
    (gg, gu, gha, gat, gm, gain_mid), done = ffn_back(
        offs, hid, gft, ghf, act, dact, gain_f, own, arrays, (kept_done,)
    )
    gu_sides = ([normed_ffn], [(gg, 0), (gu, 0)])
    done = down.first((done,))
    (send,), done = products(offs, *gu_sides, slots, None, (done,))
    got = place.swap(send, CORE)
    done = down.second((done,))
    kept, done = products(offs, *gu_sides, slots, got, (done,))
    gate_up = Reduce(place, offs, kept)
    finish = [gha, gat, gain_fin, gain_mid, score]

    def back(first, acc, left, after):
        return attend_back(
            first, slots // 2, common + (hot,), gm, mixed, acc, left, finish, all_qkv, heads, size,
            after,
        )

    (left, tables, acc), done = back(0, None, None, (done,))
    finish.append(tables)
    done = down.third((done,))
    done = gate_up.first((done,))
    (left, _, dx, both, small), done = back(slots // 2, acc, left, (done,))
    right, left_ = place.both_ways(dx, dx)
    done = gate_up.second_and_third((done,))
    (send,), _ = attn_products(offs, left, both, small, None, (done,))
    kept, done = attn_products(offs, left, both, small, place.swap(send, CORE))
    attn = Reduce(place, offs, kept)
    (*so_far, right, left_), done = collect(1, slots, offs, right, left_, dx, None, (done,))
    right, left_ = place.both_ways(right, left_)
    done = start_after = attn.first((done,))
    done = attn.second((done,))
    (*so_far, right, left_), done = collect(2, slots, offs, right, left_, dx, so_far, (done,))
    right, left_ = place.both_ways(right, left_)
    (grad_down, grad_proj, grad_gate, grad_up), done = gathered(
        down.total, gate_up.total, (d, w_proj.shape[1], hidden, hidden), (start_after,),
        (done,),
    )
    done = attn.third((done,))
    (input_grad, packed), done = collect(3, slots, offs, right, left_, dx, so_far, (done,))
    last, _ = place.first_round(*halves(attn.total, 0), (done,))
    grad_q, grad_k, grad_v, grad_out, small = unpack(
        offs, place.second_round(*last), 4, small.shape[2]
    )

    input_grad = input_grad.reshape(rows * length, d)
    n, m = score.shape
    packed = packed.astype(f32).reshape(slots, 16, d // 128, 128)[:, :, : 2 * (n // 16), :m]
    packed = packed[:, :, 0::2] + packed[:, :, 1::2]
    scores = packed.transpose(0, 2, 1, 3).reshape(slots, n, m)
    return (
        scores,
        input_grad,
        small[:, 0],
        grad_q.T,
        grad_k.T,
        grad_v.T,
        grad_out,
        small[:buckets, 64 : 64 + heads],
        small[:, 2],
        grad_gate,
        grad_up,
        grad_down,
        small[:, 1],
        grad_proj,
    )


def solution(mesh):
    n_dp, n_mp = mesh.shape["dp"], mesh.shape["mp"]
    mesh = Mesh(mesh.devices.reshape(n_dp // 8, 2, 2, 2, n_mp), dp + ("mp",))
    return jax.shard_map(
        local,
        mesh=mesh,
        in_specs=(
            P(dp, None),
            P(dp, None),
            P(dp, None),
            P(dp, None, None),
            P(dp, None, None),
            P(dp, None, None),
            P(),
            P(None, "mp"),
            P(None, "mp"),
            P(None, "mp"),
            P("mp", None),
            P(None, "mp"),
            P(),
            P(None, "mp"),
            P(None, "mp"),
            P("mp", None),
            P(),
            P(),
        ),
        out_specs=(
            P(dp, None, None),
            P(dp, None),
            P(),
            P(None, "mp"),
            P(None, "mp"),
            P(None, "mp"),
            P("mp", None),
            P(None, "mp"),
            P(),
            P(None, "mp"),
            P(None, "mp"),
            P("mp", None),
            P(),
            P(),
        ),
        check_vma=False,
    )
```

```python
import functools
import math

import jax
import jax.numpy as jnp
import numpy as np
from jax import lax
from jax.experimental import pallas as pl
from jax.experimental.pallas import tpu as pltpu
from jax.sharding import Mesh
from jax.sharding import PartitionSpec as P

f32 = jnp.float32
bf16 = jnp.bfloat16
eps = 1e-06
masked_logit = -1e30
gelu_c = math.sqrt(2.0 / math.pi)
CORE, XBIT, YBIT = "core", "x", "y"
group = ("y", "x", "core")
dp = ("out",) + group
span = 1024
tile = 128


def bucket_hot(buckets, length):
    column = np.arange(span)
    base = length - tile
    offset = np.where(column < base + length, column - base, column - span - base)
    distance = np.abs(offset)
    far = 8 + sum((distance >= t).astype(np.int32) for t in (12, 16, 23, 32, 46, 64, 91))
    bucket = np.where(distance < 8, distance, far) + 16 * (offset > 0)
    hot = (bucket[None, :] == np.arange(tile)[:, None]) & (np.arange(tile)[:, None] < buckets)
    return hot.astype(np.float32)


def dot(a, b, dims=((1,), (0,))):
    return lax.dot_general(a, b, (dims, ((), ())), preferred_element_type=f32)


def rms_scale(v):
    return lax.rsqrt(jnp.mean(v * v, axis=-1, keepdims=True) + eps)


def rms_back(v, gain, grad):
    s = rms_scale(v)
    w = grad * gain
    value = s * w - v * ((s * s * s) * jnp.mean(w * v, axis=-1, keepdims=True))
    return value, jnp.sum(grad * v * s, axis=0, keepdims=True)


def whole(shape):
    return pl.BlockSpec(shape, lambda *_: (0,) * len(shape))


ANY = pl.BlockSpec(memory_space=pl.ANY)
token_shape = (8, 128)


def launch(
    kernel, name, args, in_specs, out_specs, out_shape, grid=(1,), offs=None, scratch=(),
    cost=None, after=(), alias=None, n_alias=1, mib=16,
):
    first = 0 if offs is None else 1
    n_in, n_out, n_after = first + len(args), len(out_shape), len(after)

    def body(*refs):
        ins, rest = refs[:n_in], refs[n_in + n_after :]
        outs, token, own = rest[:n_out], rest[n_out], rest[n_out + 1 :]
        token[...] = jnp.zeros(token_shape, f32)
        kernel(*ins, *outs, *own)

    specs = dict(
        grid=grid,
        in_specs=list(in_specs) + [ANY] * n_after,
        out_specs=list(out_specs) + [whole(token_shape)],
        scratch_shapes=list(scratch),
    )
    if offs is None:
        specs = dict(specs)
        scalars = []
    else:
        specs = dict(grid_spec=pltpu.PrefetchScalarGridSpec(num_scalar_prefetch=1, **specs))
        scalars = [offs]
    *outs, token = pl.pallas_call(
        body,
        out_shape=list(out_shape) + [jax.ShapeDtypeStruct(token_shape, f32)],
        input_output_aliases=(
            {} if alias is None else {alias + first + i: i for i in range(n_alias)}
        ),
        compiler_params=pltpu.CompilerParams(
            vmem_limit_bytes=mib << 20, dimension_semantics=("arbitrary",)
        ),
        cost_estimate=cost or cheap,
        name=name,
        **specs,
    )(*scalars, *args, *after)
    return outs, token


cheap = pl.CostEstimate(flops=1 << 20, bytes_accessed=1 << 16, transcendentals=0)


def cost(flops, mib, transcendentals=0):
    return pl.CostEstimate(
        flops=flops, bytes_accessed=mib << 20, transcendentals=transcendentals
    )


def like(dtype, *shapes):
    return [jax.ShapeDtypeStruct(shape, dtype) for shape in shapes]


class Place:
    def __init__(self):
        self.n_out, self.n_mp = lax.axis_size("out"), lax.axis_size("mp")
        self.c, self.x, self.y = (lax.axis_index(name) for name in ("core", "x", "y"))
        self.z = lax.axis_index("mp")
        self.p = self.c * 4 + self.y * 2 + self.x

    def swap(self, v, name):
        return lax.ppermute(v, name, [(0, 1), (1, 0)])

    def shift(self, v, k):
        n = self.n_mp
        return lax.ppermute(v, "mp", [(i, (i + k) % n) for i in range(n)])

    def offsets(self, rows):
        half = rows // 2
        out = []
        for flip in (0, 4):
            p = self.p ^ flip
            for other, extra in (
                (0, 0), (1, 0), (0, half), (2, half), (2, 0), (3, 0), (1, half), (3, half),
            ):
                out.append((p ^ other) * rows + extra)
        return jnp.stack(out + [self.z, self.c, self.x, self.y]).astype(jnp.int32)

    def both_ways(self, right, left):
        n = self.n_mp
        right = lax.ppermute(right, "mp", [(i, i + 1) for i in range(n - 1)])
        return right, lax.ppermute(left, "mp", [(i + 1, i) for i in range(n - 1)])

    def first_round(self, a, b, after=()):
        return stack_pairs(a, self.swap(a, XBIT), b, self.swap(b, YBIT), after)

    def second_round(self, sa, sb, after=()):
        ya, xb = self.swap(sa, YBIT), self.swap(sb, XBIT)
        if after:
            ya, xb = relay([ya, xb], after)
        near = [sa, sb, ya, xb]
        return near + [self.swap(t, CORE) for t in near]


def pick(v, axis, index):
    return lax.dynamic_index_in_dim(v, index, axis, keepdims=False)


def halves(v, axis):
    half = v.shape[axis] // 2
    return (
        lax.slice_in_dim(v, 0, half, axis=axis),
        lax.slice_in_dim(v, half, 2 * half, axis=axis),
    )


def chunk_copies(offs, own, arrays, dst, sems, first=0, slot=0):
    slots, rows, width = dst.shape
    half = rows // 16
    skip = 0 if slot else 1
    pairs = [
        (ref, dst.at[0, :, pl.ds(column, ref.shape[1])]) for ref, column in own
    ]
    for at in range(16):
        src = arrays[at // 2].at[at % 2, pl.ds(slot + skip - 1, slots - skip)]
        if src.shape[2] != width:
            src = src.at[:, :, pl.ds(first, width)]
        start = pl.multiple_of(offs[at], 16)
        pairs.append((src, dst.at[pl.ds(skip, slots - skip), pl.ds(start, half), :]))
    return [pltpu.make_async_copy(s, d, sems.at[i]) for i, (s, d) in enumerate(pairs)]


copies_per_chunk = 20


def gathered_copies(gathered, dst, sems, shard=None):
    full = gathered.shape[4]
    out = []
    for at, (c, y, x) in enumerate(np.ndindex(2, 2, 2)):
        rows = pl.ds(at * full, full)
        if shard is None:
            out.append((gathered.at[y, x, c], dst.at[:, rows, :]))
        else:
            out.append((gathered.at[y, x, c, shard], dst.at[rows, :]))
    return [pltpu.make_async_copy(s, d, sems.at[i]) for i, (s, d) in enumerate(out)]


def split_kernel(sc, v_ref, *refs):
    *others, a_ref, b_ref = refs
    half = a_ref.shape[1]
    n, _, width = v_ref.shape
    for k in range(1, n):
        at = lax.rem(sc[16] + n - k, n)
        a_ref[k - 1, :, :width] = v_ref[at, :half, :]
        b_ref[k - 1, :, :width] = v_ref[at, half:, :]
        a_ref[k - 1, :, width:] = others[k - 1][:half, :]
        b_ref[k - 1, :, width:] = others[k - 1][half:, :]


def split(offs, v, others, after=()):
    n, rows, width = v.shape
    out = (n - 1, rows // 2, width + others[0].shape[1])
    return launch(
        split_kernel, "split", [v, *others], [whole(x.shape) for x in (v, *others)],
        [whole(out)] * 2, like(bf16, out, out), offs=offs, after=after,
    )


def relay_kernel(*refs):
    half = len(refs) // 2
    for a, b in zip(refs[:half], refs[half:]):
        b[...] = a[...]


def relay(arrays, after):
    specs = [whole(a.shape) for a in arrays]
    return launch(
        relay_kernel, "relay", arrays, specs, specs,
        [jax.ShapeDtypeStruct(a.shape, a.dtype) for a in arrays], after=after,
    )[0]


def collect_kernel(step, n, sc, right, left, own, *refs):
    out, rest, *on = refs
    length = out.shape[1]
    side = pl.program_id(0)
    z = sc[16]

    @pl.when((side == 0) & (z >= step))
    def _():
        out[0] = right[:length, :].astype(f32)
        rest[0] = right[length:, :]

    @pl.when((side == 1) & (z + step < n))
    def _():
        out[0] = left[:length, :].astype(f32)
        rest[0] = left[length:, :]

    @pl.when(((side == 0) & (z < step)) | ((side == 1) & (z + step >= n)))
    def _():
        out[0] = own[:length, :].astype(f32)
        rest[0] = own[length:, :]

    @pl.when(side == 0)
    def _():
        for new, old in zip(on, (right, left)):
            new[...] = old[...]


def collect(step, n, offs, right, left, own, so_far, after):
    rows, d = own.shape
    length = rows // tile * tile

    def index(i, sc):
        z = sc[16]
        near, far = jnp.where(z >= step, z - step, z), jnp.where(z + step < n, z + step, z)
        return (jnp.where(i == 0, near, far), 0, 0)

    goes_on = step < n - 1
    kept = list(so_far or ())
    shapes = [(n, length, d), (n, rows - length, d)]
    out_shape = like(f32, shapes[0]) + like(bf16, shapes[1])
    out_specs = [pl.BlockSpec((1,) + shape[1:], index) for shape in shapes]
    if goes_on:
        out_shape += like(bf16, own.shape, own.shape)
        out_specs += [whole(own.shape)] * 2

    def kernel(sc, right, left, own, *refs):
        collect_kernel(step, n, sc, right, left, own, *refs[len(kept) :])

    return launch(
        kernel, f"collect{step}", [right, left, own, *kept],
        [whole(own.shape)] * 3 + [ANY] * len(kept), out_specs, out_shape, grid=(2,), offs=offs,
        after=after, alias=3 if kept else None, n_alias=2,
    )


def skew(base):
    t = jnp.broadcast_to(base, (8, span))
    row = lax.broadcasted_iota(jnp.int32, (8, span), 0)
    for step in (1, 2, 4):
        t = jnp.where((row & step) != 0, pltpu.roll(t, step, 1), t)
    while t.shape[0] < tile:
        t = jnp.concatenate([t, pltpu.roll(t, t.shape[0], 1)], axis=0)
    return t


def unskew(t):
    while t.shape[0] > 8:
        n = t.shape[0] // 2
        t = t[:n] + pltpu.roll(t[n:], span - n, 1)
    row = lax.broadcasted_iota(jnp.int32, (8, span), 0)
    for step in (1, 2, 4):
        t = jnp.where((row & step) != 0, pltpu.roll(t, span - step, 1), t)
    return jnp.sum(t, axis=0, keepdims=True)


def fill_mask(mask, segs, pads, seg_cols, row):
    length = mask.shape[0]
    rows = segs.shape[0]
    chosen = lax.broadcasted_iota(jnp.int32, (rows, length), 0) == row
    seg_k = jnp.sum(jnp.where(chosen, segs, 0.0), axis=0, keepdims=True)
    pad_k = jnp.sum(jnp.where(chosen, pads, 0.0), axis=0, keepdims=True)
    code = jnp.where(pad_k == 1.0, seg_k, -1.0)
    lane = lax.broadcasted_iota(jnp.int32, seg_cols.shape, 1)
    seg_q = jnp.sum(jnp.where(lane == row, seg_cols, 0.0), axis=1, keepdims=True)
    q = lax.broadcasted_iota(jnp.int32, (tile, length), 0)
    k = lax.broadcasted_iota(jnp.int32, (tile, length), 1)
    for a in range(length // tile):
        own = seg_q[a * tile : (a + 1) * tile]
        ok = (own == code) | (q + a * tile == k)
        mask[a * tile : (a + 1) * tile, :] = jnp.where(ok, 0.0, masked_logit)


def fill_bias(bias, table, hot, heads):
    base = dot(table, hot[0 : table.shape[1], :])
    for h in range(heads):
        bias[h] = skew(base[h : h + 1, :])


def normalize(x_ref, gain, normed):
    for a in range(x_ref.shape[0] // tile):
        rows = slice(a * tile, (a + 1) * tile)
        v = x_ref[rows, :].astype(f32)
        normed[rows, :] = (v * rms_scale(v) * gain).astype(bf16)


chunk = 32


def head_groups(heads, size):
    per = tile // size
    out = []
    for first in range(0, heads, per):
        members = range(first, min(heads, first + per))
        lanes = slice(first * size, (members[-1] + 1) * size)
        out.append((lanes, [(h, (h - first) * size) for h in members]))
    return out


def only(v, lane, size):
    if v.shape[1] == size:
        return v
    at = lax.broadcasted_iota(jnp.int32, v.shape, 1)
    return jnp.where((at >= lane) & (at < lane + size), v, jnp.zeros_like(v))


def merge(parts, size):
    out = parts[0]
    at = lax.broadcasted_iota(jnp.int32, out.shape, 1)
    for i, part in enumerate(parts[1:]):
        out = jnp.where(at >= (i + 1) * size, part, out)
    return out


def project_heads(normed_ref, w, parts):
    rows = parts[0].shape[1]
    for i, part in enumerate(parts):
        part[...] = dot(
            normed_ref[...], w[i * rows : (i + 1) * rows, :], ((1,), (1,))
        ).astype(bf16)


def softmax_chunks(length):
    for r in range(0, length, chunk):
        at = length - tile - r // tile * tile
        yield slice(r, r + chunk), slice(r % tile, r % tile + chunk), slice(at, at + length)


def attend_kernel(
    first, heads, size, sc, x_ref, seg_ref, pad_ref, segc_ref, gain_ref, w_ref, hot_ref,
    out_ref, normed, query, keys, values, mask, bias, logits, probs, inverse,
):
    length = x_ref.shape[0]
    wide = heads * size
    buckets = 32
    row = lax.rem(sc[16] + first + pl.program_id(0), seg_ref.shape[0])
    normalize(x_ref, gain_ref[...], normed)
    project_heads(normed, w_ref, (query, keys, values))
    fill_mask(mask, seg_ref[...], pad_ref[...], segc_ref[...], row)

    @pl.when(pl.program_id(0) == 0)
    def _():
        fill_bias(bias, w_ref[3 * wide : 3 * wide + 16, :tile][:, :buckets], hot_ref, heads)

    for lanes, members in head_groups(heads, size):
        parts = []
        for i, (h, lane) in enumerate(members):
            logits[i % 2] = dot(only(query[:, lanes], lane, size), keys[:, lanes], ((1,), (1,)))
            for rows, inner, at in softmax_chunks(length):
                v = logits[i % 2, rows, :] + bias[h, inner, at] + mask[rows, :]
                e = jnp.exp(v - jnp.max(v, axis=1, keepdims=True))
                total = jnp.sum(e, axis=1, keepdims=True)
                inverse[rows, :] = jnp.broadcast_to(1.0 / total, (chunk, tile))
                probs[i % 2, rows, :] = e.astype(bf16)
            part = dot(probs[i % 2], values[:, lanes])
            parts.append(part * inverse[:, : part.shape[1]])
        out_ref[0, :length, lanes] = merge(parts, size).astype(bf16)
    out_ref[0, length:, :] = w_ref[3 * wide : 3 * wide + 16, :wide]


def attend(first, offs, tokens, segs, pads, seg_cols, gain, w_qkv, hot, heads, size, after=()):
    rows, length = segs.shape
    d = tokens.shape[1]
    wide = heads * size
    args = [tokens, segs, pads, seg_cols, gain, w_qkv, hot]
    specs = [pl.BlockSpec((length, d), lambda i, sc: (lax.rem(sc[16] + first + i, rows), 0))]
    return launch(
        functools.partial(attend_kernel, first, heads, size), "attend", args,
        specs + [whole(v.shape) for v in args[1:]],
        [pl.BlockSpec((1, length + 16, wide), lambda i, sc: (i, 0, 0))],
        like(bf16, (rows, length + 16, wide)),
        grid=(rows,), offs=offs,
        scratch=[
            pltpu.VMEM((length, d), bf16),
            pltpu.VMEM((length, wide), bf16),
            pltpu.VMEM((length, wide), bf16),
            pltpu.VMEM((length, wide), bf16),
            pltpu.VMEM((length, length), f32),
            pltpu.VMEM((heads, tile, span), f32),
            pltpu.VMEM((2, length, length), f32),
            pltpu.VMEM((2, length, length), bf16),
            pltpu.VMEM((length, tile), f32),
        ],
        cost=cost(
            rows * (6 * length * d * wide + 4 * wide * length * length), 4,
            rows * heads * length * length,
        ),
        after=after,
    )


def high_low(v):
    high = v.astype(bf16)
    return high, (v - high.astype(f32)).astype(bf16)


def attend_back_slot(
    heads, size, mixed_ref, gm_ref, hot_ref, w, left_ref, table_out, acc,
    normed, query, keys, values, mask, bias, logits, gprobs, probs, dlog, skewed, diag,
):
    length = normed.shape[0]
    wide = heads * size
    fill_bias(bias, mixed_ref[length:, :tile][:, :32], hot_ref, heads)
    project_heads(normed, w, (query, keys, values))
    for lanes, members in head_groups(heads, size):
        q, k, v = query[:, lanes], keys[:, lanes], values[:, lanes]
        grad = gm_ref[:, lanes]
        results = []
        for h, lane in members:
            logits[...] = dot(only(q, lane, size), k, ((1,), (1,)))
            gprobs[...] = dot(only(grad, lane, size), v, ((1,), (1,)))
            skewed[...] = jnp.zeros_like(skewed)
            for rows, inner, at in softmax_chunks(length):
                t = logits[rows, :] + bias[h, inner, at] + mask[rows, :]
                e = jnp.exp(t - jnp.max(t, axis=1, keepdims=True))
                p = e * (1.0 / jnp.sum(e, axis=1, keepdims=True))
                probs[rows, :] = p.astype(bf16)
                gp = gprobs[rows, :]
                gl = p * (gp - jnp.sum(gp * p, axis=1, keepdims=True))
                dlog[rows, :] = gl.astype(bf16)
                skewed[inner, at] += gl
            diag[h : h + 1, :] = unskew(skewed[...])
            results.append(
                (
                    dot(dlog[...], k),
                    dot(dlog[...], q, ((0,), (0,))),
                    dot(probs[...], grad, ((0,), (0,))),
                )
            )
        for part in range(3):
            merged = merge([r[part] for r in results], size)
            left_ref[part, :, lanes] = merged.astype(bf16)
    left_ref[3] = mixed_ref[:length, :]
    high, low = high_low(diag[...])
    table = dot(high, hot_ref[...], ((1,), (1,))) + dot(low, hot_ref[...], ((1,), (1,)))
    table_out[...] = table
    value = sum(
        dot(left_ref[part], w[part * wide : (part + 1) * wide, :]) for part in range(3)
    )
    acc[...] += value


def attend_back_kernel(
    first, count, last, heads, size, sc, x_ref, seg_ref, pad_ref, segc_ref, gain_ref, hot_ref,
    gm_ref, *refs,
):
    mixed_refs, refs = refs[:count], list(refs[count:])
    acc_in = refs.pop(0) if first else None
    if last:
        gha_ref, gat_ref, fin_ref, mid_ref, score_ref = refs[:5]
        refs = refs[5:]
        tables = [refs.pop(0)] if first else []
    w_ref = refs[0]
    refs = refs[1 + (1 if first else 0) :]
    left_ref, table_out = refs[:2]
    if last:
        dx_ref, both_ref, small_ref, acc = refs[2:6]
        refs = refs[6:]
    else:
        acc, refs = refs[2], refs[3:]
    (
        w, sems, normed, query, keys, values, mask, bias, logits, gprobs, probs, dlog, skewed, diag,
    ) = refs
    length, d = x_ref.shape
    wide = heads * size
    row = sc[16]
    gain = gain_ref[...]
    blocks = length // tile
    copies = [
        gathered_copies(w_ref, w.at[i], sems.at[i], lax.rem(row + 4 - first - i, 4))
        for i in range(count)
    ]
    for copy in sum(copies, []):
        copy.start()
    normalize(x_ref, gain, normed)
    fill_mask(mask, seg_ref[...], pad_ref[...], segc_ref[...], row)
    diag[...] = jnp.zeros_like(diag)
    if acc_in is None:
        acc[...] = jnp.zeros_like(acc)
    else:
        acc[...] = acc_in[...]
    for i in range(count):
        for copy in copies[i]:
            copy.wait()
        attend_back_slot(
            heads, size, mixed_refs[i], gm_ref.at[i], hot_ref, w.at[i], left_ref.at[i],
            table_out.at[8 * i : 8 * i + 8], acc,
            normed, query, keys, values, mask, bias, logits, gprobs, probs, dlog, skewed, diag,
        )
    if not last:
        return
    total = jnp.zeros((1, d), f32)
    for a in range(blocks):
        rows = slice(a * tile, (a + 1) * tile)
        back, part = rms_back(x_ref[rows, :].astype(f32), gain, acc[rows, :])
        dx_ref[rows, :] = (gha_ref[rows, :] + back).astype(bf16)
        total = total + part
    both_ref[0] = normed[...]
    both_ref[1] = gat_ref[...]
    dx_ref[length:, :] = jnp.zeros((dx_ref.shape[0] - length, d), bf16)
    n = score_ref.shape[0] // 16
    cols = score_ref.shape[1]
    high, low = high_low(score_ref[...])
    for i in range(n):
        rows = slice(16 * i, 16 * i + 16)
        dx_ref[length : length + 16, 2 * i * tile : 2 * i * tile + cols] = high[rows]
        dx_ref[length : length + 16, (2 * i + 1) * tile : (2 * i + 1) * tile + cols] = low[rows]
    line = lax.broadcasted_iota(jnp.int32, (8, d), 0)
    gains = jnp.where(
        line == 0, total, jnp.where(line == 1, fin_ref[...], jnp.where(line == 2, mid_ref[...], 0.0))
    )
    line = lax.broadcasted_iota(jnp.int32, (8, tile), 0)
    column = lax.broadcasted_iota(jnp.int32, (8, tile), 1)

    def turned(value, at):
        place = jnp.where(column == line + at, 1.0, 0.0).astype(bf16)
        high, low = high_low(value)
        return dot(high, place, ((0,), (0,))) + dot(low, place, ((0,), (0,)))

    gains = turned(gains, 0)
    tables = [t[8 * i : 8 * i + 8] for t in tables + [table_out] for i in range(t.shape[0] // 8)]
    for k, value in enumerate(tables):
        small_ref[k] = gains.astype(bf16)
        small_ref[k, 0:tile, :] = (gains[0:tile] + turned(value, tile // 2)).astype(bf16)


def attend_back(
    first, count, common, grad_mixed, mixed, acc, left, finish, weights, heads, size, after=()
):
    offs, *shared = common
    rows, length = shared[1].shape
    d = shared[0].shape[1]
    slots = grad_mixed.shape[0]
    wide = heads * size
    last = first + count == slots
    mixed = mixed[first : first + count]
    args = [*shared, grad_mixed, *mixed]
    specs = [pl.BlockSpec((length, d), lambda i, sc: (sc[16], 0))]
    specs += [whole(v.shape) for v in shared[1:]]
    specs.append(pl.BlockSpec((count, length, wide), lambda i, sc: (first // count, 0, 0)))
    specs += [whole(m.shape) for m in mixed]
    if first:
        args.append(acc)
        specs.append(whole(acc.shape))
    if last:
        args += finish
        specs += [whole(v.shape) for v in finish]
    args += [weights] + ([left] if first else [])
    specs += [ANY] * (2 if first else 1)
    out_specs = [
        pl.BlockSpec((count, 4, length, wide), lambda i, sc: (first // count, 0, 0, 0)),
        whole((8 * count, tile)),
    ]
    out_shape = like(bf16, (slots, 4, length, wide)) + like(f32, (8 * count, tile))
    scratch = []
    if last:
        shapes = ((length + 16, d), (2, length, d), (slots, d, tile))
        out_specs += [whole(shape) for shape in shapes]
        out_shape += like(bf16, *shapes)
        scratch = [pltpu.VMEM((length, d), f32)]
    else:
        out_specs.append(whole((length, d)))
        out_shape += like(f32, (length, d))
    return launch(
        functools.partial(attend_back_kernel, first, count, last, heads, size),
        f"attend_back{first}",
        args, specs, out_specs, out_shape, offs=offs,
        scratch=scratch
        + [
            pltpu.VMEM((count, 8 * weights.shape[4], d), bf16),
            pltpu.SemaphoreType.DMA((count, 8)),
            pltpu.VMEM((length, d), bf16),
            pltpu.VMEM((length, wide), bf16),
            pltpu.VMEM((length, wide), bf16),
            pltpu.VMEM((length, wide), bf16),
            pltpu.VMEM((length, length), f32),
            pltpu.VMEM((heads, tile, span), f32),
            pltpu.VMEM((length, length), f32),
            pltpu.VMEM((length, length), f32),
            pltpu.VMEM((length, length), bf16),
            pltpu.VMEM((length, length), bf16),
            pltpu.VMEM((tile, span), f32),
            pltpu.VMEM((8, span), f32),
        ],
        cost=cost(
            count * (12 * length * d * wide + 14 * wide * length * length), 16,
            count * heads * length * length,
        ),
        after=after, alias=len(args) - 1 if first else None, mib=32,
    )


def gate_up(normed_ref, w, act_ref, dact_ref, inner_ref):
    hidden = act_ref.shape[2]
    for n in range(hidden // 256):
        cols = slice(n * 256, (n + 1) * 256)
        normed = normed_ref[...]
        gate = dot(normed, w[:, cols])
        up = dot(normed, w[:, hidden + n * 256 : hidden + (n + 1) * 256])
        t = jnp.tanh(gelu_c * (gate + 0.044715 * gate * gate * gate))
        half = 0.5 * (1.0 + t)
        act = gate * half
        slope = half + 0.5 * gate * (1.0 - t * t) * (
            gelu_c * (1.0 + 3 * 0.044715 * gate * gate)
        )
        act_ref[0, :, cols] = act.astype(bf16)
        dact_ref[0, :, cols] = (up * slope).astype(bf16)
        inner_ref[0, :, cols] = (act * up).astype(bf16)


def forward_kernel(
    sc, x_ref, gain_ref, gain_l_ref, wp_ref, padc_ref, query_ref, cot_ref, top_ref, *refs
):
    slots = 4
    mixed, own, arrays = refs[:slots], refs[slots : slots + 4], refs[slots + 4 : slots + 12]
    hid_ref, normed_ref, act_ref, dact_ref, inner_ref = refs[slots + 12 : slots + 17]
    score_ref, nfin, ge, total_ref, gft_ref, ghf_ref = refs[slots + 17 : slots + 23]
    w, wd, wo, w_sems, d_sems, o_sems, acc, embed, unit = refs[slots + 23 :]
    length, d = x_ref.shape
    hidden = act_ref.shape[2]
    step = pl.program_id(0)
    blocks = length // tile
    w_copies = chunk_copies(sc, zip(own, (0, hidden)), arrays, w, w_sems)
    d_copies = chunk_copies(sc, [(own[2], 0)], arrays, wd, d_sems, 2 * hidden)
    o_copies = chunk_copies(sc, [(own[3], 0)], arrays, wo, o_sems, 3 * hidden)

    @pl.when(step == 0)
    def _():
        for copy in o_copies + w_copies + d_copies:
            copy.start()
        for copy in o_copies:
            copy.wait()
        gain = gain_ref[...]
        for a in range(blocks):
            rows = slice(a * tile, (a + 1) * tile)
            h = x_ref[rows, :].astype(f32)
            for k in range(slots):
                h = h + dot(mixed[k][rows, :], wo[k], ((1,), (1,)))
            hid_ref[rows, :] = h
            acc[rows, :] = h
            normed_ref[rows, :] = (h * rms_scale(h) * gain).astype(bf16)
        for copy in w_copies[:2] + d_copies[:1]:
            copy.wait()

    @pl.when(step == 1)
    def _():
        for copy in w_copies[2:] + d_copies[1:]:
            copy.wait()

    gate_up(normed_ref, w.at[step], act_ref, dact_ref, inner_ref)
    acc[...] += dot(inner_ref[0], wd[step])

    @pl.when(step == slots - 1)
    def _():
        lane = lax.broadcasted_iota(jnp.int32, padc_ref.shape, 1)
        pad = jnp.sum(jnp.where(lane == sc[16], padc_ref[...], 0.0), axis=1, keepdims=True)
        gain = gain_l_ref[...]
        for a in range(blocks):
            rows = slice(a * tile, (a + 1) * tile)
            h = acc[rows, :]
            n = (h * rms_scale(h) * gain).astype(bf16)
            nfin[rows, :] = n
            e = dot(n, wp_ref[...])
            embed[rows, :] = e
            inverse = lax.rsqrt(jnp.sum(e * e, axis=1, keepdims=True) + eps)
            unit[rows, :] = (e * inverse * pad[rows]).astype(bf16)
        query = query_ref[0]
        cot = cot_ref[0]
        top = top_ref[0]
        scored = dot(query, unit[...], ((1,), (1,)))
        place = lax.broadcasted_iota(jnp.int32, scored.shape, 1)
        out_lane = lax.broadcasted_iota(jnp.int32, cot.shape, 1)
        chosen = jnp.zeros_like(cot)
        weight = jnp.zeros_like(scored)
        for j in range(top.shape[1]):
            here = place == top[:, j : j + 1]
            mine = jnp.sum(jnp.where(here, scored, 0.0), axis=1, keepdims=True)
            chosen = jnp.where(out_lane == j, mine, chosen)
            weight = weight + jnp.where(here, cot[:, j : j + 1], 0.0)
        score_ref[...] = chosen
        high, low = high_low(weight)
        gunit = dot(high, query, ((0,), (0,))) + dot(low, query, ((0,), (0,)))
        total = jnp.zeros((1, d), f32)
        for a in range(blocks):
            rows = slice(a * tile, (a + 1) * tile)
            e = embed[rows, :]
            inverse = lax.rsqrt(jnp.sum(e * e, axis=1, keepdims=True) + eps)
            u = gunit[rows] * pad[rows]
            cube = (inverse * inverse * inverse) * jnp.sum(u * e, axis=1, keepdims=True)
            g = (inverse * u - e * cube).astype(bf16)
            ge[rows, :] = g
            back, part = rms_back(acc[rows, :], gain, dot(g, wp_ref[...], ((1,), (1,))))
            total = total + part
            ghf_ref[rows, :] = back
            gft_ref[rows, :] = back.astype(bf16)
        total_ref[...] = total


def forward(
    offs, tokens, gain, gain_l, w_proj, pad_cols, query, cot, top, mixed, own, arrays, length
):
    d = tokens.shape[1]
    slots = len(mixed)
    hidden = own[0].shape[1]
    wide = own[3].shape[1]
    e = w_proj.shape[1]
    three = (slots, length, hidden)
    score, low, embed, total = cot.shape[1:], (length, d), (length, e), (1, d)
    per_slot = pl.BlockSpec((1, length, hidden), lambda i, sc: (i, 0, 0))

    def row_block(v):
        return pl.BlockSpec((1,) + v.shape[1:], lambda i, sc: (sc[16], 0, 0))

    return launch(
        forward_kernel, "forward",
        [tokens, gain, gain_l, w_proj, pad_cols, query, cot, top, *mixed, *own, *arrays],
        [pl.BlockSpec((length, d), lambda i, sc: (sc[16], 0))]
        + [whole(v.shape) for v in (gain, gain_l, w_proj, pad_cols)]
        + [row_block(v) for v in (query, cot, top)]
        + [whole(m.shape) for m in mixed]
        + [ANY] * 12,
        [whole(low), whole(low)] + [per_slot] * 3
        + [whole(v) for v in (score, low, embed, total, low, low)],
        like(f32, low) + like(bf16, low, three, three, three) + like(f32, score)
        + like(bf16, low, embed) + like(f32, total) + like(bf16, low) + like(f32, low),
        grid=(slots,), offs=offs,
        scratch=[
            pltpu.VMEM((slots, d, 2 * hidden), bf16),
            pltpu.VMEM((slots, hidden, d), bf16),
            pltpu.VMEM((slots, d, wide), bf16),
            pltpu.SemaphoreType.DMA((copies_per_chunk,)),
            pltpu.SemaphoreType.DMA((copies_per_chunk,)),
            pltpu.SemaphoreType.DMA((copies_per_chunk,)),
            pltpu.VMEM((length, d), f32),
            pltpu.VMEM((length, e), f32),
            pltpu.VMEM((length, e), bf16),
        ],
        cost=cost(2 * length * d * (d + 3 * slots * hidden), 24, slots * length * hidden),
        mib=58,
    )


def ffn_back_kernel(sc, hid_ref, gft_ref, ghf_ref, act_ref, dact_ref, gain_ref, *refs):
    slots = 4
    own, arrays, refs = refs[:4], refs[4:12], refs[12:]
    gg_ref, gu_ref, gha_ref, gat_ref, gm_ref, total_ref, w, wd, wo, w_sems, d_sems, acc = refs
    length, d = hid_ref.shape
    hidden = wd.shape[1]
    step = pl.program_id(0)
    w_copies = chunk_copies(sc, zip(own, (0, hidden)), arrays, w, w_sems.at[0])
    w_copies += chunk_copies(sc, [(own[3], 0)], arrays, wo, w_sems.at[1], 3 * hidden)
    d_copies = chunk_copies(sc, [(own[2], 0)], arrays, wd, d_sems, 2 * hidden)
    blocks = length // tile

    @pl.when(step == 0)
    def _():
        for copy in d_copies[:1] + w_copies[:2] + d_copies[1:] + w_copies[2:]:
            copy.start()
        acc[...] = jnp.zeros_like(acc)
        for copy in d_copies[:1] + w_copies[:2]:
            copy.wait()

    @pl.when(step == 1)
    def _():
        for copy in d_copies[1:] + w_copies[2:]:
            copy.wait()

    def part(n, carry):
        cols = pl.ds(pl.multiple_of(n * 256, 256), 256)
        gi = dot(gft_ref[...], wd[step, cols, :], ((1,), (1,)))
        gg_ref[0, :, cols] = (gi * dact_ref[0, :, cols].astype(f32)).astype(bf16)
        gu_ref[0, :, cols] = (gi * act_ref[0, :, cols].astype(f32)).astype(bf16)
        return carry

    lax.fori_loop(0, hidden // 256, part, 0)
    acc[...] += dot(gg_ref[0], w[step, :, :hidden], ((1,), (1,))) + dot(
        gu_ref[0], w[step, :, hidden : 2 * hidden], ((1,), (1,))
    )

    @pl.when(step == slots - 1)
    def _():
        gain = gain_ref[...]
        total = jnp.zeros((1, d), f32)
        for a in range(blocks):
            rows = slice(a * tile, (a + 1) * tile)
            back, part = rms_back(hid_ref[rows, :], gain, acc[rows, :])
            total = total + part
            g = ghf_ref[rows, :] + back
            gha_ref[rows, :] = g
            g = g.astype(bf16)
            gat_ref[rows, :] = g
            for k in range(slots):
                gm_ref[k, rows, :] = dot(g, wo[k]).astype(bf16)
        total_ref[...] = total


def ffn_back(offs, hid, gft, ghf, act, dact, gain, own, arrays, after=()):
    length, d = hid.shape
    slots, _, hidden = act.shape
    wide = own[3].shape[1]
    mixed = (slots, length, wide)
    block = pl.BlockSpec((1, length, hidden), lambda i, sc: (i, 0, 0))
    return launch(
        ffn_back_kernel, "ffn_back",
        [hid, gft, ghf, act, dact, gain, *own, *arrays],
        [whole(v.shape) for v in (hid, gft, ghf)] + [block] * 2 + [whole(gain.shape)] + [ANY] * 12,
        [block, block] + [whole(v) for v in (hid.shape, hid.shape, mixed, (1, d))],
        like(bf16, act.shape, act.shape) + like(f32, hid.shape) + like(bf16, hid.shape, mixed)
        + like(f32, (1, d)),
        grid=(slots,), offs=offs,
        scratch=[
            pltpu.VMEM((slots, d, 2 * hidden), bf16),
            pltpu.VMEM((slots, hidden, d), bf16),
            pltpu.VMEM((slots, d, wide), bf16),
            pltpu.SemaphoreType.DMA((2, copies_per_chunk)),
            pltpu.SemaphoreType.DMA((copies_per_chunk,)),
            pltpu.VMEM((length, d), f32),
        ],
        cost=cost(2 * length * d * (3 * slots * hidden + d), 24),
        after=after, mib=42,
    )


def keep_parts(sc, out, refs):
    send_a, keep_a, send_b, keep_b = refs
    half = send_a.shape[2]
    x, y = sc[18], sc[19]

    def rows(y, x, extra):
        at = pl.multiple_of((2 * y + x) * (2 * half) + extra, 16)
        return out[pl.ds(at, half), :]

    for other in range(2):
        send_a[0, other] = rows(other, 1 - x, 0)
        keep_a[0, other] = rows(other, x, 0)
        send_b[0, other] = rows(1 - y, other, half)
        keep_b[0, other] = rows(y, other, half)


def parts_of(slots, rows, width):
    part = (1, 2, rows // 8, width)
    spec = pl.BlockSpec(part, lambda i, sc: (i, 0, 0, 0))
    return [spec] * 4, [jax.ShapeDtypeStruct((slots,) + part[1:], bf16)] * 4


def product_kernel(lefts, pairs, keep, sc, *refs):
    left_refs, right_refs = refs[:lefts], refs[lefts : lefts + len(pairs)]
    refs = refs[lefts + len(pairs) :]
    out = refs[-1] if keep else refs[-1].at[0]
    at = 0
    for right_ref, which in zip(right_refs, pairs):
        right = right_ref[...]
        left = left_refs[which][...]
        left, right = (v.reshape(v.shape[-2:]) for v in (left, right))
        cols = slice(at, at + right.shape[1])
        value = dot(left, right, ((0,), (0,)))
        if keep:
            value = value + refs[0][0, :, cols].astype(f32)
        out[:, cols] = value.astype(bf16)
        at += right.shape[1]
    if keep:
        keep_parts(sc, out, refs[-5:-1])


def products(offs, lefts, rights, slots, got=None, after=(), mib=16):
    keep = got is not None
    length, half = lefts[0].shape[-2], lefts[0].shape[-1] // 2
    width = sum(right.shape[-1] for right, _ in rights)

    def which(sc):
        return sc[17] if keep else 1 - sc[17]

    specs = []
    for left in lefts:
        if left.ndim == 3:
            specs.append(pl.BlockSpec((1, length, half), lambda i, sc: (i, 0, which(sc))))
        else:
            specs.append(pl.BlockSpec((length, half), lambda i, sc: (0, which(sc))))
    for right, _ in rights:
        if right.ndim == 3:
            specs.append(pl.BlockSpec((1,) + right.shape[1:], lambda i, sc: (i, 0, 0)))
        else:
            specs.append(whole(right.shape))
    args = list(lefts) + [right for right, _ in rights]
    block = pl.BlockSpec((1, half, width), lambda i, sc: (i, 0, 0))
    out_specs, out_shape, scratch = [block], like(bf16, (slots, half, width)), []
    if keep:
        specs.append(block)
        args.append(got)
        out_specs, out_shape = parts_of(slots, half, width)
        scratch = [pltpu.VMEM((half, width), bf16)]
    return launch(
        functools.partial(product_kernel, len(lefts), [i for _, i in rights], keep),
        "products_keep" if keep else "products_send",
        args, specs, out_specs, out_shape, grid=(slots,), offs=offs, scratch=scratch, after=after,
        mib=mib,
    )


def attn_product_kernel(keep, sc, la, lb, ra, rb, small, *refs):
    out = refs[-1] if keep else refs[-1].at[0]
    quarter, d = la.shape[3], ra.shape[2]
    for left, right, at in ((la, ra, 0), (lb, rb, quarter)):
        value = dot(left[0, 0], right[0], ((0,), (0,)))
        if keep:
            value = value + refs[0][0, at : at + quarter, :d].astype(f32)
        out[at : at + quarter, :d] = value.astype(bf16)
    value = small[0]
    if keep:
        value = add(value, refs[0][0, :, d:])
    out[:, d:] = value
    if keep:
        keep_parts(sc, out, refs[1:5])


def attn_products(offs, left, both, small, got=None, after=()):
    keep = got is not None
    slots, _, length, quarter = left.shape
    d = both.shape[2]
    width = d + small.shape[2]
    half = 2 * quarter

    def which(sc):
        return sc[17] if keep else 1 - sc[17]

    block = pl.BlockSpec((1, half, width), lambda i, sc: (i, 0, 0))
    specs = [
        pl.BlockSpec((1, 1, length, quarter), lambda i, sc: (i, 2 * which(sc), 0, 0)),
        pl.BlockSpec((1, 1, length, quarter), lambda i, sc: (i, 2 * which(sc) + 1, 0, 0)),
        pl.BlockSpec((1, length, d), lambda i, sc: (0, 0, 0)),
        pl.BlockSpec((1, length, d), lambda i, sc: (which(sc), 0, 0)),
        pl.BlockSpec((1, half, small.shape[2]), lambda i, sc: (i, which(sc), 0)),
    ]
    args = [left, left, both, both, small]
    out_specs, out_shape, scratch = [block], like(bf16, (slots, half, width)), []
    if keep:
        specs.append(block)
        args.append(got)
        out_specs, out_shape = parts_of(slots, half, width)
        scratch = [pltpu.VMEM((half, width), bf16)]
    return launch(
        functools.partial(attn_product_kernel, keep), "attn_keep" if keep else "attn_send",
        args, specs, out_specs, out_shape, grid=(slots,), offs=offs, scratch=scratch, after=after,
        mib=16,
    )


def add(a, b):
    return (a.astype(f32) + b.astype(f32)).astype(bf16)


def second_kernel(sc, ka, ra, kb, rb, send_a, keep_a, send_b, keep_b):
    x, y = sc[18], sc[19]
    send_a[0] = add(ka[0, 1 - y], ra[0, 1 - y])
    keep_a[0] = add(ka[0, y], ra[0, y])
    send_b[0] = add(kb[0, 1 - x], rb[0, 1 - x])
    keep_b[0] = add(kb[0, x], rb[0, x])


def second_sums(offs, *arrays, after=()):
    slots, _, half, width = arrays[0].shape
    into = pl.BlockSpec((1, 2, half, width), lambda i, sc: (i, 0, 0, 0))
    out = pl.BlockSpec((1, half, width), lambda i, sc: (i, 0, 0))
    return launch(
        second_kernel, "second_sums", arrays, [into] * 4, [out] * 4,
        like(bf16, *[(slots, half, width)] * 4), grid=(slots,), offs=offs, after=after,
    )


def third_kernel(ka, ra, kb, rb, *outs):
    half = ka.shape[1]
    for k, out in enumerate(outs):
        out[:half, :] = add(ka[k], ra[k])
        out[half:, :] = add(kb[k], rb[k])


def third_sums(*arrays, after=()):
    slots, half, width = arrays[0].shape
    shape = (2 * half, width)
    return launch(
        third_kernel, "third_sums", arrays, [whole(arrays[0].shape)] * 4, [whole(shape)] * slots,
        like(bf16, *[shape] * slots), after=after,
    )


def third_stacked_kernel(sc, ka, ra, kb, rb, out):
    n, half, _ = ka.shape
    for k in range(n):
        to = lax.rem(sc[16] + n - k, n)
        out[to, :half, :] = add(ka[k], ra[k])
        out[to, half:, :] = add(kb[k], rb[k])


def third_stacked(offs, *arrays, after=()):
    slots, half, width = arrays[0].shape
    shape = (slots, 2 * half, width)
    (out,), token = launch(
        third_stacked_kernel, "third_stacked", arrays, [whole(arrays[0].shape)] * 4,
        [whole(shape)], like(bf16, shape), offs=offs, after=after,
    )
    return out, token


def last_kernel(*refs):
    t = [ref[...].astype(f32) for ref in refs[:4]]
    refs[4][...] = ((t[0] + t[2]) + (t[1] + t[3])).astype(refs[4].dtype)


def last_sum(arrays, dtype, after=()):
    shape = arrays[0].shape
    return launch(
        last_kernel, "last_sum", arrays, [whole(shape)] * 4, [whole(shape)], like(dtype, shape),
        after=after,
    )


def stack_kernel(a, xa, b, yb, sa, sb):
    sa[0], sa[1], sb[0], sb[1] = a[...], xa[...], b[...], yb[...]


def stack_pairs(a, xa, b, yb, after):
    out = (2,) + a.shape
    return launch(
        stack_kernel, "stack_pairs", [a, xa, b, yb], [whole(a.shape)] * 4, [whole(out)] * 2,
        like(bf16, out, out), after=after,
    )


class Reduce:
    def __init__(self, place, offs, kept):
        self.place, self.offs, self.kept = place, offs, kept

    def first(self, after=()):
        send_a, keep_a, send_b, keep_b = self.kept
        ra, rb = self.place.swap(send_a, XBIT), self.place.swap(send_b, YBIT)
        self.kept, token = second_sums(self.offs, keep_a, ra, keep_b, rb, after=after)
        return token

    def second(self, after=()):
        send_a, keep_a, send_b, keep_b = self.kept
        ra, rb = self.place.swap(send_a, YBIT), self.place.swap(send_b, XBIT)
        self.kept, token = third_sums(keep_a, ra, keep_b, rb, after=after)
        return token

    def second_and_third(self, after=()):
        send_a, keep_a, send_b, keep_b = self.kept
        ra, rb = self.place.swap(send_a, YBIT), self.place.swap(send_b, XBIT)
        v, token = third_stacked(self.offs, keep_a, ra, keep_b, rb, after=after)
        total = lax.psum_scatter(v, "mp", scatter_dimension=0, tiled=True)
        if self.place.n_out > 1:
            total = lax.psum(total.astype(f32), "out").astype(bf16)
        self.total = total.reshape(v.shape[1:])
        return token

    def third(self, after=()):
        p = self.place
        t = [self.kept[0]] + [p.shift(self.kept[k], -k) for k in range(1, p.n_mp)]
        if p.n_out > 1:
            (total,), token = last_sum(t, f32, after)
            self.total = lax.psum(total, "out").astype(bf16)
        else:
            (self.total,), token = last_sum(t, bf16, after)
        return token


def open_kernel(v_ref, *outs):
    rows = v_ref.shape[3]
    for at, (c, y, x) in enumerate(np.ndindex(2, 2, 2)):
        left = 0
        for out in outs:
            value = v_ref[y, x, c, :, left : left + out.shape[1]]
            out[at * rows : (at + 1) * rows, :] = value.astype(f32)
            left += out.shape[1]


def beside_kernel(a, b, out):
    out[:, : a.shape[1]] = a[...]
    out[:, a.shape[1] :] = b[...]


def gathered(a, b, cuts, start_after, after):
    rows, width = a.shape[0], a.shape[1] + b.shape[1]
    (v,), _ = launch(
        beside_kernel, "beside", [a, b], [whole(a.shape), whole(b.shape)],
        [whole((rows, width))], like(bf16, (rows, width)), after=start_after,
    )
    v = lax.all_gather(v, group, tiled=False).reshape(2, 2, 2, rows, width)
    shapes = [(8 * rows, cut) for cut in cuts]
    return launch(
        open_kernel, "open", [v], [whole(v.shape)], [whole(shape) for shape in shapes],
        like(f32, *shapes), after=after, mib=58,
    )


def unpack_kernel(offs, *refs):
    arrays, outs, small, full = refs[:8], refs[8:-2], refs[-2], refs[-1]
    for at in range(16):
        value = arrays[at // 2][at % 2]
        rows = pl.ds(pl.multiple_of(offs[at], 16), value.shape[0])
        full[rows, :] = value.astype(f32)
    rows, d = outs[0].shape
    for i, out in enumerate(outs):
        out[...] = full[i * rows : (i + 1) * rows, :d]
    small[...] = full[:, d:]


def unpack(offs, arrays, count, small):
    half, width = arrays[0].shape[1:]
    rows, d = 16 * half, width - small
    shapes = [(rows // count, d)] * count + [(rows, small)]
    outs, _ = launch(
        unpack_kernel, "unpack", arrays, [whole(v.shape) for v in arrays],
        [whole(v) for v in shapes], like(f32, *shapes), offs=offs,
        scratch=[pltpu.VMEM((rows, width), f32)],
    )
    return outs


def local(
    tokens, segment_ids, pad_mask, top_index, query_emb, score_cot, gain_attn, w_query, w_key,
    w_value, w_out, rel_table, gain_ffn, w_gate, w_up, w_down, gain_final, w_proj,
):
    place = Place()
    slots = place.n_mp
    rows, length = segment_ids.shape
    d = tokens.shape[1]
    heads = rel_table.shape[1]
    size = w_query.shape[1] // heads
    wide = heads * size
    hot = jnp.asarray(bucket_hot(rel_table.shape[0], length), bf16)
    segs, pads = segment_ids.astype(f32), pad_mask.astype(f32)
    seg_cols, pad_cols = segs.T, pads.T
    gain_a, gain_f, gain_l = (
        g.astype(f32).reshape(1, d) for g in (gain_attn, gain_ffn, gain_final)
    )
    offs = place.offsets(d // 8)

    buckets = rel_table.shape[0]
    table = jnp.zeros((64, d), bf16).at[:heads, :buckets].set(rel_table.T)
    w_qkv = jnp.concatenate([w_query.T, w_key.T, w_value.T, table])
    w_out_t = w_out.T
    eighth = d // 8
    hidden = w_gate.shape[1]

    def piece(*arrays):
        parts = []
        for v in arrays:
            rows = v.shape[0] // 8
            parts.append(lax.dynamic_slice_in_dim(v, place.p * rows, rows, 0))
        return jnp.concatenate(parts, axis=1) if len(parts) > 1 else parts[0]

    common = (offs, tokens, segs, pads, seg_cols, gain_a)
    own = (w_gate, w_up, w_down, w_out_t)
    z1 = lax.all_gather(piece(*own[:2]), "mp")
    piece2 = piece(*own[2:])
    z2 = [place.shift(piece2, k) for k in range(1, slots)]
    (attended,), done = attend(1, *common, w_qkv, hot, heads, size)
    mixed = [attended[slots - 1]] + [place.shift(attended[k - 1], k) for k in range(1, slots)]
    halved, _ = split(offs, z1, z2, (done,))
    s1, _ = place.first_round(*halved)
    arrays = place.second_round(*s1, mixed[1:])
    (hid, normed_ffn, act, dact, inner, score, nfin, ge, gain_fin, gft, ghf), done = forward(
        offs, tokens, gain_f, gain_l, w_proj, pad_cols, query_emb, score_cot, top_index, mixed,
        own, arrays, length,
    )
    all_qkv = lax.all_gather(relay([piece(w_qkv)], (done,))[0], group + ("mp",))
    all_qkv = all_qkv.reshape((2, 2, 2, slots) + all_qkv.shape[-2:])
    down_sides = ([inner, nfin], [(gft, 0), (ge, 1)])
    (send,), _ = products(offs, *down_sides, slots, mib=58)
    kept, kept_done = products(offs, *down_sides, slots, place.swap(send, CORE))
    down = Reduce(place, offs, kept)
    (gg, gu, gha, gat, gm, gain_mid), done = ffn_back(
        offs, hid, gft, ghf, act, dact, gain_f, own, arrays, (kept_done,)
    )
    gu_sides = ([normed_ffn], [(gg, 0), (gu, 0)])
    done = down.first((done,))
    (send,), done = products(offs, *gu_sides, slots, None, (done,))
    got = place.swap(send, CORE)
    done = down.second((done,))
    kept, done = products(offs, *gu_sides, slots, got, (done,))
    gate_up = Reduce(place, offs, kept)
    finish = [gha, gat, gain_fin, gain_mid, score]

    def back(first, acc, left, after):
        return attend_back(
            first, slots // 2, common + (hot,), gm, mixed, acc, left, finish, all_qkv, heads, size,
            after,
        )

    (left, tables, acc), done = back(0, None, None, (done,))
    finish.append(tables)
    done = down.third((done,))
    done = gate_up.first((done,))
    (left, _, dx, both, small), done = back(slots // 2, acc, left, (done,))
    right, left_ = place.both_ways(dx, dx)
    done = gate_up.second_and_third((done,))
    (send,), _ = attn_products(offs, left, both, small, None, (done,))
    kept, done = attn_products(offs, left, both, small, place.swap(send, CORE))
    attn = Reduce(place, offs, kept)
    (*so_far, right, left_), done = collect(1, slots, offs, right, left_, dx, None, (done,))
    right, left_ = place.both_ways(right, left_)
    done = start_after = attn.first((done,))
    done = attn.second((done,))
    (*so_far, right, left_), done = collect(2, slots, offs, right, left_, dx, so_far, (done,))
    right, left_ = place.both_ways(right, left_)
    (grad_down, grad_proj, grad_gate, grad_up), done = gathered(
        down.total, gate_up.total, (d, w_proj.shape[1], hidden, hidden), (start_after,),
        (done,),
    )
    done = attn.third((done,))
    (input_grad, packed), done = collect(3, slots, offs, right, left_, dx, so_far, (done,))
    last, _ = place.first_round(*halves(attn.total, 0), (done,))
    grad_q, grad_k, grad_v, grad_out, small = unpack(
        offs, place.second_round(*last), 4, small.shape[2]
    )

    input_grad = input_grad.reshape(rows * length, d)
    n, m = score.shape
    packed = packed.astype(f32).reshape(slots, 16, d // 128, 128)[:, :, : 2 * (n // 16), :m]
    packed = packed[:, :, 0::2] + packed[:, :, 1::2]
    scores = packed.transpose(0, 2, 1, 3).reshape(slots, n, m)
    return (
        scores,
        input_grad,
        small[:, 0],
        grad_q.T,
        grad_k.T,
        grad_v.T,
        grad_out,
        small[:buckets, 64 : 64 + heads],
        small[:, 2],
        grad_gate,
        grad_up,
        grad_down,
        small[:, 1],
        grad_proj,
    )


def solution(mesh):
    n_dp, n_mp = mesh.shape["dp"], mesh.shape["mp"]
    mesh = Mesh(mesh.devices.reshape(n_dp // 8, 2, 2, 2, n_mp), dp + ("mp",))
    return jax.shard_map(
        local,
        mesh=mesh,
        in_specs=(
            P(dp, None),
            P(dp, None),
            P(dp, None),
            P(dp, None, None),
            P(dp, None, None),
            P(dp, None, None),
            P(),
            P(None, "mp"),
            P(None, "mp"),
            P(None, "mp"),
            P("mp", None),
            P(None, "mp"),
            P(),
            P(None, "mp"),
            P(None, "mp"),
            P("mp", None),
            P(),
            P(),
        ),
        out_specs=(
            P(dp, None, None),
            P(dp, None),
            P(),
            P(None, "mp"),
            P(None, "mp"),
            P(None, "mp"),
            P("mp", None),
            P(None, "mp"),
            P(),
            P(None, "mp"),
            P(None, "mp"),
            P("mp", None),
            P(),
            P(),
        ),
        check_vma=False,
    )
```

```python
import functools
import math

import jax
import jax.numpy as jnp
import numpy as np
from jax import lax
from jax.experimental import pallas as pl
from jax.experimental.pallas import tpu as pltpu
from jax.sharding import Mesh
from jax.sharding import PartitionSpec as P

f32 = jnp.float32
bf16 = jnp.bfloat16
eps = 1e-06
masked_logit = -1e30
gelu_c = math.sqrt(2.0 / math.pi)
CORE, XBIT, YBIT = "core", "x", "y"
group = ("y", "x", "core")
dp = ("out",) + group
span = 1024
tile = 128


def bucket_hot(buckets, length):
    column = np.arange(span)
    base = length - tile
    offset = np.where(column < base + length, column - base, column - span - base)
    distance = np.abs(offset)
    far = 8 + sum((distance >= t).astype(np.int32) for t in (12, 16, 23, 32, 46, 64, 91))
    bucket = np.where(distance < 8, distance, far) + 16 * (offset > 0)
    hot = (bucket[None, :] == np.arange(tile)[:, None]) & (np.arange(tile)[:, None] < buckets)
    return hot.astype(np.float32)


def dot(a, b, dims=((1,), (0,))):
    return lax.dot_general(a, b, (dims, ((), ())), preferred_element_type=f32)


def rms_scale(v):
    return lax.rsqrt(jnp.mean(v * v, axis=-1, keepdims=True) + eps)


def rms_back(v, gain, grad):
    s = rms_scale(v)
    w = grad * gain
    value = s * w - v * ((s * s * s) * jnp.mean(w * v, axis=-1, keepdims=True))
    return value, jnp.sum(grad * v * s, axis=0, keepdims=True)


def whole(shape):
    return pl.BlockSpec(shape, lambda *_: (0,) * len(shape))


ANY = pl.BlockSpec(memory_space=pl.ANY)
token_shape = (8, 128)


def launch(
    kernel, name, args, in_specs, out_specs, out_shape, grid=(1,), offs=None, scratch=(),
    cost=None, after=(), alias=None, n_alias=1, mib=16,
):
    first = 0 if offs is None else 1
    n_in, n_out, n_after = first + len(args), len(out_shape), len(after)

    def body(*refs):
        ins, rest = refs[:n_in], refs[n_in + n_after :]
        outs, token, own = rest[:n_out], rest[n_out], rest[n_out + 1 :]
        token[...] = jnp.zeros(token_shape, f32)
        kernel(*ins, *outs, *own)

    specs = dict(
        grid=grid,
        in_specs=list(in_specs) + [ANY] * n_after,
        out_specs=list(out_specs) + [whole(token_shape)],
        scratch_shapes=list(scratch),
    )
    if offs is None:
        specs = dict(specs)
        scalars = []
    else:
        specs = dict(grid_spec=pltpu.PrefetchScalarGridSpec(num_scalar_prefetch=1, **specs))
        scalars = [offs]
    *outs, token = pl.pallas_call(
        body,
        out_shape=list(out_shape) + [jax.ShapeDtypeStruct(token_shape, f32)],
        input_output_aliases=(
            {} if alias is None else {alias + first + i: i for i in range(n_alias)}
        ),
        compiler_params=pltpu.CompilerParams(
            vmem_limit_bytes=mib << 20, dimension_semantics=("arbitrary",)
        ),
        cost_estimate=cost or cheap,
        name=name,
        **specs,
    )(*scalars, *args, *after)
    return outs, token


cheap = pl.CostEstimate(flops=1 << 20, bytes_accessed=1 << 16, transcendentals=0)


def cost(flops, mib, transcendentals=0):
    return pl.CostEstimate(
        flops=flops, bytes_accessed=mib << 20, transcendentals=transcendentals
    )


def like(dtype, *shapes):
    return [jax.ShapeDtypeStruct(shape, dtype) for shape in shapes]


class Place:
    def __init__(self):
        self.n_out, self.n_mp = lax.axis_size("out"), lax.axis_size("mp")
        self.c, self.x, self.y = (lax.axis_index(name) for name in ("core", "x", "y"))
        self.z = lax.axis_index("mp")
        self.p = self.c * 4 + self.y * 2 + self.x

    def swap(self, v, name):
        return lax.ppermute(v, name, [(0, 1), (1, 0)])

    def shift(self, v, k):
        n = self.n_mp
        return lax.ppermute(v, "mp", [(i, (i + k) % n) for i in range(n)])

    def offsets(self, rows):
        half = rows // 2
        out = []
        for flip in (0, 4):
            p = self.p ^ flip
            for other, extra in (
                (0, 0), (1, 0), (0, half), (2, half), (2, 0), (3, 0), (1, half), (3, half),
            ):
                out.append((p ^ other) * rows + extra)
        return jnp.stack(out + [self.z, self.c, self.x, self.y]).astype(jnp.int32)

    def both_ways(self, right, left):
        n = self.n_mp
        right = lax.ppermute(right, "mp", [(i, i + 1) for i in range(n - 1)])
        return right, lax.ppermute(left, "mp", [(i + 1, i) for i in range(n - 1)])

    def first_round(self, a, b, after=()):
        return stack_pairs(a, self.swap(a, XBIT), b, self.swap(b, YBIT), after)

    def second_round(self, sa, sb, after=()):
        ya, xb = self.swap(sa, YBIT), self.swap(sb, XBIT)
        if after:
            ya, xb = relay([ya, xb], after)
        near = [sa, sb, ya, xb]
        return near + [self.swap(t, CORE) for t in near]


def pick(v, axis, index):
    return lax.dynamic_index_in_dim(v, index, axis, keepdims=False)


def halves(v, axis):
    half = v.shape[axis] // 2
    return (
        lax.slice_in_dim(v, 0, half, axis=axis),
        lax.slice_in_dim(v, half, 2 * half, axis=axis),
    )


def chunk_copies(offs, own, arrays, dst, sems, first=0, slot=0):
    slots, rows, width = dst.shape
    half = rows // 16
    skip = 0 if slot else 1
    pairs = [
        (ref, dst.at[0, :, pl.ds(column, ref.shape[1])]) for ref, column in own
    ]
    for at in range(16):
        src = arrays[at // 2].at[at % 2, pl.ds(slot + skip - 1, slots - skip)]
        if src.shape[2] != width:
            src = src.at[:, :, pl.ds(first, width)]
        start = pl.multiple_of(offs[at], 16)
        pairs.append((src, dst.at[pl.ds(skip, slots - skip), pl.ds(start, half), :]))
    return [pltpu.make_async_copy(s, d, sems.at[i]) for i, (s, d) in enumerate(pairs)]


copies_per_chunk = 20


def gathered_copies(gathered, dst, sems, shard=None):
    full = gathered.shape[4]
    out = []
    for at, (c, y, x) in enumerate(np.ndindex(2, 2, 2)):
        rows = pl.ds(at * full, full)
        if shard is None:
            out.append((gathered.at[y, x, c], dst.at[:, rows, :]))
        else:
            out.append((gathered.at[y, x, c, shard], dst.at[rows, :]))
    return [pltpu.make_async_copy(s, d, sems.at[i]) for i, (s, d) in enumerate(out)]


def split_kernel(sc, v_ref, *refs):
    *others, a_ref, b_ref = refs
    half = a_ref.shape[1]
    n, _, width = v_ref.shape
    for k in range(1, n):
        at = lax.rem(sc[16] + n - k, n)
        a_ref[k - 1, :, :width] = v_ref[at, :half, :]
        b_ref[k - 1, :, :width] = v_ref[at, half:, :]
        a_ref[k - 1, :, width:] = others[k - 1][:half, :]
        b_ref[k - 1, :, width:] = others[k - 1][half:, :]


def split(offs, v, others, after=()):
    n, rows, width = v.shape
    out = (n - 1, rows // 2, width + others[0].shape[1])
    return launch(
        split_kernel, "split", [v, *others], [whole(x.shape) for x in (v, *others)],
        [whole(out)] * 2, like(bf16, out, out), offs=offs, after=after,
    )


def relay_kernel(*refs):
    half = len(refs) // 2
    for a, b in zip(refs[:half], refs[half:]):
        b[...] = a[...]


def relay(arrays, after):
    specs = [whole(a.shape) for a in arrays]
    return launch(
        relay_kernel, "relay", arrays, specs, specs,
        [jax.ShapeDtypeStruct(a.shape, a.dtype) for a in arrays], after=after,
    )[0]


def collect_kernel(step, n, sc, right, left, own, *refs):
    out, rest, *on = refs
    length = out.shape[1]
    side = pl.program_id(0)
    z = sc[16]

    @pl.when((side == 0) & (z >= step))
    def _():
        out[0] = right[:length, :].astype(f32)
        rest[0] = right[length:, :]

    @pl.when((side == 1) & (z + step < n))
    def _():
        out[0] = left[:length, :].astype(f32)
        rest[0] = left[length:, :]

    @pl.when(((side == 0) & (z < step)) | ((side == 1) & (z + step >= n)))
    def _():
        out[0] = own[:length, :].astype(f32)
        rest[0] = own[length:, :]

    @pl.when(side == 0)
    def _():
        for new, old in zip(on, (right, left)):
            new[...] = old[...]


def collect(step, n, offs, right, left, own, so_far, after):
    rows, d = own.shape
    length = rows // tile * tile

    def index(i, sc):
        z = sc[16]
        near, far = jnp.where(z >= step, z - step, z), jnp.where(z + step < n, z + step, z)
        return (jnp.where(i == 0, near, far), 0, 0)

    goes_on = step < n - 1
    kept = list(so_far or ())
    shapes = [(n, length, d), (n, rows - length, d)]
    out_shape = like(f32, shapes[0]) + like(bf16, shapes[1])
    out_specs = [pl.BlockSpec((1,) + shape[1:], index) for shape in shapes]
    if goes_on:
        out_shape += like(bf16, own.shape, own.shape)
        out_specs += [whole(own.shape)] * 2

    def kernel(sc, right, left, own, *refs):
        collect_kernel(step, n, sc, right, left, own, *refs[len(kept) :])

    return launch(
        kernel, f"collect{step}", [right, left, own, *kept],
        [whole(own.shape)] * 3 + [ANY] * len(kept), out_specs, out_shape, grid=(2,), offs=offs,
        after=after, alias=3 if kept else None, n_alias=2,
    )


def skew(base):
    t = jnp.broadcast_to(base, (8, span))
    row = lax.broadcasted_iota(jnp.int32, (8, span), 0)
    for step in (1, 2, 4):
        t = jnp.where((row & step) != 0, pltpu.roll(t, step, 1), t)
    while t.shape[0] < tile:
        t = jnp.concatenate([t, pltpu.roll(t, t.shape[0], 1)], axis=0)
    return t


def unskew(t):
    while t.shape[0] > 8:
        n = t.shape[0] // 2
        t = t[:n] + pltpu.roll(t[n:], span - n, 1)
    row = lax.broadcasted_iota(jnp.int32, (8, span), 0)
    for step in (1, 2, 4):
        t = jnp.where((row & step) != 0, pltpu.roll(t, span - step, 1), t)
    return jnp.sum(t, axis=0, keepdims=True)


def fill_mask(mask, segs, pads, seg_cols, row):
    length = mask.shape[0]
    rows = segs.shape[0]
    chosen = lax.broadcasted_iota(jnp.int32, (rows, length), 0) == row
    seg_k = jnp.sum(jnp.where(chosen, segs, 0.0), axis=0, keepdims=True)
    pad_k = jnp.sum(jnp.where(chosen, pads, 0.0), axis=0, keepdims=True)
    code = jnp.where(pad_k == 1.0, seg_k, -1.0)
    lane = lax.broadcasted_iota(jnp.int32, seg_cols.shape, 1)
    seg_q = jnp.sum(jnp.where(lane == row, seg_cols, 0.0), axis=1, keepdims=True)
    q = lax.broadcasted_iota(jnp.int32, (tile, length), 0)
    k = lax.broadcasted_iota(jnp.int32, (tile, length), 1)
    for a in range(length // tile):
        own = seg_q[a * tile : (a + 1) * tile]
        ok = (own == code) | (q + a * tile == k)
        mask[a * tile : (a + 1) * tile, :] = jnp.where(ok, 0.0, masked_logit)


def fill_bias(bias, table, hot, heads):
    base = dot(table, hot[0 : table.shape[1], :])
    for h in range(heads):
        bias[h] = skew(base[h : h + 1, :])


def normalize(x_ref, gain, normed):
    for a in range(x_ref.shape[0] // tile):
        rows = slice(a * tile, (a + 1) * tile)
        v = x_ref[rows, :].astype(f32)
        normed[rows, :] = (v * rms_scale(v) * gain).astype(bf16)


chunk = 32


def head_groups(heads, size):
    per = tile // size
    out = []
    for first in range(0, heads, per):
        members = range(first, min(heads, first + per))
        lanes = slice(first * size, (members[-1] + 1) * size)
        out.append((lanes, [(h, (h - first) * size) for h in members]))
    return out


def only(v, lane, size):
    if v.shape[1] == size:
        return v
    at = lax.broadcasted_iota(jnp.int32, v.shape, 1)
    return jnp.where((at >= lane) & (at < lane + size), v, jnp.zeros_like(v))


def merge(parts, size):
    out = parts[0]
    at = lax.broadcasted_iota(jnp.int32, out.shape, 1)
    for i, part in enumerate(parts[1:]):
        out = jnp.where(at >= (i + 1) * size, part, out)
    return out


def project_heads(normed_ref, w, parts):
    rows = parts[0].shape[1]
    for i, part in enumerate(parts):
        part[...] = dot(
            normed_ref[...], w[i * rows : (i + 1) * rows, :], ((1,), (1,))
        ).astype(bf16)


def softmax_chunks(length):
    for r in range(0, length, chunk):
        at = length - tile - r // tile * tile
        yield slice(r, r + chunk), slice(r % tile, r % tile + chunk), slice(at, at + length)


def attend_kernel(
    first, heads, size, sc, x_ref, seg_ref, pad_ref, segc_ref, gain_ref, w_ref, hot_ref,
    out_ref, normed, query, keys, values, mask, bias, logits, probs, inverse,
):
    length = x_ref.shape[0]
    wide = heads * size
    buckets = 32
    row = lax.rem(sc[16] + first + pl.program_id(0), seg_ref.shape[0])
    normalize(x_ref, gain_ref[...], normed)
    project_heads(normed, w_ref, (query, keys, values))
    fill_mask(mask, seg_ref[...], pad_ref[...], segc_ref[...], row)

    @pl.when(pl.program_id(0) == 0)
    def _():
        fill_bias(bias, w_ref[3 * wide : 3 * wide + 16, :tile][:, :buckets], hot_ref, heads)

    for lanes, members in head_groups(heads, size):
        parts = []
        for i, (h, lane) in enumerate(members):
            logits[i % 2] = dot(only(query[:, lanes], lane, size), keys[:, lanes], ((1,), (1,)))
            for rows, inner, at in softmax_chunks(length):
                v = logits[i % 2, rows, :] + bias[h, inner, at] + mask[rows, :]
                e = jnp.exp(v - jnp.max(v, axis=1, keepdims=True))
                total = jnp.sum(e, axis=1, keepdims=True)
                inverse[rows, :] = jnp.broadcast_to(1.0 / total, (chunk, tile))
                probs[i % 2, rows, :] = e.astype(bf16)
            part = dot(probs[i % 2], values[:, lanes])
            parts.append(part * inverse[:, : part.shape[1]])
        out_ref[0, :length, lanes] = merge(parts, size).astype(bf16)
    out_ref[0, length:, :] = w_ref[3 * wide : 3 * wide + 16, :wide]


def attend(first, offs, tokens, segs, pads, seg_cols, gain, w_qkv, hot, heads, size, after=()):
    rows, length = segs.shape
    d = tokens.shape[1]
    wide = heads * size
    args = [tokens, segs, pads, seg_cols, gain, w_qkv, hot]
    specs = [pl.BlockSpec((length, d), lambda i, sc: (lax.rem(sc[16] + first + i, rows), 0))]
    return launch(
        functools.partial(attend_kernel, first, heads, size), "attend", args,
        specs + [whole(v.shape) for v in args[1:]],
        [pl.BlockSpec((1, length + 16, wide), lambda i, sc: (i, 0, 0))],
        like(bf16, (rows, length + 16, wide)),
        grid=(rows,), offs=offs,
        scratch=[
            pltpu.VMEM((length, d), bf16),
            pltpu.VMEM((length, wide), bf16),
            pltpu.VMEM((length, wide), bf16),
            pltpu.VMEM((length, wide), bf16),
            pltpu.VMEM((length, length), f32),
            pltpu.VMEM((heads, tile, span), f32),
            pltpu.VMEM((2, length, length), f32),
            pltpu.VMEM((2, length, length), bf16),
            pltpu.VMEM((length, tile), f32),
        ],
        cost=cost(
            rows * (6 * length * d * wide + 4 * wide * length * length), 4,
            rows * heads * length * length,
        ),
        after=after,
    )


def high_low(v):
    high = v.astype(bf16)
    return high, (v - high.astype(f32)).astype(bf16)


def attend_back_slot(
    heads, size, mixed_ref, gm_ref, hot_ref, w, left_ref, table_out, acc,
    normed, query, keys, values, mask, bias, logits, gprobs, probs, dlog, skewed, diag,
):
    length = normed.shape[0]
    wide = heads * size
    fill_bias(bias, mixed_ref[length:, :tile][:, :32], hot_ref, heads)
    project_heads(normed, w, (query, keys, values))
    for lanes, members in head_groups(heads, size):
        q, k, v = query[:, lanes], keys[:, lanes], values[:, lanes]
        grad = gm_ref[:, lanes]
        results = []
        for h, lane in members:
            logits[...] = dot(only(q, lane, size), k, ((1,), (1,)))
            gprobs[...] = dot(only(grad, lane, size), v, ((1,), (1,)))
            skewed[...] = jnp.zeros_like(skewed)
            for rows, inner, at in softmax_chunks(length):
                t = logits[rows, :] + bias[h, inner, at] + mask[rows, :]
                e = jnp.exp(t - jnp.max(t, axis=1, keepdims=True))
                p = e * (1.0 / jnp.sum(e, axis=1, keepdims=True))
                probs[rows, :] = p.astype(bf16)
                gp = gprobs[rows, :]
                gl = p * (gp - jnp.sum(gp * p, axis=1, keepdims=True))
                dlog[rows, :] = gl.astype(bf16)
                skewed[inner, at] += gl
            diag[h : h + 1, :] = unskew(skewed[...])
            results.append(
                (
                    dot(dlog[...], k),
                    dot(dlog[...], q, ((0,), (0,))),
                    dot(probs[...], grad, ((0,), (0,))),
                )
            )
        for part in range(3):
            merged = merge([r[part] for r in results], size)
            left_ref[part, :, lanes] = merged.astype(bf16)
    left_ref[3] = mixed_ref[:length, :]
    high, low = high_low(diag[...])
    table = dot(high, hot_ref[...], ((1,), (1,))) + dot(low, hot_ref[...], ((1,), (1,)))
    table_out[...] = table
    value = sum(
        dot(left_ref[part], w[part * wide : (part + 1) * wide, :]) for part in range(3)
    )
    acc[...] += value


def attend_back_kernel(
    first, count, last, heads, size, sc, x_ref, seg_ref, pad_ref, segc_ref, gain_ref, hot_ref,
    gm_ref, *refs,
):
    mixed_refs, refs = refs[:count], list(refs[count:])
    acc_in = refs.pop(0) if first else None
    if last:
        gha_ref, gat_ref, fin_ref, mid_ref, score_ref = refs[:5]
        refs = refs[5:]
        tables = [refs.pop(0)] if first else []
    w_ref = refs[0]
    refs = refs[1 + (1 if first else 0) :]
    left_ref, table_out = refs[:2]
    if last:
        dx_ref, both_ref, small_ref, acc = refs[2:6]
        refs = refs[6:]
    else:
        acc, refs = refs[2], refs[3:]
    (
        w, sems, normed, query, keys, values, mask, bias, logits, gprobs, probs, dlog, skewed, diag,
    ) = refs
    length, d = x_ref.shape
    wide = heads * size
    row = sc[16]
    gain = gain_ref[...]
    blocks = length // tile
    copies = [
        gathered_copies(w_ref, w.at[i], sems.at[i], lax.rem(row + 4 - first - i, 4))
        for i in range(count)
    ]
    for copy in sum(copies, []):
        copy.start()
    normalize(x_ref, gain, normed)
    fill_mask(mask, seg_ref[...], pad_ref[...], segc_ref[...], row)
    diag[...] = jnp.zeros_like(diag)
    if acc_in is None:
        acc[...] = jnp.zeros_like(acc)
    else:
        acc[...] = acc_in[...]
    for i in range(count):
        for copy in copies[i]:
            copy.wait()
        attend_back_slot(
            heads, size, mixed_refs[i], gm_ref.at[i], hot_ref, w.at[i], left_ref.at[i],
            table_out.at[8 * i : 8 * i + 8], acc,
            normed, query, keys, values, mask, bias, logits, gprobs, probs, dlog, skewed, diag,
        )
    if not last:
        return
    total = jnp.zeros((1, d), f32)
    for a in range(blocks):
        rows = slice(a * tile, (a + 1) * tile)
        back, part = rms_back(x_ref[rows, :].astype(f32), gain, acc[rows, :])
        dx_ref[rows, :] = (gha_ref[rows, :] + back).astype(bf16)
        total = total + part
    both_ref[0] = normed[...]
    both_ref[1] = gat_ref[...]
    dx_ref[length:, :] = jnp.zeros((dx_ref.shape[0] - length, d), bf16)
    n = score_ref.shape[0] // 16
    cols = score_ref.shape[1]
    high, low = high_low(score_ref[...])
    for i in range(n):
        rows = slice(16 * i, 16 * i + 16)
        dx_ref[length : length + 16, 2 * i * tile : 2 * i * tile + cols] = high[rows]
        dx_ref[length : length + 16, (2 * i + 1) * tile : (2 * i + 1) * tile + cols] = low[rows]
    line = lax.broadcasted_iota(jnp.int32, (8, d), 0)
    gains = jnp.where(
        line == 0, total, jnp.where(line == 1, fin_ref[...], jnp.where(line == 2, mid_ref[...], 0.0))
    )
    line = lax.broadcasted_iota(jnp.int32, (8, tile), 0)
    column = lax.broadcasted_iota(jnp.int32, (8, tile), 1)

    def turned(value, at):
        place = jnp.where(column == line + at, 1.0, 0.0).astype(bf16)
        high, low = high_low(value)
        return dot(high, place, ((0,), (0,))) + dot(low, place, ((0,), (0,)))

    gains = turned(gains, 0)
    tables = [t[8 * i : 8 * i + 8] for t in tables + [table_out] for i in range(t.shape[0] // 8)]
    for k, value in enumerate(tables):
        small_ref[k] = gains.astype(bf16)
        small_ref[k, 0:tile, :] = (gains[0:tile] + turned(value, tile // 2)).astype(bf16)


def attend_back(
    first, count, common, grad_mixed, mixed, acc, left, finish, weights, heads, size, after=()
):
    offs, *shared = common
    rows, length = shared[1].shape
    d = shared[0].shape[1]
    slots = grad_mixed.shape[0]
    wide = heads * size
    last = first + count == slots
    mixed = mixed[first : first + count]
    args = [*shared, grad_mixed, *mixed]
    specs = [pl.BlockSpec((length, d), lambda i, sc: (sc[16], 0))]
    specs += [whole(v.shape) for v in shared[1:]]
    specs.append(pl.BlockSpec((count, length, wide), lambda i, sc: (first // count, 0, 0)))
    specs += [whole(m.shape) for m in mixed]
    if first:
        args.append(acc)
        specs.append(whole(acc.shape))
    if last:
        args += finish
        specs += [whole(v.shape) for v in finish]
    args += [weights] + ([left] if first else [])
    specs += [ANY] * (2 if first else 1)
    out_specs = [
        pl.BlockSpec((count, 4, length, wide), lambda i, sc: (first // count, 0, 0, 0)),
        whole((8 * count, tile)),
    ]
    out_shape = like(bf16, (slots, 4, length, wide)) + like(f32, (8 * count, tile))
    scratch = []
    if last:
        shapes = ((length + 16, d), (2, length, d), (slots, d, tile))
        out_specs += [whole(shape) for shape in shapes]
        out_shape += like(bf16, *shapes)
        scratch = [pltpu.VMEM((length, d), f32)]
    else:
        out_specs.append(whole((length, d)))
        out_shape += like(f32, (length, d))
    return launch(
        functools.partial(attend_back_kernel, first, count, last, heads, size),
        f"attend_back{first}",
        args, specs, out_specs, out_shape, offs=offs,
        scratch=scratch
        + [
            pltpu.VMEM((count, 8 * weights.shape[4], d), bf16),
            pltpu.SemaphoreType.DMA((count, 8)),
            pltpu.VMEM((length, d), bf16),
            pltpu.VMEM((length, wide), bf16),
            pltpu.VMEM((length, wide), bf16),
            pltpu.VMEM((length, wide), bf16),
            pltpu.VMEM((length, length), f32),
            pltpu.VMEM((heads, tile, span), f32),
            pltpu.VMEM((length, length), f32),
            pltpu.VMEM((length, length), f32),
            pltpu.VMEM((length, length), bf16),
            pltpu.VMEM((length, length), bf16),
            pltpu.VMEM((tile, span), f32),
            pltpu.VMEM((8, span), f32),
        ],
        cost=cost(
            count * (12 * length * d * wide + 14 * wide * length * length), 16,
            count * heads * length * length,
        ),
        after=after, alias=len(args) - 1 if first else None, mib=32,
    )


def gate_up(normed_ref, w, act_ref, dact_ref, inner_ref):
    hidden = act_ref.shape[2]
    for n in range(hidden // 256):
        cols = slice(n * 256, (n + 1) * 256)
        normed = normed_ref[...]
        gate = dot(normed, w[:, cols])
        up = dot(normed, w[:, hidden + n * 256 : hidden + (n + 1) * 256])
        t = jnp.tanh(gelu_c * (gate + 0.044715 * gate * gate * gate))
        half = 0.5 * (1.0 + t)
        act = gate * half
        slope = half + 0.5 * gate * (1.0 - t * t) * (
            gelu_c * (1.0 + 3 * 0.044715 * gate * gate)
        )
        act_ref[0, :, cols] = act.astype(bf16)
        dact_ref[0, :, cols] = (up * slope).astype(bf16)
        inner_ref[0, :, cols] = (act * up).astype(bf16)


def forward_kernel(
    sc, x_ref, gain_ref, gain_l_ref, wp_ref, padc_ref, query_ref, cot_ref, top_ref, *refs
):
    slots = 4
    mixed, own, arrays = refs[:slots], refs[slots : slots + 4], refs[slots + 4 : slots + 12]
    hid_ref, normed_ref, act_ref, dact_ref, inner_ref = refs[slots + 12 : slots + 17]
    score_ref, nfin, ge, total_ref, gft_ref, ghf_ref = refs[slots + 17 : slots + 23]
    w, wd, wo, w_sems, d_sems, o_sems, acc, embed, unit = refs[slots + 23 :]
    length, d = x_ref.shape
    hidden = act_ref.shape[2]
    step = pl.program_id(0)
    blocks = length // tile
    w_copies = chunk_copies(sc, zip(own, (0, hidden)), arrays, w, w_sems)
    d_copies = chunk_copies(sc, [(own[2], 0)], arrays, wd, d_sems, 2 * hidden)
    o_copies = chunk_copies(sc, [(own[3], 0)], arrays, wo, o_sems, 3 * hidden)

    @pl.when(step == 0)
    def _():
        for copy in o_copies + w_copies[:2] + d_copies[:1] + w_copies[2:] + d_copies[1:]:
            copy.start()
        for copy in o_copies:
            copy.wait()
        gain = gain_ref[...]
        for a in range(blocks):
            rows = slice(a * tile, (a + 1) * tile)
            h = x_ref[rows, :].astype(f32)
            for k in range(slots):
                h = h + dot(mixed[k][rows, :], wo[k], ((1,), (1,)))
            hid_ref[rows, :] = h
            acc[rows, :] = h
            normed_ref[rows, :] = (h * rms_scale(h) * gain).astype(bf16)
        for copy in w_copies[:2] + d_copies[:1]:
            copy.wait()

    @pl.when(step == 1)
    def _():
        for copy in w_copies[2:] + d_copies[1:]:
            copy.wait()

    gate_up(normed_ref, w.at[step], act_ref, dact_ref, inner_ref)
    acc[...] += dot(inner_ref[0], wd[step])

    @pl.when(step == slots - 1)
    def _():
        lane = lax.broadcasted_iota(jnp.int32, padc_ref.shape, 1)
        pad = jnp.sum(jnp.where(lane == sc[16], padc_ref[...], 0.0), axis=1, keepdims=True)
        gain = gain_l_ref[...]
        for a in range(blocks):
            rows = slice(a * tile, (a + 1) * tile)
            h = acc[rows, :]
            n = (h * rms_scale(h) * gain).astype(bf16)
            nfin[rows, :] = n
            e = dot(n, wp_ref[...])
            embed[rows, :] = e
            inverse = lax.rsqrt(jnp.sum(e * e, axis=1, keepdims=True) + eps)
            unit[rows, :] = (e * inverse * pad[rows]).astype(bf16)
        query = query_ref[0]
        cot = cot_ref[0]
        top = top_ref[0]
        scored = dot(query, unit[...], ((1,), (1,)))
        place = lax.broadcasted_iota(jnp.int32, scored.shape, 1)
        out_lane = lax.broadcasted_iota(jnp.int32, cot.shape, 1)
        chosen = jnp.zeros_like(cot)
        weight = jnp.zeros_like(scored)
        for j in range(top.shape[1]):
            here = place == top[:, j : j + 1]
            mine = jnp.sum(jnp.where(here, scored, 0.0), axis=1, keepdims=True)
            chosen = jnp.where(out_lane == j, mine, chosen)
            weight = weight + jnp.where(here, cot[:, j : j + 1], 0.0)
        score_ref[...] = chosen
        high, low = high_low(weight)
        gunit = dot(high, query, ((0,), (0,))) + dot(low, query, ((0,), (0,)))
        total = jnp.zeros((1, d), f32)
        for a in range(blocks):
            rows = slice(a * tile, (a + 1) * tile)
            e = embed[rows, :]
            inverse = lax.rsqrt(jnp.sum(e * e, axis=1, keepdims=True) + eps)
            u = gunit[rows] * pad[rows]
            cube = (inverse * inverse * inverse) * jnp.sum(u * e, axis=1, keepdims=True)
            g = (inverse * u - e * cube).astype(bf16)
            ge[rows, :] = g
            back, part = rms_back(acc[rows, :], gain, dot(g, wp_ref[...], ((1,), (1,))))
            total = total + part
            ghf_ref[rows, :] = back
            gft_ref[rows, :] = back.astype(bf16)
        total_ref[...] = total


def forward(
    offs, tokens, gain, gain_l, w_proj, pad_cols, query, cot, top, mixed, own, arrays, length
):
    d = tokens.shape[1]
    slots = len(mixed)
    hidden = own[0].shape[1]
    wide = own[3].shape[1]
    e = w_proj.shape[1]
    three = (slots, length, hidden)
    score, low, embed, total = cot.shape[1:], (length, d), (length, e), (1, d)
    per_slot = pl.BlockSpec((1, length, hidden), lambda i, sc: (i, 0, 0))

    def row_block(v):
        return pl.BlockSpec((1,) + v.shape[1:], lambda i, sc: (sc[16], 0, 0))

    return launch(
        forward_kernel, "forward",
        [tokens, gain, gain_l, w_proj, pad_cols, query, cot, top, *mixed, *own, *arrays],
        [pl.BlockSpec((length, d), lambda i, sc: (sc[16], 0))]
        + [whole(v.shape) for v in (gain, gain_l, w_proj, pad_cols)]
        + [row_block(v) for v in (query, cot, top)]
        + [whole(m.shape) for m in mixed]
        + [ANY] * 12,
        [whole(low), whole(low)] + [per_slot] * 3
        + [whole(v) for v in (score, low, embed, total, low, low)],
        like(f32, low) + like(bf16, low, three, three, three) + like(f32, score)
        + like(bf16, low, embed) + like(f32, total) + like(bf16, low) + like(f32, low),
        grid=(slots,), offs=offs,
        scratch=[
            pltpu.VMEM((slots, d, 2 * hidden), bf16),
            pltpu.VMEM((slots, hidden, d), bf16),
            pltpu.VMEM((slots, d, wide), bf16),
            pltpu.SemaphoreType.DMA((copies_per_chunk,)),
            pltpu.SemaphoreType.DMA((copies_per_chunk,)),
            pltpu.SemaphoreType.DMA((copies_per_chunk,)),
            pltpu.VMEM((length, d), f32),
            pltpu.VMEM((length, e), f32),
            pltpu.VMEM((length, e), bf16),
        ],
        cost=cost(2 * length * d * (d + 3 * slots * hidden), 24, slots * length * hidden),
        mib=58,
    )


def ffn_back_kernel(sc, hid_ref, gft_ref, ghf_ref, act_ref, dact_ref, gain_ref, *refs):
    slots = 4
    own, arrays, refs = refs[:4], refs[4:12], refs[12:]
    gg_ref, gu_ref, gha_ref, gat_ref, gm_ref, total_ref, w, wd, wo, w_sems, d_sems, acc = refs
    length, d = hid_ref.shape
    hidden = wd.shape[1]
    step = pl.program_id(0)
    w_copies = chunk_copies(sc, zip(own, (0, hidden)), arrays, w, w_sems.at[0])
    w_copies += chunk_copies(sc, [(own[3], 0)], arrays, wo, w_sems.at[1], 3 * hidden)
    d_copies = chunk_copies(sc, [(own[2], 0)], arrays, wd, d_sems, 2 * hidden)
    blocks = length // tile

    @pl.when(step == 0)
    def _():
        for copy in d_copies[:1] + w_copies[:2] + d_copies[1:] + w_copies[2:]:
            copy.start()
        acc[...] = jnp.zeros_like(acc)
        for copy in d_copies[:1] + w_copies[:2]:
            copy.wait()

    @pl.when(step == 1)
    def _():
        for copy in d_copies[1:] + w_copies[2:]:
            copy.wait()

    def part(n, carry):
        cols = pl.ds(pl.multiple_of(n * 256, 256), 256)
        gi = dot(gft_ref[...], wd[step, cols, :], ((1,), (1,)))
        gg_ref[0, :, cols] = (gi * dact_ref[0, :, cols].astype(f32)).astype(bf16)
        gu_ref[0, :, cols] = (gi * act_ref[0, :, cols].astype(f32)).astype(bf16)
        return carry

    lax.fori_loop(0, hidden // 256, part, 0)
    acc[...] += dot(gg_ref[0], w[step, :, :hidden], ((1,), (1,))) + dot(
        gu_ref[0], w[step, :, hidden : 2 * hidden], ((1,), (1,))
    )

    @pl.when(step == slots - 1)
    def _():
        gain = gain_ref[...]
        total = jnp.zeros((1, d), f32)
        for a in range(blocks):
            rows = slice(a * tile, (a + 1) * tile)
            back, part = rms_back(hid_ref[rows, :], gain, acc[rows, :])
            total = total + part
            g = ghf_ref[rows, :] + back
            gha_ref[rows, :] = g
            g = g.astype(bf16)
            gat_ref[rows, :] = g
            for k in range(slots):
                gm_ref[k, rows, :] = dot(g, wo[k]).astype(bf16)
        total_ref[...] = total


def ffn_back(offs, hid, gft, ghf, act, dact, gain, own, arrays, after=()):
    length, d = hid.shape
    slots, _, hidden = act.shape
    wide = own[3].shape[1]
    mixed = (slots, length, wide)
    block = pl.BlockSpec((1, length, hidden), lambda i, sc: (i, 0, 0))
    return launch(
        ffn_back_kernel, "ffn_back",
        [hid, gft, ghf, act, dact, gain, *own, *arrays],
        [whole(v.shape) for v in (hid, gft, ghf)] + [block] * 2 + [whole(gain.shape)] + [ANY] * 12,
        [block, block] + [whole(v) for v in (hid.shape, hid.shape, mixed, (1, d))],
        like(bf16, act.shape, act.shape) + like(f32, hid.shape) + like(bf16, hid.shape, mixed)
        + like(f32, (1, d)),
        grid=(slots,), offs=offs,
        scratch=[
            pltpu.VMEM((slots, d, 2 * hidden), bf16),
            pltpu.VMEM((slots, hidden, d), bf16),
            pltpu.VMEM((slots, d, wide), bf16),
            pltpu.SemaphoreType.DMA((2, copies_per_chunk)),
            pltpu.SemaphoreType.DMA((copies_per_chunk,)),
            pltpu.VMEM((length, d), f32),
        ],
        cost=cost(2 * length * d * (3 * slots * hidden + d), 24),
        after=after, mib=42,
    )


def keep_parts(sc, out, refs):
    send_a, keep_a, send_b, keep_b = refs
    half = send_a.shape[2]
    x, y = sc[18], sc[19]

    def rows(y, x, extra):
        at = pl.multiple_of((2 * y + x) * (2 * half) + extra, 16)
        return out[pl.ds(at, half), :]

    for other in range(2):
        send_a[0, other] = rows(other, 1 - x, 0)
        keep_a[0, other] = rows(other, x, 0)
        send_b[0, other] = rows(1 - y, other, half)
        keep_b[0, other] = rows(y, other, half)


def parts_of(slots, rows, width):
    part = (1, 2, rows // 8, width)
    spec = pl.BlockSpec(part, lambda i, sc: (i, 0, 0, 0))
    return [spec] * 4, [jax.ShapeDtypeStruct((slots,) + part[1:], bf16)] * 4


def product_kernel(lefts, pairs, keep, sc, *refs):
    left_refs, right_refs = refs[:lefts], refs[lefts : lefts + len(pairs)]
    refs = refs[lefts + len(pairs) :]
    out = refs[-1] if keep else refs[-1].at[0]
    at = 0
    for right_ref, which in zip(right_refs, pairs):
        right = right_ref[...]
        left = left_refs[which][...]
        left, right = (v.reshape(v.shape[-2:]) for v in (left, right))
        cols = slice(at, at + right.shape[1])
        value = dot(left, right, ((0,), (0,)))
        if keep:
            value = value + refs[0][0, :, cols].astype(f32)
        out[:, cols] = value.astype(bf16)
        at += right.shape[1]
    if keep:
        keep_parts(sc, out, refs[-5:-1])


def products(offs, lefts, rights, slots, got=None, after=(), mib=16):
    keep = got is not None
    length, half = lefts[0].shape[-2], lefts[0].shape[-1] // 2
    width = sum(right.shape[-1] for right, _ in rights)

    def which(sc):
        return sc[17] if keep else 1 - sc[17]

    specs = []
    for left in lefts:
        if left.ndim == 3:
            specs.append(pl.BlockSpec((1, length, half), lambda i, sc: (i, 0, which(sc))))
        else:
            specs.append(pl.BlockSpec((length, half), lambda i, sc: (0, which(sc))))
    for right, _ in rights:
        if right.ndim == 3:
            specs.append(pl.BlockSpec((1,) + right.shape[1:], lambda i, sc: (i, 0, 0)))
        else:
            specs.append(whole(right.shape))
    args = list(lefts) + [right for right, _ in rights]
    block = pl.BlockSpec((1, half, width), lambda i, sc: (i, 0, 0))
    out_specs, out_shape, scratch = [block], like(bf16, (slots, half, width)), []
    if keep:
        specs.append(block)
        args.append(got)
        out_specs, out_shape = parts_of(slots, half, width)
        scratch = [pltpu.VMEM((half, width), bf16)]
    return launch(
        functools.partial(product_kernel, len(lefts), [i for _, i in rights], keep),
        "products_keep" if keep else "products_send",
        args, specs, out_specs, out_shape, grid=(slots,), offs=offs, scratch=scratch, after=after,
        mib=mib,
    )


def attn_product_kernel(keep, sc, la, lb, ra, rb, small, *refs):
    out = refs[-1] if keep else refs[-1].at[0]
    quarter, d = la.shape[3], ra.shape[2]
    for left, right, at in ((la, ra, 0), (lb, rb, quarter)):
        value = dot(left[0, 0], right[0], ((0,), (0,)))
        if keep:
            value = value + refs[0][0, at : at + quarter, :d].astype(f32)
        out[at : at + quarter, :d] = value.astype(bf16)
    value = small[0]
    if keep:
        value = add(value, refs[0][0, :, d:])
    out[:, d:] = value
    if keep:
        keep_parts(sc, out, refs[1:5])


def attn_products(offs, left, both, small, got=None, after=()):
    keep = got is not None
    slots, _, length, quarter = left.shape
    d = both.shape[2]
    width = d + small.shape[2]
    half = 2 * quarter

    def which(sc):
        return sc[17] if keep else 1 - sc[17]

    block = pl.BlockSpec((1, half, width), lambda i, sc: (i, 0, 0))
    specs = [
        pl.BlockSpec((1, 1, length, quarter), lambda i, sc: (i, 2 * which(sc), 0, 0)),
        pl.BlockSpec((1, 1, length, quarter), lambda i, sc: (i, 2 * which(sc) + 1, 0, 0)),
        pl.BlockSpec((1, length, d), lambda i, sc: (0, 0, 0)),
        pl.BlockSpec((1, length, d), lambda i, sc: (which(sc), 0, 0)),
        pl.BlockSpec((1, half, small.shape[2]), lambda i, sc: (i, which(sc), 0)),
    ]
    args = [left, left, both, both, small]
    out_specs, out_shape, scratch = [block], like(bf16, (slots, half, width)), []
    if keep:
        specs.append(block)
        args.append(got)
        out_specs, out_shape = parts_of(slots, half, width)
        scratch = [pltpu.VMEM((half, width), bf16)]
    return launch(
        functools.partial(attn_product_kernel, keep), "attn_keep" if keep else "attn_send",
        args, specs, out_specs, out_shape, grid=(slots,), offs=offs, scratch=scratch, after=after,
        mib=16,
    )


def add(a, b):
    return (a.astype(f32) + b.astype(f32)).astype(bf16)


def second_kernel(sc, ka, ra, kb, rb, send_a, keep_a, send_b, keep_b):
    x, y = sc[18], sc[19]
    send_a[0] = add(ka[0, 1 - y], ra[0, 1 - y])
    keep_a[0] = add(ka[0, y], ra[0, y])
    send_b[0] = add(kb[0, 1 - x], rb[0, 1 - x])
    keep_b[0] = add(kb[0, x], rb[0, x])


def second_sums(offs, *arrays, after=()):
    slots, _, half, width = arrays[0].shape
    into = pl.BlockSpec((1, 2, half, width), lambda i, sc: (i, 0, 0, 0))
    out = pl.BlockSpec((1, half, width), lambda i, sc: (i, 0, 0))
    return launch(
        second_kernel, "second_sums", arrays, [into] * 4, [out] * 4,
        like(bf16, *[(slots, half, width)] * 4), grid=(slots,), offs=offs, after=after,
    )


def third_kernel(ka, ra, kb, rb, *outs):
    half = ka.shape[1]
    for k, out in enumerate(outs):
        out[:half, :] = add(ka[k], ra[k])
        out[half:, :] = add(kb[k], rb[k])


def third_sums(*arrays, after=()):
    slots, half, width = arrays[0].shape
    shape = (2 * half, width)
    return launch(
        third_kernel, "third_sums", arrays, [whole(arrays[0].shape)] * 4, [whole(shape)] * slots,
        like(bf16, *[shape] * slots), after=after,
    )


def third_stacked_kernel(sc, ka, ra, kb, rb, out):
    n, half, _ = ka.shape
    for k in range(n):
        to = lax.rem(sc[16] + n - k, n)
        out[to, :half, :] = add(ka[k], ra[k])
        out[to, half:, :] = add(kb[k], rb[k])


def third_stacked(offs, *arrays, after=()):
    slots, half, width = arrays[0].shape
    shape = (slots, 2 * half, width)
    (out,), token = launch(
        third_stacked_kernel, "third_stacked", arrays, [whole(arrays[0].shape)] * 4,
        [whole(shape)], like(bf16, shape), offs=offs, after=after,
    )
    return out, token


def last_kernel(*refs):
    t = [ref[...].astype(f32) for ref in refs[:4]]
    refs[4][...] = ((t[0] + t[2]) + (t[1] + t[3])).astype(refs[4].dtype)


def last_sum(arrays, dtype, after=()):
    shape = arrays[0].shape
    return launch(
        last_kernel, "last_sum", arrays, [whole(shape)] * 4, [whole(shape)], like(dtype, shape),
        after=after,
    )


def stack_kernel(a, xa, b, yb, sa, sb):
    sa[0], sa[1], sb[0], sb[1] = a[...], xa[...], b[...], yb[...]


def stack_pairs(a, xa, b, yb, after):
    out = (2,) + a.shape
    return launch(
        stack_kernel, "stack_pairs", [a, xa, b, yb], [whole(a.shape)] * 4, [whole(out)] * 2,
        like(bf16, out, out), after=after,
    )


class Reduce:
    def __init__(self, place, offs, kept):
        self.place, self.offs, self.kept = place, offs, kept

    def first(self, after=()):
        send_a, keep_a, send_b, keep_b = self.kept
        ra, rb = self.place.swap(send_a, XBIT), self.place.swap(send_b, YBIT)
        self.kept, token = second_sums(self.offs, keep_a, ra, keep_b, rb, after=after)
        return token

    def second(self, after=()):
        send_a, keep_a, send_b, keep_b = self.kept
        ra, rb = self.place.swap(send_a, YBIT), self.place.swap(send_b, XBIT)
        self.kept, token = third_sums(keep_a, ra, keep_b, rb, after=after)
        return token

    def second_and_third(self, after=()):
        send_a, keep_a, send_b, keep_b = self.kept
        ra, rb = self.place.swap(send_a, YBIT), self.place.swap(send_b, XBIT)
        v, token = third_stacked(self.offs, keep_a, ra, keep_b, rb, after=after)
        total = lax.psum_scatter(v, "mp", scatter_dimension=0, tiled=True)
        if self.place.n_out > 1:
            total = lax.psum(total.astype(f32), "out").astype(bf16)
        self.total = total.reshape(v.shape[1:])
        return token

    def third(self, after=()):
        p = self.place
        t = [self.kept[0]] + [p.shift(self.kept[k], -k) for k in range(1, p.n_mp)]
        if p.n_out > 1:
            (total,), token = last_sum(t, f32, after)
            self.total = lax.psum(total, "out").astype(bf16)
        else:
            (self.total,), token = last_sum(t, bf16, after)
        return token


def open_kernel(v_ref, *outs):
    rows = v_ref.shape[3]
    for at, (c, y, x) in enumerate(np.ndindex(2, 2, 2)):
        left = 0
        for out in outs:
            value = v_ref[y, x, c, :, left : left + out.shape[1]]
            out[at * rows : (at + 1) * rows, :] = value.astype(f32)
            left += out.shape[1]


def beside_kernel(a, b, out):
    out[:, : a.shape[1]] = a[...]
    out[:, a.shape[1] :] = b[...]


def gathered(a, b, cuts, start_after, after):
    rows, width = a.shape[0], a.shape[1] + b.shape[1]
    (v,), _ = launch(
        beside_kernel, "beside", [a, b], [whole(a.shape), whole(b.shape)],
        [whole((rows, width))], like(bf16, (rows, width)), after=start_after,
    )
    v = lax.all_gather(v, group, tiled=False).reshape(2, 2, 2, rows, width)
    shapes = [(8 * rows, cut) for cut in cuts]
    return launch(
        open_kernel, "open", [v], [whole(v.shape)], [whole(shape) for shape in shapes],
        like(f32, *shapes), after=after, mib=58,
    )


def unpack_kernel(offs, *refs):
    arrays, outs, small, full = refs[:8], refs[8:-2], refs[-2], refs[-1]
    for at in range(16):
        value = arrays[at // 2][at % 2]
        rows = pl.ds(pl.multiple_of(offs[at], 16), value.shape[0])
        full[rows, :] = value.astype(f32)
    rows, d = outs[0].shape
    for i, out in enumerate(outs):
        out[...] = full[i * rows : (i + 1) * rows, :d]
    small[...] = full[:, d:]


def unpack(offs, arrays, count, small):
    half, width = arrays[0].shape[1:]
    rows, d = 16 * half, width - small
    shapes = [(rows // count, d)] * count + [(rows, small)]
    outs, _ = launch(
        unpack_kernel, "unpack", arrays, [whole(v.shape) for v in arrays],
        [whole(v) for v in shapes], like(f32, *shapes), offs=offs,
        scratch=[pltpu.VMEM((rows, width), f32)],
    )
    return outs


def local(
    tokens, segment_ids, pad_mask, top_index, query_emb, score_cot, gain_attn, w_query, w_key,
    w_value, w_out, rel_table, gain_ffn, w_gate, w_up, w_down, gain_final, w_proj,
):
    place = Place()
    slots = place.n_mp
    rows, length = segment_ids.shape
    d = tokens.shape[1]
    heads = rel_table.shape[1]
    size = w_query.shape[1] // heads
    wide = heads * size
    hot = jnp.asarray(bucket_hot(rel_table.shape[0], length), bf16)
    segs, pads = segment_ids.astype(f32), pad_mask.astype(f32)
    seg_cols, pad_cols = segs.T, pads.T
    gain_a, gain_f, gain_l = (
        g.astype(f32).reshape(1, d) for g in (gain_attn, gain_ffn, gain_final)
    )
    offs = place.offsets(d // 8)

    buckets = rel_table.shape[0]
    table = jnp.zeros((64, d), bf16).at[:heads, :buckets].set(rel_table.T)
    w_qkv = jnp.concatenate([w_query.T, w_key.T, w_value.T, table])
    w_out_t = w_out.T
    eighth = d // 8
    hidden = w_gate.shape[1]

    def piece(*arrays):
        parts = []
        for v in arrays:
            rows = v.shape[0] // 8
            parts.append(lax.dynamic_slice_in_dim(v, place.p * rows, rows, 0))
        return jnp.concatenate(parts, axis=1) if len(parts) > 1 else parts[0]

    common = (offs, tokens, segs, pads, seg_cols, gain_a)
    own = (w_gate, w_up, w_down, w_out_t)
    z1 = lax.all_gather(piece(*own[:2]), "mp")
    piece2 = piece(*own[2:])
    z2 = [place.shift(piece2, k) for k in range(1, slots)]
    (attended,), done = attend(1, *common, w_qkv, hot, heads, size)
    mixed = [attended[slots - 1]] + [place.shift(attended[k - 1], k) for k in range(1, slots)]
    halved, _ = split(offs, z1, z2, (done,))
    s1, _ = place.first_round(*halved)
    arrays = place.second_round(*s1, mixed[1:])
    (hid, normed_ffn, act, dact, inner, score, nfin, ge, gain_fin, gft, ghf), done = forward(
        offs, tokens, gain_f, gain_l, w_proj, pad_cols, query_emb, score_cot, top_index, mixed,
        own, arrays, length,
    )
    all_qkv = lax.all_gather(relay([piece(w_qkv)], (done,))[0], group + ("mp",))
    all_qkv = all_qkv.reshape((2, 2, 2, slots) + all_qkv.shape[-2:])
    down_sides = ([inner, nfin], [(gft, 0), (ge, 1)])
    (send,), _ = products(offs, *down_sides, slots, mib=58)
    kept, kept_done = products(offs, *down_sides, slots, place.swap(send, CORE))
    down = Reduce(place, offs, kept)
    (gg, gu, gha, gat, gm, gain_mid), done = ffn_back(
        offs, hid, gft, ghf, act, dact, gain_f, own, arrays, (kept_done,)
    )
    gu_sides = ([normed_ffn], [(gg, 0), (gu, 0)])
    done = down.first((done,))
    (send,), done = products(offs, *gu_sides, slots, None, (done,))
    got = place.swap(send, CORE)
    done = down.second((done,))
    kept, done = products(offs, *gu_sides, slots, got, (done,))
    gate_up = Reduce(place, offs, kept)
    finish = [gha, gat, gain_fin, gain_mid, score]

    def back(first, acc, left, after):
        return attend_back(
            first, slots // 2, common + (hot,), gm, mixed, acc, left, finish, all_qkv, heads, size,
            after,
        )

    (left, tables, acc), done = back(0, None, None, (done,))
    finish.append(tables)
    done = down.third((done,))
    done = gate_up.first((done,))
    (left, _, dx, both, small), done = back(slots // 2, acc, left, (done,))
    right, left_ = place.both_ways(dx, dx)
    done = gate_up.second_and_third((done,))
    (send,), _ = attn_products(offs, left, both, small, None, (done,))
    kept, done = attn_products(offs, left, both, small, place.swap(send, CORE))
    attn = Reduce(place, offs, kept)
    (*so_far, right, left_), done = collect(1, slots, offs, right, left_, dx, None, (done,))
    right, left_ = place.both_ways(right, left_)
    done = start_after = attn.first((done,))
    done = attn.second((done,))
    (*so_far, right, left_), done = collect(2, slots, offs, right, left_, dx, so_far, (done,))
    right, left_ = place.both_ways(right, left_)
    (grad_down, grad_proj, grad_gate, grad_up), done = gathered(
        down.total, gate_up.total, (d, w_proj.shape[1], hidden, hidden), (start_after,),
        (done,),
    )
    done = attn.third((done,))
    (input_grad, packed), done = collect(3, slots, offs, right, left_, dx, so_far, (done,))
    last, _ = place.first_round(*halves(attn.total, 0), (done,))
    grad_q, grad_k, grad_v, grad_out, small = unpack(
        offs, place.second_round(*last), 4, small.shape[2]
    )

    input_grad = input_grad.reshape(rows * length, d)
    n, m = score.shape
    packed = packed.astype(f32).reshape(slots, 16, d // 128, 128)[:, :, : 2 * (n // 16), :m]
    packed = packed[:, :, 0::2] + packed[:, :, 1::2]
    scores = packed.transpose(0, 2, 1, 3).reshape(slots, n, m)
    return (
        scores,
        input_grad,
        small[:, 0],
        grad_q.T,
        grad_k.T,
        grad_v.T,
        grad_out,
        small[:buckets, 64 : 64 + heads],
        small[:, 2],
        grad_gate,
        grad_up,
        grad_down,
        small[:, 1],
        grad_proj,
    )


def solution(mesh):
    n_dp, n_mp = mesh.shape["dp"], mesh.shape["mp"]
    mesh = Mesh(mesh.devices.reshape(n_dp // 8, 2, 2, 2, n_mp), dp + ("mp",))
    return jax.shard_map(
        local,
        mesh=mesh,
        in_specs=(
            P(dp, None),
            P(dp, None),
            P(dp, None),
            P(dp, None, None),
            P(dp, None, None),
            P(dp, None, None),
            P(),
            P(None, "mp"),
            P(None, "mp"),
            P(None, "mp"),
            P("mp", None),
            P(None, "mp"),
            P(),
            P(None, "mp"),
            P(None, "mp"),
            P("mp", None),
            P(),
            P(),
        ),
        out_specs=(
            P(dp, None, None),
            P(dp, None),
            P(),
            P(None, "mp"),
            P(None, "mp"),
            P(None, "mp"),
            P("mp", None),
            P(None, "mp"),
            P(),
            P(None, "mp"),
            P(None, "mp"),
            P("mp", None),
            P(),
            P(),
        ),
        check_vma=False,
    )
```
